128 devices in a mesh: dp: 16 (over z, x), row: 2 (over y_hi), col: 4 (over y_lo, core).
Axes of the slice: x: 4, y: 4 (y_hi: 2, y_lo: 2; y = y_hi * 2 + y_lo), z: 4, core: 2. Of those that a mesh axis runs over, the one named last changes fastest.
Arguments:
- hidden_in: bfloat16 [16384, 960], P(('dp', 'col')), may hold values from -6 to 6
- segment_ids: int32 [16384], P(('dp', 'col')), may hold values from 0 to 2, as said below
- attn_gain: float32 [960], replicated, may hold values from 0.1 to 1.9
- q_weight: bfloat16 [960, 960], P('row', 'col'), may hold values from -0.1875 to 0.1875
- k_weight: bfloat16 [960, 320], P('row', 'col'), may hold values from -0.1875 to 0.1875
- v_weight: bfloat16 [960, 320], P('row', 'col'), may hold values from -0.1875 to 0.1875
- o_weight: bfloat16 [960, 960], P('row', 'col'), may hold values from -3.5 to 3.5
- ffn_gain: float32 [960], replicated, may hold values from 0.1 to 1.9
- gate_weight: bfloat16 [960, 2560], P('row', 'col'), may hold values from -0.1875 to 0.1875
- up_weight: bfloat16 [960, 2560], P('row', 'col'), may hold values from -0.1875 to 0.1875
- down_weight: bfloat16 [2560, 960], P('row', 'col'), may hold values from -0.125 to 0.125
- d_out: bfloat16 [16384, 960], P(('dp', 'col')), may hold values from -6 to 6
Outputs:
- block_out: float32 [16384, 960], P(('dp', 'col'))
- input_grad: float32 [16384, 960], P(('dp', 'col'))
- attn_gain_grad: float32 [960], replicated
- q_grad: float32 [960, 960], P('row', 'col')
- k_grad: float32 [960, 320], P('row', 'col')
- v_grad: float32 [960, 320], P('row', 'col')
- o_grad: float32 [960, 960], P('row', 'col')
- ffn_gain_grad: float32 [960], replicated
- gate_grad: float32 [960, 2560], P('row', 'col')
- up_grad: float32 [960, 2560], P('row', 'col')
- down_grad: float32 [2560, 960], P('row', 'col')
The draws below stay inside these ranges and needn't reach their ends.
Inputs may be any that keep to these rules, and one draw needn't show every extreme that they name: `segment_ids`: within each sequence of 1024 consecutive tokens the ids never fall, start at 0 and take the values 0, 1 and 2; document 0 holds 204 to 255 tokens, document 2 ends the sequence with 1 to 256 tokens.
All inputs are finite; a program needn't handle non-finite values.
Results may differ from the reference program's by a relative error of at most 0.025.
Values may be sent and summed in bfloat16 or wider, within the bound.
A program may use at most 128 MiB of HBM per device.

```python
import jax
import jax.numpy as jnp
from jax import lax

D = 960
FF = 2560
HEADS = 15
KV_HEADS = 5
HEAD_DIM = 64
SEQ_LEN = 1024
QD = 960
KVD = 320
TOKENS = 16384


def draw_segment_ids(key, part):
    key = jax.random.fold_in(key, 17)
    first_key, last_key = jax.random.split(key)
    seq_count = TOKENS // SEQ_LEN
    first_cut = jax.random.randint(first_key, (seq_count, 1), SEQ_LEN // 5, SEQ_LEN // 4)
    last_cut = jax.random.randint(last_key, (seq_count, 1), SEQ_LEN - SEQ_LEN // 4, SEQ_LEN)
    places = jnp.arange(SEQ_LEN, dtype=jnp.int32)[None, :]
    doc_ids = (places >= first_cut).astype(jnp.int32) + (places >= last_cut).astype(jnp.int32)
    return doc_ids.reshape(TOKENS).astype(jnp.int32)


def block_scale(own_key, shape, shards, least, largest):
    loudness, own = 1.0, jax.random.fold_in(own_key, 6)
    for axis_at, blocks in shards:
        heights = jnp.exp(jax.random.uniform(jax.random.fold_in(own, axis_at), (blocks,), jnp.float32, least / len(shards), largest / len(shards)))
        loudness = loudness * jnp.repeat(heights, shape[axis_at] // blocks).reshape([-1 if axis == axis_at else 1 for axis in range(len(shape))])
    return loudness


def scatter_about(stream_key, shape, width, bound, pieces=(), kind=jnp.bfloat16):
    drawn = jax.random.normal(stream_key, shape, jnp.float32) * width
    if len(pieces) > 0:
        drawn = block_scale(stream_key, shape, pieces, -0.22, 0.18) * drawn
    return jnp.clip(drawn, min=-bound, max=bound).astype(kind)


def setup_inputs(seed: int = 0) -> dict:
    streams_of = jax.random.split(jax.random.key(seed), 13)
    return {
        "hidden_in": scatter_about(streams_of[0], (TOKENS, D), 1.0, 6.0, ((0, 64),)),
        "segment_ids": draw_segment_ids(jax.random.fold_in(streams_of[12], 71), 0),
        "attn_gain": jnp.clip(1.0 + 0.18 * jax.random.normal(streams_of[2], (D,), jnp.float32), 0.1, 1.9),
        "q_weight": scatter_about(streams_of[3], (D, QD), D ** -0.5, 0.1875, ((0, 2), (1, 4))),
        "k_weight": scatter_about(streams_of[4], (D, KVD), D ** -0.5, 0.1875, ((0, 2), (1, 4))),
        "v_weight": scatter_about(streams_of[5], (D, KVD), D ** -0.5, 0.1875, ((0, 2), (1, 4))),
        "o_weight": scatter_about(streams_of[6], (QD, D), (max(QD // 256, 1)) ** -0.5, 3.5, ((0, 2), (1, 4))),
        "ffn_gain": jnp.clip(1.0 + 0.18 * jax.random.normal(streams_of[7], (D,), jnp.float32), 0.1, 1.9),
        "gate_weight": scatter_about(streams_of[8], (D, FF), D ** -0.5, 0.1875, ((0, 2), (1, 4))),
        "up_weight": scatter_about(streams_of[9], (D, FF), D ** -0.5, 0.1875, ((0, 2), (1, 4))),
        "down_weight": scatter_about(streams_of[10], (FF, D), FF ** -0.5, 0.125, ((0, 2), (1, 4))),
        "d_out": scatter_about(streams_of[11], (TOKENS, D), 1.0, 6.0, ((0, 64),)),
    }


@jax.custom_vjp
def low(v):
    return lax.optimization_barrier(v.astype(jnp.bfloat16)).astype(jnp.float32)

@jax.custom_vjp
def low_back(v):
    return v

def low_keep(v):
    return (low(v), None)

def low_pass(kept, grad):
    return (grad,)

def back_keep(v):
    return (v, None)

def back_low(kept, grad):
    return (low(grad),)
low.defvjp(low_keep, low_pass)
low_back.defvjp(back_keep, back_low)
norm_eps = 1e-05
rope_base = 100000.0
highest = lax.Precision.HIGHEST

def matmul_hi(left, right):
    return jnp.dot(left, right, precision=highest)

def rms_norm(values, gain_vec):
    return values * lax.rsqrt(lax.optimization_barrier(jnp.mean(values * values, axis=1, keepdims=True)) + norm_eps) * gain_vec

def rotate(values, places):
    half_dim = values.shape[-1] // 2
    frequency = rope_base ** (-jnp.arange(half_dim, dtype=jnp.float32) * 2.0 / values.shape[-1])
    angles = places.astype(jnp.float32)[:, None] * frequency[None, :]
    cosine = jnp.cos(angles)[:, None, :]
    sine_part = jnp.sin(angles)[:, None, :]
    first_half = values[..., :half_dim]
    second_half = values[..., half_dim:]
    return jnp.concatenate([first_half * cosine - second_half * sine_part, second_half * cosine + first_half * sine_part], axis=-1)

def seq_forward(tokens, doc_ids, params):
    attn_gain, q_weight, k_weight, v_weight, o_weight, ffn_gain, gate_weight, up_weight, down_weight = params
    length = tokens.shape[0]
    share_heads = HEADS // KV_HEADS
    scaling = HEAD_DIM ** (-0.5)
    positions = jnp.arange(length, dtype=jnp.int32)
    places = positions - lax.optimization_barrier(jnp.sum((doc_ids[None, :] < doc_ids[:, None]).astype(jnp.int32), axis=1))
    normed = low(rms_norm(tokens, attn_gain))
    query_rows = low_back(low(matmul_hi(normed, q_weight)))
    key_rows = low_back(low(matmul_hi(normed, k_weight)))
    value_rows = low_back(low(matmul_hi(normed, v_weight)))
    turned_queries = low(rotate(query_rows.reshape(length, HEADS, HEAD_DIM), places)).reshape(length, KV_HEADS, share_heads, HEAD_DIM)
    turned_keys = low(rotate(key_rows.reshape(length, KV_HEADS, HEAD_DIM), places))
    value_heads = value_rows.reshape(length, KV_HEADS, HEAD_DIM)
    allowed = (doc_ids[:, None] == doc_ids[None, :]) & (positions[None, :] <= positions[:, None])
    raw_scores = low_back(jnp.einsum('qkgd,pkd->kgqp', turned_queries, turned_keys, precision=highest) * scaling)
    masked = jnp.where(allowed, raw_scores, -jnp.inf)
    row_top = lax.optimization_barrier(jnp.max(masked, axis=-1, keepdims=True))
    exp_terms = jnp.exp(masked - row_top)
    attn_probs = low(exp_terms / lax.optimization_barrier(jnp.sum(exp_terms, axis=-1, keepdims=True)))
    attended = jnp.einsum('kgqp,pkd->qkgd', attn_probs, value_heads, precision=highest)
    attn_rows = low_back(low(attended.reshape(length, HEADS * HEAD_DIM)))
    middle = tokens + low_back(matmul_hi(attn_rows, o_weight))
    normed_two = low(rms_norm(middle, ffn_gain))
    gate_vals = low_back(low(matmul_hi(normed_two, gate_weight)))
    up_vals = low_back(low(matmul_hi(normed_two, up_weight)))
    hidden = low(jax.nn.silu(gate_vals) * up_vals)
    return middle + low_back(matmul_hi(hidden, down_weight))

def reference(hidden_in, segment_ids, attn_gain, q_weight, k_weight, v_weight, o_weight, ffn_gain, gate_weight, up_weight, down_weight, d_out):
    seq_count = hidden_in.shape[0] // SEQ_LEN
    stacked = hidden_in.astype(jnp.float32).reshape(seq_count, SEQ_LEN, D)
    doc_rows = segment_ids.reshape(seq_count, SEQ_LEN)
    params = (attn_gain.astype(jnp.float32), q_weight.astype(jnp.float32), k_weight.astype(jnp.float32), v_weight.astype(jnp.float32), o_weight.astype(jnp.float32), ffn_gain.astype(jnp.float32), gate_weight.astype(jnp.float32), up_weight.astype(jnp.float32), down_weight.astype(jnp.float32))

    def forward(inputs, weights):

        def one_seq(pair):
            return seq_forward(pair[0], pair[1], weights)
        return lax.map(jax.checkpoint(one_seq), (inputs, doc_rows))
    outputs, pullback = jax.vjp(forward, stacked, params)
    d_inputs, d_params = pullback(d_out.astype(jnp.float32).reshape(seq_count, SEQ_LEN, D))
    return (outputs.reshape(-1, D), d_inputs.reshape(-1, D), d_params[0], d_params[1], d_params[2], d_params[3], d_params[4], d_params[5], d_params[6], d_params[7], d_params[8])
```

```python
import functools

import jax
import jax.numpy as jnp
from jax import lax
from jax.experimental import pallas as pl
from jax.experimental.pallas import tpu as pltpu
from jax.sharding import PartitionSpec as P

HEADS = 15
KV_HEADS = 5
HEAD_DIM = 64
SHARE = HEADS // KV_HEADS
D = 960
FF = 2560
QD = 960
KVD = 320
SCALING = HEAD_DIM ** (-0.5)
MESH = pl.DeviceIdType.MESH
F32 = jnp.float32
BF16 = jnp.bfloat16
VMEM_LIMIT = 48 * 1024 * 1024

norm_eps = 1e-05
rope_base = 100000.0


def place():
    row, col = lax.axis_index("row"), lax.axis_index("col")
    return lax.axis_index("dp"), row * 2 + col // 2, col % 2


def device(dp, y, s):
    return (dp, y // 2, (y % 2) * 2 + s)


def block_of(y, s):
    return ((y % 2) * 2 + s) * 2 + y // 2


def meet(others):
    barrier = pltpu.get_barrier_semaphore()
    for other in others:
        pl.semaphore_signal(barrier, inc=1, device_id=other, device_id_type=MESH)
    pl.semaphore_wait(barrier, len(others))


def send(src, dst, send_sem, recv_sem, other):
    copy = pltpu.make_async_remote_copy(
        src_ref=src,
        dst_ref=dst,
        send_sem=send_sem,
        recv_sem=recv_sem,
        device_id=other,
        device_id_type=MESH,
    )
    copy.start()
    return copy


def ring_gather_kernel(count, both_cores, splits, *refs):
    ins, outs = refs[:count], refs[count : 2 * count]
    local_sem, send_sem, recv_sem = refs[2 * count :]
    dp, y, s = place()
    up, down, far = (y + 1) % 4, (y + 3) % 4, (y + 2) % 4
    index = block_of if both_cores else (lambda y_at, s_at: y_at)
    to_up, to_down, to_mate = device(dp, up, s), device(dp, down, s), device(dp, y, 1 - s)
    meet([to_up, to_down] + ([to_mate] if both_cores else []))
    mine = index(y, s)
    pending, local = [], []

    def ship(a, n, src, dst, other):
        pending.append(send(src, dst, send_sem.at[a, n], recv_sem.at[a, n], other))

    def arrive(a, n, dst):
        pltpu.make_async_remote_copy(
            src_ref=dst,
            dst_ref=dst,
            send_sem=send_sem.at[a, n],
            recv_sem=recv_sem.at[a, n],
            device_id=to_up,
            device_id_type=MESH,
        ).wait_recv()

    for a in range(count):
        out = outs[a].at[mine]
        ship(a, 0, ins[a], out, to_up)
        ship(a, 1, ins[a], out, to_down)
    for a in range(count):
        out = outs[a].at[mine]
        if both_cores:
            ship(a, 4, ins[a], out, to_mate)
        keep = pltpu.make_async_copy(ins[a], out, local_sem.at[a])
        keep.start()
        local.append(keep)
    for a in range(count):
        half = pl.ds(0, splits[a])
        rest = pl.ds(splits[a], ins[a].shape[0] - splits[a])
        low, high, opposite = index(down, s), index(up, s), index(far, s)
        arrive(a, 0, outs[a].at[low])
        ship(a, 2, outs[a].at[low, half], outs[a].at[low, half], to_up)
        if both_cores:
            ship(a, 5, outs[a].at[low], outs[a].at[low], to_mate)
        arrive(a, 1, outs[a].at[high])
        ship(a, 3, outs[a].at[high, rest], outs[a].at[high, rest], to_down)
        if both_cores:
            ship(a, 6, outs[a].at[high], outs[a].at[high], to_mate)
        arrive(a, 2, outs[a].at[opposite, half])
        if both_cores:
            ship(a, 7, outs[a].at[opposite, half], outs[a].at[opposite, half], to_mate)
        arrive(a, 3, outs[a].at[opposite, rest])
        if both_cores:
            ship(a, 8, outs[a].at[opposite, rest], outs[a].at[opposite, rest], to_mate)
    if both_cores:
        for a in range(count):
            half = pl.ds(0, splits[a])
            rest = pl.ds(splits[a], ins[a].shape[0] - splits[a])
            arrive(a, 4, outs[a].at[index(y, 1 - s)])
            arrive(a, 5, outs[a].at[index(down, 1 - s)])
            arrive(a, 6, outs[a].at[index(up, 1 - s)])
            arrive(a, 7, outs[a].at[index(far, 1 - s), half])
            arrive(a, 8, outs[a].at[index(far, 1 - s), rest])
    for copy in pending:
        copy.wait_send()
    for copy in local:
        copy.wait()


def ring_gather(arrays, splits, both_cores, collective_id):
    count = len(arrays)
    blocks = 8 if both_cores else 4
    return pl.pallas_call(
        functools.partial(ring_gather_kernel, count, both_cores, splits),
        out_shape=[jax.ShapeDtypeStruct((blocks,) + a.shape, a.dtype) for a in arrays],
        in_specs=[pl.BlockSpec(memory_space=pl.ANY)] * count,
        out_specs=[pl.BlockSpec(memory_space=pl.ANY)] * count,
        scratch_shapes=[
            pltpu.SemaphoreType.DMA((count,)),
            pltpu.SemaphoreType.DMA((count, 9)),
            pltpu.SemaphoreType.DMA((count, 9)),
        ],
        compiler_params=pltpu.CompilerParams(collective_id=collective_id, has_side_effects=True),
    )(*arrays)


def reduce_ring(get, here, dp, y, s, out_ref, early, sums, landed, send_sem, recv_sem):
    up, down, far = (y + 1) % 4, (y + 3) % 4, (y + 2) % 4
    to_up, to_down = device(dp, up, s), device(dp, down, s)
    far_block = get(far)
    first = send(far_block.at[0], early.at[0], send_sem.at[0], recv_sem.at[0], to_down)
    second = send(far_block.at[1], early.at[1], send_sem.at[1], recv_sem.at[1], to_up)
    down_block, up_block = get(down), get(up)
    third = send(down_block.at[1], landed.at[0, 1], send_sem.at[2], recv_sem.at[2], to_down)
    fourth = send(up_block.at[0], landed.at[1, 0], send_sem.at[3], recv_sem.at[3], to_up)
    first.wait_recv()
    sums[0] = (down_block[0].astype(F32) + early[0].astype(F32)).astype(BF16)
    fifth = send(sums.at[0], landed.at[0, 0], send_sem.at[4], recv_sem.at[4], to_down)
    second.wait_recv()
    sums[1] = (up_block[1].astype(F32) + early[1].astype(F32)).astype(BF16)
    sixth = send(sums.at[1], landed.at[1, 1], send_sem.at[5], recv_sem.at[5], to_up)
    mine = get(y)
    fourth.wait_recv()
    fifth.wait_recv()
    out_ref[0] = mine[0].astype(F32) + landed[0, 0].astype(F32) + landed[1, 0].astype(F32)
    third.wait_recv()
    sixth.wait_recv()
    out_ref[1] = mine[1].astype(F32) + landed[0, 1].astype(F32) + landed[1, 1].astype(F32)
    for copy in (first, second, third, fourth, fifth, sixth):
        copy.wait_send()


def ring_sum_kernel(x_ref, out_ref, early, sums, landed, send_sem, recv_sem):
    dp, y, s = place()
    meet([device(dp, (y + 1) % 4, s), device(dp, (y + 3) % 4, s)])
    reduce_ring(lambda t: x_ref.at[t], None, dp, y, s, out_ref, early, sums, landed, send_sem, recv_sem)


def ring_sum(x, collective_id):
    _, halves, rows, columns = x.shape
    return pl.pallas_call(
        ring_sum_kernel,
        out_shape=jax.ShapeDtypeStruct((2, rows, columns), F32),
        in_specs=[pl.BlockSpec(memory_space=pltpu.VMEM)],
        out_specs=pl.BlockSpec(memory_space=pltpu.VMEM),
        scratch_shapes=[
            pltpu.VMEM((2, rows, columns), BF16),
            pltpu.VMEM((2, rows, columns), BF16),
            pltpu.VMEM((2, 2, rows, columns), BF16),
            pltpu.SemaphoreType.DMA((6,)),
            pltpu.SemaphoreType.DMA((6,)),
        ],
        compiler_params=pltpu.CompilerParams(
            collective_id=collective_id, has_side_effects=True, vmem_limit_bytes=VMEM_LIMIT
        ),
    )(x)


def group_sum_kernel(x_ref, out_ref, mate, total, early, sums, landed, mate_send, mate_recv, send_sem, recv_sem):
    dp, y, s = place()
    meet([device(dp, (y + 1) % 4, s), device(dp, (y + 3) % 4, s), device(dp, y, 1 - s)])
    copies = []
    for step in range(4):
        t = (y + 2 + step) % 4
        copies.append(
            send(
                x_ref.at[block_of(t, 1 - s)],
                mate.at[step],
                mate_send.at[step],
                mate_recv.at[step],
                device(dp, y, 1 - s),
            )
        )
    for step in range(4):
        t = (y + 2 + step) % 4
        copies[step].wait_recv()
        total[step] = (x_ref[block_of(t, s)].astype(F32) + mate[step].astype(F32)).astype(BF16)
    reduce_ring(
        lambda t: total.at[(t - y + 2) % 4],
        None, dp, y, s, out_ref, early, sums, landed, send_sem, recv_sem,
    )
    for copy in copies:
        copy.wait_send()


def group_sum(x, collective_id):
    _, halves, rows, columns = x.shape
    return pl.pallas_call(
        group_sum_kernel,
        out_shape=jax.ShapeDtypeStruct((2, rows, columns), F32),
        in_specs=[pl.BlockSpec(memory_space=pltpu.VMEM)],
        out_specs=pl.BlockSpec(memory_space=pltpu.VMEM),
        scratch_shapes=[
            pltpu.VMEM((4, 2, rows, columns), BF16),
            pltpu.VMEM((4, 2, rows, columns), BF16),
            pltpu.VMEM((2, rows, columns), BF16),
            pltpu.VMEM((2, rows, columns), BF16),
            pltpu.VMEM((2, 2, rows, columns), BF16),
            pltpu.SemaphoreType.DMA((4,)),
            pltpu.SemaphoreType.DMA((4,)),
            pltpu.SemaphoreType.DMA((6,)),
            pltpu.SemaphoreType.DMA((6,)),
        ],
        compiler_params=pltpu.CompilerParams(
            collective_id=collective_id, has_side_effects=True, vmem_limit_bytes=VMEM_LIMIT
        ),
    )(x)


def ring_swap_kernel(split, x_ref, out_ref, relay_low, relay_high, local_sem, send_sem, recv_sem):
    dp, y, s = place()
    up, down, far = (y + 1) % 4, (y + 3) % 4, (y + 2) % 4
    to_up, to_down = device(dp, up, s), device(dp, down, s)
    meet([to_up, to_down])
    low, high = pl.ds(0, split), pl.ds(split, x_ref.shape[1] - split)
    copies = [
        send(x_ref.at[far, low], relay_low, send_sem.at[0], recv_sem.at[0], to_down),
        send(x_ref.at[far, high], relay_high, send_sem.at[1], recv_sem.at[1], to_up),
        send(x_ref.at[down], out_ref.at[y], send_sem.at[2], recv_sem.at[2], to_down),
        send(x_ref.at[up], out_ref.at[y], send_sem.at[3], recv_sem.at[3], to_up),
    ]
    keep = pltpu.make_async_copy(x_ref.at[y], out_ref.at[y], local_sem)
    keep.start()
    copies[0].wait_recv()
    copies.append(send(relay_low, out_ref.at[up, low], send_sem.at[4], recv_sem.at[4], to_down))
    copies[1].wait_recv()
    copies.append(send(relay_high, out_ref.at[down, high], send_sem.at[5], recv_sem.at[5], to_up))
    for copy in copies[2:]:
        copy.wait_recv()
    for copy in copies:
        copy.wait_send()
    keep.wait()


def ring_swap(x, split, collective_id):
    _, rows, columns = x.shape
    return pl.pallas_call(
        functools.partial(ring_swap_kernel, split),
        out_shape=jax.ShapeDtypeStruct(x.shape, x.dtype),
        in_specs=[pl.BlockSpec(memory_space=pl.ANY)],
        out_specs=pl.BlockSpec(memory_space=pl.ANY),
        scratch_shapes=[
            pltpu.VMEM((split, columns), x.dtype),
            pltpu.VMEM((rows - split, columns), x.dtype),
            pltpu.SemaphoreType.DMA,
            pltpu.SemaphoreType.DMA((6,)),
            pltpu.SemaphoreType.DMA((6,)),
        ],
        compiler_params=pltpu.CompilerParams(collective_id=collective_id, has_side_effects=True),
    )(x)


def dp_sum_kernel(x_ref, out_ref, mate, mine, parts, total, pair_send, pair_recv, send_sem, recv_sem, back_send, back_recv):
    dp, y, s = place()
    peers = [device((dp + k) % 16, y, s) for k in range(1, 16)]
    to_mate = device(dp, y, 1 - s)
    meet(peers + [to_mate])
    swap = send(x_ref.at[1 - s], mate, pair_send, pair_recv, to_mate)
    swap.wait_recv()
    mine[...] = (x_ref[s].astype(F32) + mate[...].astype(F32)).astype(BF16)
    copies = []
    for k in range(1, 16):
        copies.append(
            send(mine.at[(dp + k) % 16], parts.at[k - 1], send_sem.at[k - 1], recv_sem.at[k - 1], peers[k - 1])
        )
    acc = mine[dp].astype(F32)
    for k in range(15):
        copies[k].wait_recv()
        acc = acc + parts[k].astype(F32)
    total[...] = acc.astype(BF16)
    out_ref[dp] = acc.astype(BF16)
    back = []
    for k in range(1, 16):
        back.append(send(total, out_ref.at[dp], back_send.at[k - 1], back_recv.at[k - 1], peers[k - 1]))
    for copy in back:
        copy.wait_recv()
    for copy in back + copies + [swap]:
        copy.wait_send()


def dp_sum(x, collective_id):
    _, chunks, rows, columns = x.shape
    return pl.pallas_call(
        dp_sum_kernel,
        out_shape=jax.ShapeDtypeStruct((16, rows, columns), BF16),
        in_specs=[pl.BlockSpec(memory_space=pltpu.VMEM)],
        out_specs=pl.BlockSpec(memory_space=pltpu.VMEM),
        scratch_shapes=[
            pltpu.VMEM((16, rows, columns), BF16),
            pltpu.VMEM((16, rows, columns), BF16),
            pltpu.VMEM((15, rows, columns), BF16),
            pltpu.VMEM((rows, columns), BF16),
            pltpu.SemaphoreType.DMA,
            pltpu.SemaphoreType.DMA,
            pltpu.SemaphoreType.DMA((15,)),
            pltpu.SemaphoreType.DMA((15,)),
            pltpu.SemaphoreType.DMA((15,)),
            pltpu.SemaphoreType.DMA((15,)),
        ],
        compiler_params=pltpu.CompilerParams(
            collective_id=collective_id, has_side_effects=True, vmem_limit_bytes=VMEM_LIMIT
        ),
    )(x)


def dot_nt(a, b):
    return lax.dot_general(a, b, (((1,), (1,)), ((), ())), preferred_element_type=F32)


def dot_tn(a, b):
    return lax.dot_general(a, b, (((0,), (0,)), ((), ())), preferred_element_type=F32)


def heads_of(x, group):
    first = group * SHARE
    return jnp.concatenate(
        [x[:, (first + j) * HEAD_DIM : (first + j + 1) * HEAD_DIM] for j in range(SHARE)], axis=0
    )


def mask_of(seg_q, seg_k, pos_q):
    keys = lax.broadcasted_iota(jnp.int32, (seg_q.shape[0], seg_k.shape[1]), 1)
    return jnp.where((seg_q == seg_k) & (keys <= pos_q), 0.0, -jnp.inf).astype(F32)


def attend_kernel(q_ref, kv_ref, seg_q_ref, seg_k_ref, pos_ref, o_ref, lse_ref):
    rows, keys = q_ref.shape[0], kv_ref.shape[0]
    bias = mask_of(seg_q_ref[...], seg_k_ref[...], pos_ref[...])
    for g in range(KV_HEADS):
        key = kv_ref[:, g * HEAD_DIM : (g + 1) * HEAD_DIM]
        value = kv_ref[:, KVD + g * HEAD_DIM : KVD + (g + 1) * HEAD_DIM]
        scores = dot_nt(heads_of(q_ref, g), key) * SCALING
        scores = scores.reshape(SHARE, rows, keys) + bias[None]
        top = jnp.max(scores, axis=-1, keepdims=True)
        terms = jnp.exp(scores - top)
        total = jnp.sum(terms, axis=-1, keepdims=True)
        probs = (terms / total).astype(BF16).reshape(SHARE * rows, keys)
        out = jnp.dot(probs, value, preferred_element_type=F32)
        for j in range(SHARE):
            at = (g * SHARE + j) * HEAD_DIM
            o_ref[:, at : at + HEAD_DIM] = out[j * rows : (j + 1) * rows].astype(BF16)
        lse_ref[g] = (top + jnp.log(total)).reshape(SHARE * rows, 1)


def attend(q, kv, seg_q, seg_k, pos_q):
    rows = q.shape[0]
    return pl.pallas_call(
        attend_kernel,
        out_shape=[
            jax.ShapeDtypeStruct((rows, QD), BF16),
            jax.ShapeDtypeStruct((KV_HEADS, SHARE * rows, 1), F32),
        ],
        compiler_params=pltpu.CompilerParams(vmem_limit_bytes=VMEM_LIMIT),
        cost_estimate=pl.CostEstimate(flops=2 * 2 * rows * 1024 * QD, bytes_accessed=3000000, transcendentals=rows * 1024 * HEADS),
    )(q, kv, seg_q, seg_k, pos_q)


def attend_back_kernel(q_ref, kv_ref, do_ref, lse_ref, seg_q_ref, seg_k_ref, pos_ref, dq_ref, dkv_ref):
    rows, keys = q_ref.shape[0], kv_ref.shape[0]
    bias = mask_of(seg_q_ref[...], seg_k_ref[...], pos_ref[...])
    for g in range(KV_HEADS):
        own = slice(g * HEAD_DIM, (g + 1) * HEAD_DIM)
        val = slice(KVD + g * HEAD_DIM, KVD + (g + 1) * HEAD_DIM)
        key, value = kv_ref[:, own], kv_ref[:, val]
        query, d_out = heads_of(q_ref, g), heads_of(do_ref, g)
        scores = dot_nt(query, key) * SCALING
        scores = scores.reshape(SHARE, rows, keys) + bias[None]
        probs = jnp.exp(scores.reshape(SHARE * rows, keys) - lse_ref[g])
        d_probs = dot_nt(d_out, value)
        inner = jnp.sum(probs * d_probs, axis=-1, keepdims=True)
        d_scores = (probs * (d_probs - inner)).astype(BF16)
        d_query = jnp.dot(d_scores, key, preferred_element_type=F32) * SCALING
        for j in range(SHARE):
            at = (g * SHARE + j) * HEAD_DIM
            dq_ref[:, at : at + HEAD_DIM] = d_query[j * rows : (j + 1) * rows]
        dkv_ref[:, own] = (dot_tn(d_scores, query) * SCALING).astype(BF16)
        dkv_ref[:, val] = dot_tn(probs.astype(BF16), d_out).astype(BF16)


def attend_back(q, kv, d_o, lse, seg_q, seg_k, pos_q):
    rows = q.shape[0]
    return pl.pallas_call(
        attend_back_kernel,
        out_shape=[
            jax.ShapeDtypeStruct((rows, QD), F32),
            jax.ShapeDtypeStruct(kv.shape, BF16),
        ],
        compiler_params=pltpu.CompilerParams(vmem_limit_bytes=VMEM_LIMIT),
        cost_estimate=pl.CostEstimate(flops=5 * 2 * rows * 1024 * QD, bytes_accessed=5000000, transcendentals=rows * 1024 * HEADS),
    )(q, kv, d_o, lse, seg_q, seg_k, pos_q)


def unit_rows(values):
    inverse = lax.rsqrt(jnp.mean(values * values, axis=-1, keepdims=True) + norm_eps)
    return values * inverse, inverse


def norm_back(gradient, unit, inverse, gain_vec):
    scaled = gradient * gain_vec
    inner_sum = jnp.mean(scaled * unit, axis=1, keepdims=True)
    return (inverse * (scaled - unit * inner_sum), jnp.sum(gradient * unit, axis=0))


def rotation(places, width):
    half = HEAD_DIM // 2
    frequency = rope_base ** (-jnp.arange(half, dtype=F32) * 2.0 / HEAD_DIM)
    angles = places.astype(F32)[:, None] * frequency[None, :]
    cosine, sine = jnp.cos(angles), jnp.sin(angles)
    heads = width // HEAD_DIM
    return (
        jnp.tile(jnp.concatenate([cosine, cosine], axis=1), (1, heads)),
        jnp.tile(jnp.concatenate([-sine, sine], axis=1), (1, heads)),
    )


def rotate(values, cosine, sine):
    width, half = values.shape[1], HEAD_DIM // 2
    lane = lax.broadcasted_iota(jnp.int32, values.shape, 1) % HEAD_DIM
    swapped = jnp.where(lane < half, jnp.roll(values, -half, axis=1), jnp.roll(values, half, axis=1))
    return values * cosine[:, :width] + swapped * sine[:, :width]


def shards(
    hidden_in,
    segment_ids,
    attn_gain,
    q_weight,
    k_weight,
    v_weight,
    o_weight,
    ffn_gain,
    gate_weight,
    up_weight,
    down_weight,
    d_out,
):
    rows_here = hidden_in.shape[0]
    own_rows = rows_here // 2
    row, col = lax.axis_index("row"), lax.axis_index("col")
    y_low, s = col // 2, col % 2
    y = row * 2 + y_low
    group = ("row", "col")
    swap_rs = [(r * 4 + 2 * a + b, b * 4 + 2 * a + r) for r in range(2) for a in range(2) for b in range(2)]
    swap_ra = [(r * 4 + 2 * a + b, a * 4 + 2 * r + b) for r in range(2) for a in range(2) for b in range(2)]
    mates = [(0, 1), (1, 0), (2, 3), (3, 2)]
    across = [(0, 2), (1, 3), (2, 0), (3, 1)]

    attn_block = jnp.concatenate([q_weight, k_weight, v_weight, o_weight], axis=1)
    own_ids = lax.dynamic_slice_in_dim(segment_ids, row * own_rows, own_rows, 0)
    id_rows = jnp.broadcast_to(own_ids.astype(BF16)[None, :], (32, own_rows))
    attn_all, ids_all = ring_gather([attn_block, id_rows], (240, 16), True, 1)
    attn_all = attn_all.reshape(4, D, 640)
    docs_all = ids_all[:, 0, :].reshape(8 * own_rows).astype(jnp.int32)

    def join_mates(half):
        other = lax.ppermute(half, "col", mates)
        return jnp.concatenate(
            [jnp.where(s == 0, half, other), jnp.where(s == 0, other, half)], axis=0
        )

    gate_up_own = jnp.concatenate([gate_weight, up_weight], axis=1)
    gate_up_block = join_mates(lax.ppermute(gate_up_own, group, swap_rs))
    down_parts = lax.all_to_all(
        down_weight.reshape(4, 320, 240), "col", split_axis=0, concat_axis=0, tiled=True
    )
    down_half = down_parts.transpose(1, 0, 2).reshape(320, D)
    down_block = join_mates(lax.ppermute(down_half, group, swap_ra))

    def ring_rows(local):
        other = lax.ppermute(local, "col", across)
        mine, theirs = local.reshape(2, own_rows, D), other.reshape(2, own_rows, D)
        first = jnp.where(y_low == 0, mine, theirs)
        second = jnp.where(y_low == 0, theirs, mine)
        return jnp.stack([first, second], axis=1).reshape(4 * own_rows, D)

    hidden_ring = ring_rows(hidden_in)
    d_out_ring = ring_rows(d_out)

    start = col * rows_here + row * own_rows
    pos_q = start + jnp.arange(own_rows, dtype=jnp.int32)
    earlier = jnp.sum((docs_all[None, :] < own_ids[:, None]).astype(jnp.int32), axis=1)
    places = pos_q - earlier
    seg_q, seg_k, pos_col = own_ids[:, None], docs_all[None, :], pos_q[:, None]
    cosine, sine = rotation(places, QD)
    tokens = lax.dynamic_slice_in_dim(hidden_in, row * own_rows, own_rows, 0).astype(F32)
    d_out_own = lax.dynamic_slice_in_dim(d_out, row * own_rows, own_rows, 0).astype(F32)

    unit_one, inverse_one = unit_rows(tokens)
    normed_one = (unit_one * attn_gain).astype(BF16)
    qkv = [
        jnp.dot(normed_one, attn_all[c, :, :400], preferred_element_type=F32).astype(BF16)
        for c in range(4)
    ]
    q = jnp.concatenate([part[:, :240] for part in qkv], axis=1)
    k = jnp.concatenate([part[:, 240:320] for part in qkv], axis=1)
    v = jnp.concatenate([part[:, 320:] for part in qkv], axis=1)
    queries = rotate(q.astype(F32), cosine, sine).astype(BF16)
    keys = rotate(k.astype(F32), cosine, sine).astype(BF16)
    kv_all = ring_gather([jnp.concatenate([keys, v], axis=1)], (64,), True, 2)[0].reshape(8 * own_rows, 2 * KVD)
    attn_rows, lse = attend(queries, kv_all, seg_q, seg_k, pos_col)
    attn_out = jnp.concatenate(
        [jnp.dot(attn_rows, attn_all[c, :, 400:], preferred_element_type=F32) for c in range(4)],
        axis=1,
    )
    middle = tokens + attn_out
    unit_two, inverse_two = unit_rows(middle)
    normed_two = (unit_two * ffn_gain).astype(BF16)
    normed_two_ring = ring_gather([normed_two], (64,), False, 3)[0].reshape(4 * own_rows, D)

    gate_up = jnp.dot(normed_two_ring, gate_up_block, preferred_element_type=F32).astype(BF16)
    gate_vals, up_vals = gate_up[:, :640].astype(F32), gate_up[:, 640:].astype(F32)
    sig_gate = jax.nn.sigmoid(gate_vals)
    silu_gate = gate_vals * sig_gate
    hidden_mid = (silu_gate * up_vals).astype(BF16)
    ffn_part = jnp.dot(hidden_mid, down_block, preferred_element_type=F32).astype(BF16)
    d_hidden = dot_nt(d_out_ring, down_block)
    d_gate = (d_hidden * up_vals * sig_gate * (1.0 + gate_vals * (1.0 - sig_gate))).astype(BF16)
    d_up = (d_hidden * silu_gate).astype(BF16)
    d_gate_up = jnp.concatenate([d_gate, d_up], axis=1)
    d_normed_part = dot_nt(d_gate_up, gate_up_block).astype(BF16)
    sums = ring_sum(
        jnp.stack([ffn_part.reshape(4, own_rows, D), d_normed_part.reshape(4, own_rows, D)], axis=1), 4
    )

    gate_up_grad = dot_tn(normed_two_ring, d_gate_up).astype(BF16).reshape(2, 480, 1280)
    down_grad = dot_tn(hidden_mid, d_out_ring).astype(BF16).reshape(2, 320, D)

    def mate_sum(halves):
        keep = jnp.where(s == 0, halves[0], halves[1])
        give = jnp.where(s == 0, halves[1], halves[0])
        return (keep.astype(F32) + lax.ppermute(give, "col", mates).astype(F32)).astype(BF16)

    gate_up_share = lax.psum_scatter(mate_sum(gate_up_grad), "dp", scatter_dimension=0, tiled=True)
    down_share = lax.psum_scatter(mate_sum(down_grad), "dp", scatter_dimension=0, tiled=True)
    gate_up_total = lax.all_gather(
        lax.ppermute(gate_up_share, group, swap_rs), "dp", axis=0, tiled=True
    )
    down_cols = lax.all_to_all(
        lax.ppermute(down_share, group, swap_ra).reshape(20, 4, 240).transpose(1, 0, 2),
        "col",
        split_axis=0,
        concat_axis=0,
        tiled=True,
    )
    down_total = (
        lax.all_gather(down_cols, "dp", axis=0).transpose(1, 0, 2, 3).reshape(1280, 240)
    )

    block_own = (middle + sums[0]).astype(BF16)
    d_middle, ffn_gain_part = norm_back(sums[1], unit_two, inverse_two, ffn_gain)
    d_middle = d_middle + d_out_own

    d_y1 = d_middle.astype(BF16)
    d_o = sum(dot_nt(d_y1[:, c * 240 : (c + 1) * 240], attn_all[c, :, 400:]) for c in range(4)).astype(BF16)
    d_queries, d_kv = attend_back(queries, kv_all, d_o, lse, seg_q, seg_k, pos_col)
    d_kv_own = group_sum(d_kv.reshape(8, 2, own_rows // 2, 2 * KVD), 5).reshape(own_rows, 2 * KVD)
    d_q = rotate(d_queries, cosine, -sine).astype(BF16)
    d_k = rotate(d_kv_own[:, :KVD], cosine, -sine).astype(BF16)
    d_v = d_kv_own[:, KVD:].astype(BF16)
    d_qkv = [
        jnp.concatenate(
            [
                d_q[:, c * 240 : (c + 1) * 240],
                d_k[:, c * 80 : (c + 1) * 80],
                d_v[:, c * 80 : (c + 1) * 80],
            ],
            axis=1,
        )
        for c in range(4)
    ]
    d_normed_one = sum(dot_nt(d_qkv[c], attn_all[c, :, :400]) for c in range(4))
    d_tokens, attn_gain_part = norm_back(d_normed_one, unit_one, inverse_one, attn_gain)
    input_own = (d_tokens + d_middle).astype(BF16)

    gains = jnp.stack([attn_gain_part, ffn_gain_part]).astype(BF16)
    gain_rows = jnp.pad(gains, ((0, 30), (0, 1792 - D)))
    outgoing = []
    for t in range(4):
        r, a = t // 2, t % 2
        body = jnp.concatenate(
            [
                d_qkv[2 * a],
                d_qkv[2 * a + 1],
                attn_rows[:, r * 480 : (r + 1) * 480],
                d_y1[:, a * 480 : (a + 1) * 480],
                jnp.zeros((own_rows, 32), BF16),
            ],
            axis=1,
        )
        outgoing.append(jnp.concatenate([body, gain_rows], axis=0))
    incoming = ring_swap(jnp.stack(outgoing), 80, 6)
    acts = incoming[:, :own_rows].reshape(4 * own_rows, 1792)
    gain_sums = jnp.sum(incoming[:, own_rows : own_rows + 2, :D].astype(F32), axis=0)
    unit_ring, _ = unit_rows(hidden_ring.astype(F32))
    normed_ring = (unit_ring * attn_gain).astype(BF16)
    normed_half = lax.dynamic_slice_in_dim(normed_ring, row * 480, 480, 1)
    qkv_grad = dot_tn(normed_half, acts[:, :800]).astype(BF16)
    o_grad = dot_tn(acts[:, 800:1280], acts[:, 1280:1760]).astype(BF16)
    gain_block = jnp.pad(
        jnp.pad(gain_sums, ((0, 0), (0, 320))).astype(BF16).reshape(4, 640), ((0, 28), (0, 0))
    )
    blocks = [
        jnp.concatenate(
            [
                jnp.concatenate(
                    [qkv_grad[:, b * 400 : (b + 1) * 400], o_grad[:, b * 240 : (b + 1) * 240]], axis=1
                ),
                gain_block,
            ],
            axis=0,
        )
        for b in range(2)
    ]
    totals = dp_sum(jnp.stack(blocks).reshape(2, 16, 32, 640), 7).reshape(512, 640).astype(F32)
    gain_totals = totals[480:484].reshape(2, 1280)[:, :D]

    def join_rows(own):
        other = lax.ppermute(own, "row", [(0, 1), (1, 0)])
        return jnp.concatenate(
            [jnp.where(row == 0, own, other), jnp.where(row == 0, other, own)], axis=0
        ).astype(F32)

    return (
        join_rows(block_own),
        join_rows(input_own),
        gain_totals[0],
        totals[:480, :240],
        totals[:480, 240:320],
        totals[:480, 320:400],
        totals[:480, 400:],
        gain_totals[1],
        gate_up_total[:, :640].astype(F32),
        gate_up_total[:, 640:].astype(F32),
        down_total.astype(F32),
    )


def solution(mesh):
    rows, blocks = P(("dp", "col"), None), P("row", "col")
    return jax.shard_map(
        shards,
        mesh=mesh,
        in_specs=(
            rows, P(("dp", "col")), P(), blocks, blocks, blocks, blocks, P(), blocks, blocks, blocks, rows,
        ),
        out_specs=(rows, rows, P(), blocks, blocks, blocks, blocks, P(), blocks, blocks, blocks),
        check_vma=False,
    )
```

```python
import jax
import jax.numpy as jnp
import numpy as np
from jax import lax
from jax.experimental import pallas as pl
from jax.experimental.pallas import tpu as pltpu
from jax.sharding import PartitionSpec as P

HEADS = 15
KV_HEADS = 5
HEAD_DIM = 64
SHARE = HEADS // KV_HEADS
D = 960
HALF = 480
QD = 960
KVD = 320
UNITS = 640
OWN = 128
KEYS = 1024
SCALING = HEAD_DIM ** (-0.5)
MESH = pl.DeviceIdType.MESH
F32 = jnp.float32
BF16 = jnp.bfloat16
SLOTS = 288
CHUNKS = 15

norm_eps = 1e-05
rope_base = 100000.0


def dot(a, b):
    return jnp.dot(a, b, preferred_element_type=F32)


def dot_nt(a, b):
    return lax.dot_general(a, b, (((1,), (1,)), ((), ())), preferred_element_type=F32)


def dot_tn(a, b):
    return lax.dot_general(a, b, (((0,), (0,)), ((), ())), preferred_element_type=F32)


def heads_of(x, group):
    first = group * SHARE
    return jnp.concatenate(
        [x[:, (first + j) * HEAD_DIM : (first + j + 1) * HEAD_DIM] for j in range(SHARE)], axis=0
    )


def rows_of(index, count):
    return pl.ds(pl.multiple_of(index * count, count), count)


class Place:
    def __init__(self, send_sem, recv_sem):
        col = lax.axis_index("col")
        self.dp, self.row = lax.axis_index("dp"), lax.axis_index("row")
        self.ranks = lax.axis_size("dp")
        self.z, self.x = self.dp // 4, self.dp % 4
        self.low, self.s = col // 2, col % 2
        self.y = self.row * 2 + self.low
        self.up, self.down, self.far = (self.y + 1) % 4, (self.y + 3) % 4, (self.y + 2) % 4
        self.send_sem, self.recv_sem, self.used = send_sem, recv_sem, 0
        self.open = []

    def device(self, y, s):
        return (self.dp, y // 2, (y % 2) * 2 + s)

    def rank(self, z, x):
        return (z * 4 + x, self.row, self.low * 2 + self.s)

    def peer(self, k):
        return ((self.dp + k) % self.ranks, self.row, self.low * 2 + self.s)

    def slots(self, count):
        first = self.used
        self.used += count
        assert self.used <= SLOTS
        return first

    def wire(self, src, dst, other, slot, recv_slot=None):
        return pltpu.make_async_remote_copy(
            src_ref=src,
            dst_ref=dst,
            send_sem=self.send_sem.at[slot],
            recv_sem=self.recv_sem.at[slot if recv_slot is None else recv_slot],
            device_id=other,
            device_id_type=MESH,
        )

    def send(self, src, dst, other):
        copy = self.wire(src, dst, other, self.slots(1))
        copy.start()
        self.open.append(copy)
        return copy

    def others(self):
        others = [self.peer(k) for k in range(1, self.ranks)]
        others += [self.device(self.y, 1 - self.s)]
        for y in (self.up, self.down, self.far):
            others += [self.device(y, self.s), self.device(y, 1 - self.s)]
        return others

    def greet(self):
        barrier = pltpu.get_barrier_semaphore()
        for other in self.others():
            pl.semaphore_signal(barrier, inc=1, device_id=other, device_id_type=MESH)

    def meet(self):
        pl.semaphore_wait(pltpu.get_barrier_semaphore(), len(self.others()))


class Gather:
    def __init__(self, at, buf, rows, split, index=None):
        self.at, self.buf = at, buf
        self.both = index is not None
        if index is None:
            self.mine, self.low, self.high, self.opposite = 0, 1, 2, 3
            self.to_up, self.to_down, self.on_up, self.on_down = 1, 2, 3, 3
        else:
            self.mine, self.low = index(at.y, at.s), index(at.down, at.s)
            self.high, self.opposite = index(at.up, at.s), index(at.far, at.s)
            self.to_up, self.to_down = self.mine, self.mine
            self.on_up, self.on_down = self.low, self.high
        self.first, self.second = pl.ds(0, split), pl.ds(split, rows - split)
        self.up_device, self.down_device = at.device(at.up, at.s), at.device(at.down, at.s)
        self.mate = at.device(at.y, 1 - at.s)
        self.from_mate = []

    def ship(self, index, part, to_index, other):
        return self.at.send(self.buf.at[index, part], self.buf.at[to_index, part], other)

    def to_mate(self, index):
        if self.both:
            self.from_mate.append(self.at.send(self.buf.at[index], self.buf.at[index], self.mate))

    def start(self):
        self.up_first = self.ship(self.mine, self.first, self.to_up, self.up_device)
        self.down_second = self.ship(self.mine, self.second, self.to_down, self.down_device)
        self.up_second = self.ship(self.mine, self.second, self.to_up, self.up_device)
        self.down_first = self.ship(self.mine, self.first, self.to_down, self.down_device)
        self.to_mate(self.mine)

    def relay(self):
        self.up_first.wait_recv()
        self.up_far = self.ship(self.low, self.first, self.on_up, self.up_device)
        self.down_second.wait_recv()
        self.down_far = self.ship(self.high, self.second, self.on_down, self.down_device)

    def near(self):
        self.up_second.wait_recv()
        self.to_mate(self.low)
        self.down_first.wait_recv()
        self.to_mate(self.high)

    def finish(self):
        self.up_far.wait_recv()
        self.down_far.wait_recv()
        self.to_mate(self.opposite)
        for copy in self.from_mate:
            copy.wait_recv()


class Reduce:
    def __init__(self, at, blocks, early, sums, landed):
        self.at, self.blocks = at, blocks
        self.early, self.sums, self.landed = early, sums, landed
        self.up_device, self.down_device = at.device(at.up, at.s), at.device(at.down, at.s)

    def start_far(self):
        at, far = self.at, self.blocks.at[3]
        self.first = at.send(far.at[0], self.early.at[0], self.down_device)
        self.second = at.send(far.at[1], self.early.at[1], self.up_device)

    def start_near(self):
        at = self.at
        self.third = at.send(self.blocks.at[1, 1], self.landed.at[0, 1], self.down_device)
        self.fourth = at.send(self.blocks.at[2, 0], self.landed.at[1, 0], self.up_device)

    def middle(self):
        at, blocks, early, sums = self.at, self.blocks, self.early, self.sums
        self.first.wait_recv()
        sums[0] = (blocks[1, 0].astype(F32) + early[0].astype(F32)).astype(BF16)
        self.fifth = at.send(sums.at[0], self.landed.at[0, 0], self.down_device)
        self.second.wait_recv()
        sums[1] = (blocks[2, 1].astype(F32) + early[1].astype(F32)).astype(BF16)
        self.sixth = at.send(sums.at[1], self.landed.at[1, 1], self.up_device)

    def finish(self):
        for copy in (self.third, self.fourth, self.fifth, self.sixth):
            copy.wait_recv()
        total = (
            self.blocks[0].astype(F32) + self.landed[0].astype(F32) + self.landed[1].astype(F32)
        )
        return total.reshape(total.shape[0] * total.shape[1], total.shape[2])


class RankSum:
    def __init__(self, at, halves, mate, kept, parts, total, out):
        self.at, self.halves, self.mate, self.kept = at, halves, mate, kept
        self.parts, self.total, self.out = parts, total, out

    def start(self):
        at = self.at
        self.swap = at.send(self.halves.at[1 - at.s], self.mate, at.device(at.y, 1 - at.s))

    def join(self):
        at = self.at
        self.swap.wait_recv()

        def add(i, carry):
            rows = rows_of(i, 32)
            self.kept[rows] = (
                self.halves[at.s, rows].astype(F32) + self.mate[rows].astype(F32)
            ).astype(BF16)
            return carry

        lax.fori_loop(0, 16, add, 0)

    def scatter(self):
        at = self.at
        self.join()
        self.copies = [
            at.send(self.kept.at[rows_of((at.dp + k) % at.ranks, 32)], self.parts.at[k - 1], at.peer(k))
            for k in range(1, at.ranks)
        ]

    def reduce(self):
        at = self.at
        acc = self.kept[rows_of(at.dp, 32)].astype(F32)
        for k, copy in enumerate(self.copies):
            copy.wait_recv()
            acc = acc + self.parts[k].astype(F32)
        self.total[...] = acc.astype(BF16)

    def gather(self):
        at = self.at
        own = self.out.at[rows_of(at.dp, 32)]
        self.back = [at.send(own, own, at.peer(k)) for k in range(1, at.ranks)]

    def finish(self):
        for copy in self.back:
            copy.wait_recv()


class Spread:
    def __init__(self, at, buf, guard=None):
        self.at, self.buf, self.guard = at, buf, guard
        self.slot = at.slots(18)

    def guarded(self, act):
        if self.guard is None:
            act()
        else:
            pl.when(self.guard)(act)

    def along(self, half, second, step):
        at = self.at
        if (half == 0) != second:
            return at.rank((at.z + step) % 4, at.x)
        return at.rank(at.z, (at.x + step) % 4)

    def first_copy(self, half, n):
        own = self.buf.at[self.at.z, self.at.x, half]
        return self.at.wire(own, own, self.along(half, False, (1, 3, 2)[n]), self.slot + half * 9 + n)

    def block(self, half, part, back):
        at, pair = self.at, pl.ds(2 * part, 2)
        if half == 0:
            return self.buf.at[pair, (at.x + 4 - back) % 4, half]
        return self.buf.at[(at.z + 4 - back) % 4, pair, half]

    def second_copy(self, half, n):
        step, part = ((1, 0), (3, 1), (1, 1), (3, 0))[n]
        src = self.block(half, part, 0)
        return self.at.wire(src, src, self.along(half, True, step), self.slot + half * 9 + 3 + n)

    def third_copy(self, half, n):
        step, part = ((1, 0), (3, 1))[n]
        src = self.block(half, part, step)
        return self.at.wire(src, src, self.along(half, True, step), self.slot + half * 9 + 7 + n)

    def first(self):
        def act():
            for half in range(2):
                for n in range(3):
                    self.first_copy(half, n).start()

        self.guarded(act)

    def second(self):
        def act():
            for half in range(2):
                for n in range(3):
                    self.first_copy(half, n).wait_recv()
                for n in range(4):
                    self.second_copy(half, n).start()

        self.guarded(act)

    def third(self):
        def act():
            for n in range(2):
                for half in range(2):
                    self.second_copy(half, n).wait_recv()
                    self.third_copy(half, n).start()

        self.guarded(act)

    def finish(self):
        def act():
            for half in range(2):
                for n in range(2, 4):
                    self.second_copy(half, n).wait_recv()
                for n in range(2):
                    self.third_copy(half, n).wait_recv()

        self.guarded(act)

    def drain(self):
        def act():
            for half in range(2):
                for n in range(3):
                    self.first_copy(half, n).wait_send()
                for n in range(4):
                    self.second_copy(half, n).wait_send()
                for n in range(2):
                    self.third_copy(half, n).wait_send()

        self.guarded(act)


class Collect:
    def __init__(self, at, kept, early, sums, landed, four, parts, total):
        self.at, self.kept, self.early, self.sums = at, kept, early, sums
        self.landed, self.four, self.parts, self.total = landed, four, parts, total

    def along(self, half, second, step):
        at = self.at
        if (half == 1) != second:
            return at.rank((at.z + step) % 4, at.x)
        return at.rank(at.z, (at.x + step) % 4)

    def block(self, half, step, part):
        at = self.at
        pair = slice(None) if part is None else pl.ds(2 * part, 2)
        if half == 0:
            return (pair, (at.x + step) % 4, half)
        return ((at.z + step) % 4, pair, half)

    def start(self):
        at, kept = self.at, self.kept
        self.far, self.near = {}, []
        for half in range(2):
            for n, step in ((0, 3), (1, 1)):
                self.far[half, n] = at.send(
                    kept.at[self.block(half, 2, n)], self.early.at[half, n], self.along(half, False, step)
                )
        for half in range(2):
            for n, step in ((0, 3), (1, 1)):
                self.near.append(
                    at.send(
                        kept.at[self.block(half, step, 1 - n)],
                        self.landed.at[half, n, pl.ds(2 * (1 - n), 2)],
                        self.along(half, False, step),
                    )
                )

    def middle(self):
        at, kept = self.at, self.kept
        for half in range(2):
            for n, step in ((0, 3), (1, 1)):
                self.far[half, n].wait_recv()
                self.sums[half, n] = (
                    kept[self.block(half, step, n)].astype(F32) + self.early[half, n].astype(F32)
                ).astype(BF16)
                self.near.append(
                    at.send(
                        self.sums.at[half, n],
                        self.landed.at[half, n, pl.ds(2 * n, 2)],
                        self.along(half, False, step),
                    )
                )

    def second(self):
        at = self.at
        for copy in self.near:
            copy.wait_recv()
        self.last = []
        for half in range(2):
            self.four[half] = (
                self.kept[self.block(half, 0, None)].astype(F32)
                + self.landed[half, 0].astype(F32)
                + self.landed[half, 1].astype(F32)
            ).astype(BF16)
            here = at.z if half == 0 else at.x
            for n, step in enumerate((1, 3, 2)):
                self.last.append(
                    at.send(
                        self.four.at[half, (here + step) % 4],
                        self.parts.at[half, n],
                        self.along(half, True, step),
                    )
                )

    def reduce(self):
        at = self.at
        for copy in self.last:
            copy.wait_recv()
        for half in range(2):
            acc = self.four[half, at.z if half == 0 else at.x].astype(F32)
            for n in range(3):
                acc = acc + self.parts[half, n].astype(F32)
            self.total[half] = acc.astype(BF16)


def unit_rows(values):
    inverse = lax.rsqrt(jnp.mean(values * values, axis=-1, keepdims=True) + norm_eps)
    return values * inverse, inverse


def norm_back(gradient, unit, inverse, gain_vec):
    scaled = gradient * gain_vec
    inner_sum = jnp.mean(scaled * unit, axis=1, keepdims=True)
    return (
        inverse * (scaled - unit * inner_sum),
        jnp.sum(gradient * unit, axis=0, keepdims=True),
    )


def turn(x, cosine, sine):
    half = HEAD_DIM // 2
    lane = lax.broadcasted_iota(jnp.int32, x.shape, 1) % HEAD_DIM
    swapped = jnp.where(lane < half, pltpu.roll(x, 128 - half, 1), pltpu.roll(x, half, 1))
    return x * cosine + swapped * sine


def turn_all(x, cosine, sine):
    width = x.shape[1]
    pieces = []
    for first in range(0, width, 128):
        piece = x[:, first : min(first + 128, width)]
        if piece.shape[1] < 128:
            wide = jnp.concatenate([piece, jnp.zeros_like(piece)], axis=1)
            piece = turn(wide, cosine, sine)[:, : piece.shape[1]]
        else:
            piece = turn(piece, cosine, sine)
        pieces.append(piece)
    return jnp.concatenate(pieces, axis=1)


IN_NAMES = ("hidden", "ids_in", "freq", "attn_gain", "ffn_gain")
IN_NAMES += ("q_w", "k_w", "v_w", "o_w", "gate_w", "up_w", "down_w", "d_out")
OUT_NAMES = ("block_out", "input_grad", "attn_total", "kv_total", "ffn_total")
SCRATCH = dict(
    weights=((8, 400, HALF), BF16),
    o_parts=((2, 4, 4, 2, 2, 16, HALF), BF16),
    tokens=((2, OWN, D), BF16),
    own_o=((240, HALF), BF16),
    ids=((8, 16, OWN), BF16),
    normed_one=((2, OWN, HALF), BF16),
    bias=((OWN, KEYS), F32),
    cosine=((OWN, 128), F32),
    sine=((OWN, 128), F32),
    queries=((OWN, QD), BF16),
    kv=((8, OWN, 640), BF16),
    lse=((KV_HEADS, SHARE * OWN, 1), F32),
    attn=((OWN, QD), BF16),
    attn_halves=((2, OWN, HALF), BF16),
    attn_ring=((4, OWN, HALF), BF16),
    first_ring=((4, OWN, HALF), BF16),
    d_out_ring=((4, OWN, D), BF16),
    middle=((OWN, D), F32),
    normed_ring=((4, OWN, D), BF16),
    gate_up=((D, 2 * UNITS), BF16),
    down_parts=((2, 4, 4, 2, 16, UNITS), BF16),
    gate_land=((4, 4, 2, 16, 2 * UNITS), BF16),
    down=((D, UNITS), BF16),
    units=((4, OWN, UNITS), BF16),
    d_gate_up=((4, OWN, 2 * UNITS), BF16),
    ffn_parts=((4, 2, OWN // 2, D), BF16),
    ffn_early=((2, OWN // 2, D), BF16),
    ffn_sums=((2, OWN // 2, D), BF16),
    ffn_landed=((2, 2, OWN // 2, D), BF16),
    dn_parts=((4, 2, OWN // 2, D), BF16),
    dn_early=((2, OWN // 2, D), BF16),
    dn_sums=((2, OWN // 2, D), BF16),
    dn_landed=((2, 2, OWN // 2, D), BF16),
    ffn_halves=((2, 512, 1920), BF16),
    ffn_mate=((512, 1920), BF16),
    ffn_kept=((4, 4, 2, 16, 1920), BF16),
    ffn_far=((2, 2, 2, 16, 1920), BF16),
    ffn_pairs=((2, 2, 2, 16, 1920), BF16),
    ffn_near=((2, 2, 4, 16, 1920), BF16),
    ffn_four=((2, 4, 16, 1920), BF16),
    ffn_last=((2, 3, 16, 1920), BF16),
    ffn_sum=((2, 16, 1920), BF16),
    d_middle=((OWN, D), F32),
    d_y1_halves=((2, OWN, HALF), BF16),
    d_y1_ring=((4, OWN, HALF), BF16),
    d_kv=((8, OWN, 640), BF16),
    kv_mate=((4, OWN, 640), BF16),
    kv_parts=((4, 2, OWN // 2, 640), BF16),
    kv_early=((2, OWN // 2, 640), BF16),
    kv_sums=((2, OWN // 2, 640), BF16),
    kv_landed=((2, 2, OWN // 2, 640), BF16),
    d_q=((2, OWN, HALF), BF16),
    d_q_ring=((4, OWN, HALF), BF16),
    d_kv_own=((2, OWN, 320), BF16),
    d_kv_ring=((4, OWN, 320), BF16),
    gains=((4, 8, D), F32),
    qo_two=((2, 512, HALF), BF16),
    qo_mate=((512, HALF), BF16),
    qo_kept=((512, HALF), BF16),
    qo_ranks=((15, 32, HALF), BF16),
    qo_sum=((32, HALF), BF16),
    kv_two=((2, 512, 160), BF16),
    kv_grad_mate=((512, 160), BF16),
    kv_kept=((512, 160), BF16),
    kv_ranks=((15, 32, 160), BF16),
    kv_sum=((32, 160), BF16),
    send_sem=pltpu.SemaphoreType.DMA((SLOTS,)),
    recv_sem=pltpu.SemaphoreType.DMA((SLOTS,)),
)


def block_of(y, s):
    return ((y % 2) * 2 + s) * 2 + y // 2


def layer_kernel(*refs):
    names = IN_NAMES + OUT_NAMES + tuple(SCRATCH)
    m = dict(zip(names, refs))
    at = Place(m["send_sem"], m["recv_sem"])
    row, low, s, y, dp = at.row, at.low, at.s, at.y, at.dp
    mate = at.device(y, 1 - s)
    up_device, down_device = at.device(at.up, s), at.device(at.down, s)
    far_device, cross = at.device(at.far, s), at.device(at.far, 1 - s)
    mine = block_of(y, s)
    active = dp < CHUNKS
    not_ = jnp.logical_not

    at.greet()

    weights, ids = m["weights"], m["ids"]
    weights[mine, 0:240] = m["q_w"][...].T
    weights[mine, 240:320] = m["k_w"][...]
    weights[mine, 320:400] = m["v_w"][...]
    own_row = jnp.where(row == 0, m["ids_in"][:, 0:OWN], m["ids_in"][:, OWN:]).astype(F32)
    ids[mine] = jnp.broadcast_to(own_row, (16, OWN)).astype(BF16)
    m["own_o"][...] = m["o_w"][...].T
    at.meet()

    gate_up, o_parts, down_parts = m["gate_up"], m["o_parts"], m["down_parts"]
    o_slot, down_slot, gate_slot = at.slots(3), at.slots(2), at.slots(4)
    gate_mate_slot = at.slots(1)
    own_core = s == row
    strip = rows_of(dp, 16)

    def o_copy(n):
        other = (up_device, down_device, far_device)[n]
        return at.wire(m["own_o"].at[strip], o_parts.at[s, at.z, at.x, row, low], other, o_slot + n)

    def down_copy(r):
        target = r * 2 + row
        return target, at.wire(
            m["down_w"].at[strip, pl.ds(r * UNITS, UNITS)],
            down_parts.at[s, at.z, at.x, low],
            at.device(target, s),
            down_slot + r,
            down_slot + low,
        )

    def down_arrive(a):
        return low * 2 + a, at.wire(
            m["down_w"].at[strip, pl.ds(0, UNITS)],
            down_parts.at[s, at.z, at.x, a],
            up_device,
            down_slot + a,
        )

    gate_land = m["gate_land"]

    def gate_copy(n, part):
        source = (m["gate_w"], m["up_w"])[n]
        return at.wire(
            source.at[pl.ds(pl.multiple_of(dp * 32 + 16 * part, 16), 16)],
            gate_land.at[at.z, at.x, part, :, pl.ds(UNITS * n, UNITS)],
            cross,
            gate_slot + 2 * n + part,
        )

    gate_copies = [(n, part) for n in range(2) for part in range(2)]
    o_spread = Spread(at, o_parts.at[s])
    down_spread = Spread(at, down_parts.at[s])
    gate_spread = Spread(at, gate_land, not_(own_core))
    spreads = (o_spread, gate_spread, down_spread)

    def gate_mate(half):
        rows = pl.ds(pl.multiple_of(half * HALF, 32), HALF)
        return at.wire(gate_up.at[rows], gate_up.at[rows], mate, gate_mate_slot)

    @pl.when(active)
    def _():
        o_parts[s, at.z, at.x, row, low] = m["own_o"][strip]
        for n in range(3):
            o_copy(n).start()
        for r in range(2):
            target, copy = down_copy(r)

            @pl.when(target == y)
            def _():
                down_parts[s, at.z, at.x, low] = m["down_w"][strip, r * UNITS : (r + 1) * UNITS]

            @pl.when(target != y)
            def _():
                copy.start()

        @pl.when(not_(own_core))
        def _():
            for n, part in gate_copies:
                gate_copy(n, part).start()

    @pl.when(not_(active))
    def _():
        o_parts[s, at.z, at.x] = jnp.zeros((2, 2, 16, HALF), BF16)
        down_parts[s, at.z, at.x] = jnp.zeros((2, 16, UNITS), BF16)
        gate_land[at.z, at.x] = jnp.zeros((2, 16, 2 * UNITS), BF16)

    gather_w = Gather(at, weights, 400, 192, block_of)
    gather_w.start()
    ids_copies = [at.send(ids.at[mine], ids.at[mine], mate)]
    for other in (at.up, at.down, at.far):
        for core in (s, 1 - s):
            ids_copies.append(at.send(ids.at[mine], ids.at[mine], at.device(other, core)))

    @pl.when(own_core)
    def _():
        rows = pl.ds(pl.multiple_of(row * HALF, 32), HALF)
        gate_up[rows, 0:UNITS] = m["gate_w"][...]
        gate_up[rows, UNITS:] = m["up_w"][...]
        gate_mate(row).start()

    tokens_two, d_out_ring = m["tokens"], m["d_out_ring"]
    hidden, d_out = m["hidden"][...].T, m["d_out"][...].T
    tokens_two[0], tokens_two[1] = hidden[:OWN], hidden[OWN:]
    first_half = row == 0
    d_out_ring[0] = jnp.where(first_half, d_out[:OWN], d_out[OWN:])
    d_out_ring[3] = jnp.where(first_half, d_out[OWN:], d_out[:OWN])
    attn_gain, ffn_gain = m["attn_gain"][...], m["ffn_gain"][...]
    unit_one, _ = unit_rows(tokens_two[row].astype(F32))
    normed = (unit_one * attn_gain).astype(BF16)
    m["normed_one"][0] = normed[:, :HALF]
    m["normed_one"][1] = normed[:, HALF:]
    first_ring = m["first_ring"]
    first_ring[0] = m["normed_one"][row]
    unit_far, _ = unit_rows(tokens_two[1 - row].astype(F32))
    normed_far = (unit_far * attn_gain).astype(BF16)
    first_ring[3] = jnp.where(first_half, normed_far[:, :HALF], normed_far[:, HALF:])

    for copy in ids_copies:
        copy.wait_recv()
    own_ids = jnp.broadcast_to(own_row, (OWN, OWN)).T[:, 0:1].astype(jnp.int32)
    docs = jnp.concatenate([ids[b, 0:1, :] for b in range(8)], axis=1).astype(F32).astype(jnp.int32)
    earlier = jnp.sum((docs < own_ids).astype(F32), axis=1, keepdims=True)
    start = (low * 2 + s) * 256 + row * OWN
    position = start + lax.broadcasted_iota(jnp.int32, (OWN, 1), 0)
    angles = (position.astype(F32) - earlier) * m["freq"][...]
    lane = lax.broadcasted_iota(jnp.int32, (OWN, 128), 1) % HEAD_DIM
    sine = jnp.sin(angles)
    m["cosine"][...] = jnp.cos(angles)
    m["sine"][...] = jnp.where(lane < HEAD_DIM // 2, -sine, sine)
    key_at = lax.broadcasted_iota(jnp.int32, (OWN, KEYS), 1)
    allowed = (own_ids == docs) & (key_at <= position)
    m["bias"][...] = jnp.where(allowed, 0.0, -jnp.inf).astype(F32)

    @pl.when(active)
    def _():
        for n in range(3):
            o_copy(n).wait_recv()
        for a in range(2):
            source, copy = down_arrive(a)

            @pl.when(source != y)
            def _():
                copy.wait_recv()

        @pl.when(not_(own_core))
        def _():
            for n, part in gate_copies:
                gate_copy(n, part).wait_recv()

    for spread in spreads:
        spread.first()

    gather_w.relay()
    d_out_copies = [
        at.send(d_out_ring.at[0], d_out_ring.at[1], up_device),
        at.send(d_out_ring.at[0], d_out_ring.at[2], down_device),
    ]
    for spread in spreads:
        spread.second()
    gather_w.near()
    gather_w.finish()
    parts = []
    for c in range(4):
        part = dot_nt(m["normed_one"][0], weights[2 * c]) + dot_nt(m["normed_one"][1], weights[2 * c + 1])
        parts.append(part.astype(BF16).astype(F32))
    cosine, sine = m["cosine"][...], m["sine"][...]
    k = jnp.concatenate([part[:, 240:320] for part in parts], axis=1)
    v = jnp.concatenate([part[:, 320:400] for part in parts], axis=1)
    kv = m["kv"]
    kv[mine] = jnp.concatenate([turn_all(k, cosine, sine), v], axis=1).astype(BF16)
    gather_kv = Gather(at, kv, OWN, OWN // 2, block_of)
    gather_kv.start()
    q = jnp.concatenate([part[:, 0:240] for part in parts], axis=1)
    m["queries"][...] = turn_all(q, cosine, sine).astype(BF16)
    gather_kv.relay()
    for spread in spreads:
        spread.third()
    gather_kv.near()
    gather_kv.finish()

    o_spread.finish()
    o_mate = at.send(o_parts.at[s], o_parts.at[s], mate)

    for g in range(KV_HEADS):
        key = kv[:, :, g * HEAD_DIM : (g + 1) * HEAD_DIM].reshape(KEYS, HEAD_DIM)
        value = kv[:, :, KVD + g * HEAD_DIM : KVD + (g + 1) * HEAD_DIM].reshape(KEYS, HEAD_DIM)
        scores = dot_nt(heads_of(m["queries"], g), key) * SCALING
        scores = scores.reshape(SHARE, OWN, KEYS) + m["bias"][...][None]
        top = jnp.max(scores, axis=-1, keepdims=True)
        terms = jnp.exp(scores - top)
        total = jnp.sum(terms, axis=-1, keepdims=True)
        probs = (terms / total).astype(BF16).reshape(SHARE * OWN, KEYS)
        out = dot(probs, value).astype(BF16)
        for j in range(SHARE):
            head = (g * SHARE + j) * HEAD_DIM
            m["attn"][:, head : head + HEAD_DIM] = out[j * OWN : (j + 1) * OWN]
        m["lse"][g] = (top + jnp.log(total)).reshape(SHARE * OWN, 1)
    attn_halves = m["attn_halves"]
    attn_halves[0] = m["attn"][:, :HALF]
    attn_halves[1] = m["attn"][:, HALF:]
    o_mate.wait_recv()

    def o_block(r, c):
        return o_parts[c % 2, :, :, r, c // 2].reshape(256, HALF)[0:240]

    attn_out = [
        dot_nt(attn_halves[0], o_block(0, c)) + dot_nt(attn_halves[1], o_block(1, c)) for c in range(4)
    ]
    middle = tokens_two[row].astype(F32) + jnp.concatenate(attn_out, axis=1)
    m["middle"][...] = middle
    unit_two, _ = unit_rows(middle)
    ring = m["normed_ring"]
    ring[0] = (unit_two * ffn_gain).astype(BF16)
    gather_n = Gather(at, ring, OWN, OWN // 2)
    gather_n.start()

    gate_spread.finish()

    @pl.when(not_(own_core))
    def _():
        rows = pl.ds(pl.multiple_of((1 - row) * HALF, 32), HALF)
        gate_up[rows] = gate_land[...].reshape(512, 2 * UNITS)[0:HALF]
        gate_mate(1 - row).start()

    down_spread.finish()
    down_mate = at.send(down_parts.at[s], down_parts.at[s], mate)
    gather_n.relay()
    down_mate.wait_recv()
    for c in range(4):
        m["down"][c * 240 : (c + 1) * 240] = down_parts[c % 2, :, :, c // 2].reshape(256, UNITS)[0:240]
    for copy in d_out_copies:
        copy.wait_recv()
    gate_mate(row).wait_recv()

    ffn_parts, dn_parts = m["ffn_parts"], m["dn_parts"]

    def feed(p):
        gate_and_up = dot(ring[p], gate_up[...]).astype(BF16)
        gate, raise_ = gate_and_up[:, :UNITS].astype(F32), gate_and_up[:, UNITS:].astype(F32)
        sig = 1.0 / (1.0 + jnp.exp(-gate))
        silu = gate * sig
        unit = (silu * raise_).astype(BF16)
        m["units"][p] = unit
        d_unit = dot(d_out_ring[p], m["down"][...])
        d_gate = (d_unit * raise_ * sig * (1.0 + gate * (1.0 - sig))).astype(BF16)
        d_up = (d_unit * silu).astype(BF16)
        m["d_gate_up"][p] = jnp.concatenate([d_gate, d_up], axis=1)
        d_normed = dot_nt(m["d_gate_up"][p], gate_up[...]).astype(BF16)
        dn_parts[p] = d_normed.reshape(2, OWN // 2, D)

    def feed_out(p):
        ffn_parts[p] = dot_nt(m["units"][p], m["down"][...]).astype(BF16).reshape(2, OWN // 2, D)

    dn = Reduce(at, dn_parts, m["dn_early"], m["dn_sums"], m["dn_landed"])
    ffn = Reduce(at, ffn_parts, m["ffn_early"], m["ffn_sums"], m["ffn_landed"])
    feed(0)
    gather_n.near()
    feed(1)
    feed(2)
    gather_n.finish()
    feed(3)
    dn.start_far()
    dn.start_near()
    for p in (3, 1, 2):
        feed_out(p)
    dn.middle()
    ffn.start_far()
    ffn.start_near()
    feed_out(0)

    halves = m["ffn_halves"]
    tokens_n = ring[...].reshape(4 * OWN, D)
    d_gate_up = m["d_gate_up"][...].reshape(4 * OWN, 2 * UNITS)
    tokens_d = d_out_ring[...].reshape(4 * OWN, D)
    units = m["units"][...].reshape(4 * OWN, UNITS)
    for h in range(2):
        halves[h, 0:HALF, 0 : 2 * UNITS] = dot_tn(tokens_n[:, h * HALF : (h + 1) * HALF], d_gate_up).astype(BF16)
        grad = dot_tn(tokens_d[:, h * HALF : (h + 1) * HALF], units).astype(BF16)
        for i in range(CHUNKS):
            halves[h, 32 * i : 32 * i + 16, 2 * UNITS :] = grad[16 * i : 16 * i + 16]
            halves[h, 32 * i + 16 : 32 * i + 32, 2 * UNITS :] = grad[240 + 16 * i : 256 + 16 * i]
        halves[h, HALF:, :] = jnp.zeros((32, 1920), BF16)
    ffn_pair = at.send(halves.at[1 - s], m["ffn_mate"], mate)
    ffn_collect = Collect(
        at,
        m["ffn_kept"],
        m["ffn_far"],
        m["ffn_pairs"],
        m["ffn_near"],
        m["ffn_four"],
        m["ffn_last"],
        m["ffn_sum"],
    )

    d_normed = dn.finish()
    ffn.middle()
    middle = m["middle"][...]
    unit_two, inverse_two = unit_rows(middle)
    d_middle, ffn_gain_part = norm_back(d_normed, unit_two, inverse_two, ffn_gain)
    d_middle = d_middle + d_out_ring[0].astype(F32)
    m["d_middle"][...] = d_middle
    d_y1 = d_middle.astype(BF16)
    d_y1_halves, d_y1_ring = m["d_y1_halves"], m["d_y1_ring"]
    d_y1_halves[0] = d_y1[:, :HALF]
    d_y1_halves[1] = d_y1[:, HALF:]
    ffn_pair.wait_recv()
    for z in range(4):
        for x in range(4):
            rows = pl.ds(32 * (4 * z + x), 32)
            both = halves[s, rows].astype(F32) + m["ffn_mate"][rows].astype(F32)
            m["ffn_kept"][z, x] = both.astype(BF16).reshape(2, 16, 1920)
    ffn_collect.start()
    d_attn = [0.0, 0.0]
    for c in range(4):
        for r in range(2):
            d_attn[r] = d_attn[r] + dot(d_y1[:, c * 240 : (c + 1) * 240], o_block(r, c))
    d_attn = jnp.concatenate(d_attn, axis=1).astype(BF16)

    up_low, up_row, down_row = 1 - low, at.up // 2, at.down // 2
    attn_ring, first_send = m["attn_ring"], m["normed_one"]
    side_copies = [
        at.send(d_y1_halves.at[up_low], d_y1_ring.at[1], up_device),
        at.send(d_y1_halves.at[up_low], d_y1_ring.at[2], down_device),
        at.send(attn_halves.at[up_row], attn_ring.at[1], up_device),
        at.send(attn_halves.at[down_row], attn_ring.at[2], down_device),
        at.send(first_send.at[up_row], first_ring.at[1], up_device),
        at.send(first_send.at[down_row], first_ring.at[2], down_device),
        at.send(attn_halves.at[1 - row], attn_ring.at[3], far_device),
        at.send(d_y1_halves.at[low], d_y1_ring.at[3], far_device),
    ]
    attn_ring[0] = attn_halves[row]
    d_y1_ring[0] = d_y1_halves[low]

    d_kv = m["d_kv"]
    d_q = []
    for g in range(KV_HEADS):
        own = slice(g * HEAD_DIM, (g + 1) * HEAD_DIM)
        val = slice(KVD + g * HEAD_DIM, KVD + (g + 1) * HEAD_DIM)
        key = kv[:, :, own].reshape(KEYS, HEAD_DIM)
        value = kv[:, :, val].reshape(KEYS, HEAD_DIM)
        query, d_head = heads_of(m["queries"], g), heads_of(d_attn, g)
        scores = dot_nt(query, key) * SCALING
        scores = scores.reshape(SHARE, OWN, KEYS) + m["bias"][...][None]
        probs = jnp.exp(scores.reshape(SHARE * OWN, KEYS) - m["lse"][g])
        d_probs = dot_nt(d_head, value)
        inner = jnp.sum(probs * d_probs, axis=-1, keepdims=True)
        d_scores = (probs * (d_probs - inner)).astype(BF16)
        d_query = dot(d_scores, key) * SCALING
        d_q += [d_query[j * OWN : (j + 1) * OWN] for j in range(SHARE)]
        d_kv[:, :, own] = (dot_tn(d_scores, query) * SCALING).astype(BF16).reshape(8, OWN, HEAD_DIM)
        d_kv[:, :, val] = dot_tn(probs.astype(BF16), d_head).astype(BF16).reshape(8, OWN, HEAD_DIM)
        if g == 2:
            ffn_collect.middle()

    ffn_collect.second()
    kv_copies = []
    order = ((3, at.far), (1, at.down), (2, at.up), (0, y))
    for p, t in order:
        kv_copies.append(at.send(d_kv.at[block_of(t, 1 - s)], m["kv_mate"].at[p], mate))
    cosine, sine = m["cosine"][...], -m["sine"][...]
    d_q = turn_all(jnp.concatenate(d_q, axis=1), cosine, sine).astype(BF16)
    kv_sum = Reduce(at, m["kv_parts"], m["kv_early"], m["kv_sums"], m["kv_landed"])
    for (p, t), copy in zip(order, kv_copies):
        copy.wait_recv()
        both = d_kv[block_of(t, s)].astype(F32) + m["kv_mate"][p].astype(F32)
        m["kv_parts"][p] = both.astype(BF16).reshape(2, OWN // 2, 640)
        if p == 3:
            kv_sum.start_far()
        if p == 2:
            kv_sum.start_near()
    d_q_two, d_q_ring = m["d_q"], m["d_q_ring"]
    d_q_two[0], d_q_two[1] = d_q[:, :HALF], d_q[:, HALF:]
    kv_sum.middle()
    q_copies = [
        at.send(d_q_two.at[up_low], d_q_ring.at[1], up_device),
        at.send(d_q_two.at[up_low], d_q_ring.at[2], down_device),
        at.send(d_q_two.at[low], d_q_ring.at[3], far_device),
    ]
    d_q_ring[0] = d_q_two[low]
    d_normed_one = [0.0, 0.0]
    for c in range(4):
        for r in range(2):
            d_normed_one[r] = d_normed_one[r] + dot(d_q[:, c * 240 : (c + 1) * 240], weights[2 * c + r, 0:240])

    ffn_collect.reduce()
    sums, ffn_total = m["ffn_sum"], m["ffn_total"]
    gate_back_slot, back_slot = at.slots(1), at.slots(2)
    own_rows = rows_of(dp, 32)
    lanes = pl.ds(2 * UNITS, UNITS)
    owner = low * 2 + s

    def gate_back():
        both = pl.ds(0, 2 * UNITS)
        return at.wire(
            sums.at[:, :, both], ffn_total.at[at.z, at.x, :, :, both], cross, gate_back_slot
        )

    def down_back(j):
        return at.wire(
            sums.at[j, :, lanes],
            ffn_total.at[at.z, at.x, row, :, lanes],
            at.device(owner, j),
            back_slot + j,
            back_slot + row,
        )

    @pl.when(own_core)
    def _():
        ffn_total[at.z, at.x, :, :, 0 : 2 * UNITS] = sums[:, :, 0 : 2 * UNITS]

    @pl.when(not_(own_core))
    def _():
        gate_back().start()

    for j in range(2):
        here = (owner == y) & (s == j)
        copy = down_back(j)

        @pl.when(here)
        def _():
            ffn_total[at.z, at.x, row, :, 2 * UNITS :] = sums[j, :, 2 * UNITS :]

        @pl.when(not_(here))
        def _():
            copy.start()

    d_kv_sum = kv_sum.finish()
    d_k = turn_all(d_kv_sum[:, :KVD], cosine, sine).astype(BF16)
    d_v = d_kv_sum[:, KVD:].astype(BF16)
    d_kv_own, d_kv_ring = m["d_kv_own"], m["d_kv_ring"]
    for a in range(2):
        d_kv_own[a] = jnp.concatenate(
            [d_k[:, a * 160 : (a + 1) * 160], d_v[:, a * 160 : (a + 1) * 160]], axis=1
        )
    kv_out = [
        at.send(d_kv_own.at[up_low], d_kv_ring.at[1], up_device),
        at.send(d_kv_own.at[up_low], d_kv_ring.at[2], down_device),
        at.send(d_kv_own.at[low], d_kv_ring.at[3], far_device),
    ]
    d_kv_ring[0] = d_kv_own[low]

    for c in range(4):
        piece = jnp.concatenate(
            [d_k[:, c * 80 : (c + 1) * 80], d_v[:, c * 80 : (c + 1) * 80]], axis=1
        )
        for r in range(2):
            d_normed_one[r] = d_normed_one[r] + dot(piece, weights[2 * c + r, 240:400])
    unit_one, inverse_one = unit_rows(tokens_two[row].astype(F32))
    d_tokens, attn_gain_part = norm_back(
        jnp.concatenate(d_normed_one, axis=1), unit_one, inverse_one, attn_gain
    )
    gains = m["gains"]
    gains[0] = jnp.concatenate([attn_gain_part, ffn_gain_part, jnp.zeros((6, D), F32)], axis=0)
    gain_copies = [
        at.send(gains.at[0], gains.at[1], up_device),
        at.send(gains.at[0], gains.at[2], down_device),
        at.send(gains.at[0], gains.at[3], far_device),
    ]
    input_grad = m["input_grad"]
    input_grad[row] = (d_tokens + m["d_middle"][...]).astype(BF16)

    @pl.when(not_(own_core))
    def _():
        gate_back().wait_recv()

    for r in range(2):
        source = r * 2 + row

        @pl.when(not_((source == y) & (low == s)))
        def _():
            at.wire(
                sums.at[0, :, lanes],
                ffn_total.at[at.z, at.x, r, :, lanes],
                mate,
                back_slot + r,
            ).wait_recv()

    ffn_spread = Spread(at, ffn_total)
    ffn_spread.first()

    for copy in side_copies + q_copies:
        copy.wait_recv()
    first_all = first_ring[...].reshape(4 * OWN, HALF)
    q_grad = dot_tn(first_all, d_q_ring[...].reshape(4 * OWN, HALF)).astype(BF16)
    o_grad = dot_tn(
        attn_ring[...].reshape(4 * OWN, HALF), d_y1_ring[...].reshape(4 * OWN, HALF)
    ).astype(BF16)
    qo_two = m["qo_two"]
    for b in range(2):
        pick = slice(b * 240, (b + 1) * 240)
        qo_two[b, 0:HALF, :] = jnp.concatenate([q_grad[:, pick], o_grad[:, pick]], axis=1)
        qo_two[b, HALF:, :] = jnp.zeros((32, HALF), BF16)
    qo_ranks = RankSum(
        at, qo_two, m["qo_mate"], m["qo_kept"], m["qo_ranks"], m["qo_sum"], m["attn_total"]
    )
    ffn_spread.second()
    qo_ranks.start()

    for copy in kv_out + gain_copies:
        copy.wait_recv()
    kv_grad = dot_tn(first_all, d_kv_ring[...].reshape(4 * OWN, 320)).astype(BF16)
    gain_sum = (gains[0] + gains[1] + gains[2] + gains[3])[0:2].astype(BF16)
    gain_rows = [gain_sum[g : g + 1, p * 160 : (p + 1) * 160] for g in range(2) for p in range(6)]
    gain_block = jnp.concatenate(gain_rows + [jnp.zeros((20, 160), BF16)], axis=0)
    kv_two = m["kv_two"]
    for b in range(2):
        kv_two[b, 0:HALF, :] = jnp.concatenate(
            [kv_grad[:, b * 80 : (b + 1) * 80], kv_grad[:, 160 + b * 80 : 160 + (b + 1) * 80]], axis=1
        )
        kv_two[b, HALF:, :] = gain_block
    kv_ranks = RankSum(
        at, kv_two, m["kv_grad_mate"], m["kv_kept"], m["kv_ranks"], m["kv_sum"], m["kv_total"]
    )
    kv_ranks.start()
    qo_ranks.scatter()
    ffn_spread.third()
    kv_ranks.scatter()

    block_out = m["block_out"]
    block_out[row] = (m["middle"][...] + ffn.finish()).astype(BF16)
    out_copies = [
        at.send(block_out.at[row], block_out.at[row], far_device),
        at.send(input_grad.at[row], input_grad.at[row], far_device),
    ]

    qo_ranks.reduce()
    m["attn_total"][own_rows] = m["qo_sum"][...]
    qo_ranks.gather()
    kv_ranks.reduce()
    m["kv_total"][own_rows] = m["kv_sum"][...]
    kv_ranks.gather()
    for copy in out_copies:
        copy.wait_recv()
    ffn_spread.finish()
    qo_ranks.finish()
    kv_ranks.finish()

    for copy in at.open:
        copy.wait_send()
    gate_mate(row).wait_send()
    for spread in spreads + (ffn_spread,):
        spread.drain()

    @pl.when(active)
    def _():
        for n in range(3):
            o_copy(n).wait_send()
        for r in range(2):
            target, copy = down_copy(r)

            @pl.when(target != y)
            def _():
                copy.wait_send()

        @pl.when(not_(own_core))
        def _():
            for n, part in gate_copies:
                gate_copy(n, part).wait_send()

    @pl.when(not_(own_core))
    def _():
        gate_back().wait_send()

    for j in range(2):
        copy = down_back(j)

        @pl.when(not_((owner == y) & (s == j)))
        def _():
            copy.wait_send()


def results_kernel(*refs):
    ins, outs, held, sems = refs[:5], refs[5:16], refs[16:21], refs[21]
    copies = [
        pltpu.make_async_copy(src, dst, sems.at[n]) for n, (src, dst) in enumerate(zip(ins, held))
    ]
    for copy in copies:
        copy.start()
    block_in, input_in, attn_in, kv_in, ffn_in = held
    block, inputs, attn_gain, q_grad, k_grad, v_grad, o_grad, ffn_gain, gate, raise_, down = outs
    for copy in copies:
        copy.wait()
    block[...] = block_in[...].reshape(2 * OWN, D).astype(F32).T
    inputs[...] = input_in[...].reshape(2 * OWN, D).astype(F32).T
    q_grad[...] = attn_in[0:HALF, 0:240].astype(F32)
    o_grad[...] = attn_in[0:HALF, 240:480].astype(F32)
    kv_grad = kv_in[0:HALF, :].astype(F32).T
    k_grad[...] = kv_grad[0:80]
    v_grad[...] = kv_grad[80:160]
    gains = kv_in[HALF:512, :].astype(F32)
    for p in range(6):
        attn_gain[:, p * 160 : (p + 1) * 160] = gains[p : p + 1]
        ffn_gain[:, p * 160 : (p + 1) * 160] = gains[6 + p : 7 + p]
    gate[...] = ffn_in[0:CHUNKS, :, :, 0:UNITS].reshape(HALF, UNITS).astype(F32)
    raise_[...] = ffn_in[0:CHUNKS, :, :, UNITS : 2 * UNITS].reshape(HALF, UNITS).astype(F32)
    for i in range(CHUNKS):
        for r in range(2):
            down[16 * i : 16 * i + 16, r * UNITS : (r + 1) * UNITS] = ffn_in[
                i, r, :, 2 * UNITS :
            ].astype(F32)


def shards(
    hidden_in,
    segment_ids,
    attn_gain,
    q_weight,
    k_weight,
    v_weight,
    o_weight,
    ffn_gain,
    gate_weight,
    up_weight,
    down_weight,
    d_out,
):
    frequency = np.float32(rope_base) ** (-np.arange(HEAD_DIM // 2, dtype=np.float32) * 2 / HEAD_DIM)
    freq = jnp.asarray(np.tile(frequency.astype(np.float32), 4)[None, :])
    scratch = [
        pltpu.VMEM(*kind) if isinstance(kind, tuple) else kind for kind in SCRATCH.values()
    ]
    local = pl.BlockSpec(memory_space=pltpu.VMEM)
    kept = pl.pallas_call(
        layer_kernel,
        out_shape=[
            jax.ShapeDtypeStruct((2, OWN, D), BF16),
            jax.ShapeDtypeStruct((2, OWN, D), BF16),
            jax.ShapeDtypeStruct((512, HALF), BF16),
            jax.ShapeDtypeStruct((512, 160), BF16),
            jax.ShapeDtypeStruct((4, 4, 2, 16, 1920), BF16),
        ],
        in_specs=[local] * len(IN_NAMES),
        out_specs=[local] * len(OUT_NAMES),
        scratch_shapes=scratch,
        compiler_params=pltpu.CompilerParams(
            collective_id=1, has_side_effects=True, vmem_limit_bytes=60 * 1024 * 1024
        ),
    )(
        hidden_in.T,
        segment_ids[None, :],
        freq,
        attn_gain[None, :],
        ffn_gain[None, :],
        q_weight,
        k_weight.T,
        v_weight.T,
        o_weight,
        gate_weight,
        up_weight,
        down_weight.T,
        d_out.T,
    )
    shapes = [
        (D, 2 * OWN), (D, 2 * OWN), (1, D), (HALF, 240), (80, HALF), (80, HALF),
        (HALF, 240), (1, D), (HALF, UNITS), (HALF, UNITS), (240, 2 * UNITS),
    ]
    outs = pl.pallas_call(
        results_kernel,
        out_shape=[jax.ShapeDtypeStruct(shape, F32) for shape in shapes],
        in_specs=[pl.BlockSpec(memory_space=pl.ANY)] * len(OUT_NAMES),
        out_specs=[local] * len(shapes),
        scratch_shapes=[
            pltpu.VMEM((2, OWN, D), BF16),
            pltpu.VMEM((2, OWN, D), BF16),
            pltpu.VMEM((512, HALF), BF16),
            pltpu.VMEM((512, 160), BF16),
            pltpu.VMEM((16, 2, 16, 1920), BF16),
            pltpu.SemaphoreType.DMA((5,)),
        ],
        compiler_params=pltpu.CompilerParams(vmem_limit_bytes=62 * 1024 * 1024),
    )(*kept[:4], kept[4].reshape(16, 2, 16, 1920))
    turned = (0, 1, 4, 5, 10)
    outs = [out.T if i in turned else out for i, out in enumerate(outs)]
    outs[2], outs[7] = outs[2].reshape(D), outs[7].reshape(D)
    return tuple(outs)


def solution(mesh):
    rows, blocks = P(("dp", "col"), None), P("row", "col")
    return jax.shard_map(
        shards,
        mesh=mesh,
        in_specs=(
            rows, P(("dp", "col")), P(), blocks, blocks, blocks, blocks, P(), blocks, blocks, blocks, rows,
        ),
        out_specs=(rows, rows, P(), blocks, blocks, blocks, blocks, P(), blocks, blocks, blocks),
        check_vma=False,
    )
```

```python
import types

import jax
import jax.numpy as jnp
import numpy as np
from jax import lax
from jax.experimental import pallas as pl
from jax.experimental.pallas import tpu as pltpu
from jax.sharding import PartitionSpec as P

HEADS = 15
KV_HEADS = 5
HEAD_DIM = 64
SHARE = HEADS // KV_HEADS
D = 960
HALF = 480
QD = 960
KVD = 320
UNITS = 640
OWN = 128
KEYS = 1024
SCALING = HEAD_DIM ** (-0.5)
MESH = pl.DeviceIdType.MESH
F32 = jnp.float32
BF16 = jnp.bfloat16
SLOTS = 288
CHUNKS = 15

norm_eps = 1e-05
rope_base = 100000.0


def dot(a, b):
    return jnp.dot(a, b, preferred_element_type=F32)


def dot_nt(a, b):
    return lax.dot_general(a, b, (((1,), (1,)), ((), ())), preferred_element_type=F32)


def dot_tn(a, b):
    return lax.dot_general(a, b, (((0,), (0,)), ((), ())), preferred_element_type=F32)


def heads_of(x, group):
    first = group * SHARE
    return jnp.concatenate(
        [x[:, (first + j) * HEAD_DIM : (first + j + 1) * HEAD_DIM] for j in range(SHARE)], axis=0
    )


def rows_of(index, count):
    return pl.ds(pl.multiple_of(index * count, count), count)


class Place:
    def __init__(self, send_sem, recv_sem):
        col = lax.axis_index("col")
        self.dp, self.row = lax.axis_index("dp"), lax.axis_index("row")
        self.ranks = lax.axis_size("dp")
        self.z, self.x = self.dp // 4, self.dp % 4
        self.low, self.s = col // 2, col % 2
        self.y = self.row * 2 + self.low
        self.up, self.down, self.far = (self.y + 1) % 4, (self.y + 3) % 4, (self.y + 2) % 4
        self.send_sem, self.recv_sem, self.used = send_sem, recv_sem, 0
        self.open = []

    def device(self, y, s):
        return (self.dp, y // 2, (y % 2) * 2 + s)

    def rank(self, z, x):
        return (z * 4 + x, self.row, self.low * 2 + self.s)

    def peer(self, k):
        return ((self.dp + k) % self.ranks, self.row, self.low * 2 + self.s)

    def slots(self, count):
        first = self.used
        self.used += count
        assert self.used <= SLOTS
        return first

    def wire(self, src, dst, other, slot, recv_slot=None):
        return pltpu.make_async_remote_copy(
            src_ref=src,
            dst_ref=dst,
            send_sem=self.send_sem.at[slot],
            recv_sem=self.recv_sem.at[slot if recv_slot is None else recv_slot],
            device_id=other,
            device_id_type=MESH,
        )

    def send(self, src, dst, other):
        copy = self.wire(src, dst, other, self.slots(1))
        copy.start()
        self.open.append(copy)
        return copy

    def others(self):
        others = [self.peer(k) for k in range(1, self.ranks)]
        others += [self.device(self.y, 1 - self.s)]
        for y in (self.up, self.down, self.far):
            others += [self.device(y, self.s), self.device(y, 1 - self.s)]
        return others

    def greet(self):
        barrier = pltpu.get_barrier_semaphore()
        for other in self.others():
            pl.semaphore_signal(barrier, inc=1, device_id=other, device_id_type=MESH)

    def meet(self):
        pl.semaphore_wait(pltpu.get_barrier_semaphore(), len(self.others()))


class Gather:
    def __init__(self, at, buf, rows, split, index=None):
        self.at, self.buf = at, buf
        self.both = index is not None
        if index is None:
            self.mine, self.low, self.high, self.opposite = 0, 1, 2, 3
            self.to_up, self.to_down, self.on_up, self.on_down = 1, 2, 3, 3
        else:
            self.mine, self.low = index(at.y, at.s), index(at.down, at.s)
            self.high, self.opposite = index(at.up, at.s), index(at.far, at.s)
            self.to_up, self.to_down = self.mine, self.mine
            self.on_up, self.on_down = self.low, self.high
        self.first, self.second = pl.ds(0, split), pl.ds(split, rows - split)
        self.up_device, self.down_device = at.device(at.up, at.s), at.device(at.down, at.s)
        self.mate = at.device(at.y, 1 - at.s)
        self.from_mate = []

    def ship(self, index, part, to_index, other):
        return self.at.send(self.buf.at[index, part], self.buf.at[to_index, part], other)

    def to_mate(self, index):
        if self.both:
            self.from_mate.append(self.at.send(self.buf.at[index], self.buf.at[index], self.mate))

    def start(self):
        self.up_first = self.ship(self.mine, self.first, self.to_up, self.up_device)
        self.down_second = self.ship(self.mine, self.second, self.to_down, self.down_device)
        self.up_second = self.ship(self.mine, self.second, self.to_up, self.up_device)
        self.down_first = self.ship(self.mine, self.first, self.to_down, self.down_device)
        self.to_mate(self.mine)

    def relay(self):
        self.up_first.wait_recv()
        self.up_far = self.ship(self.low, self.first, self.on_up, self.up_device)
        self.down_second.wait_recv()
        self.down_far = self.ship(self.high, self.second, self.on_down, self.down_device)

    def near(self):
        self.up_second.wait_recv()
        self.to_mate(self.low)
        self.down_first.wait_recv()
        self.to_mate(self.high)

    def finish(self):
        self.up_far.wait_recv()
        self.down_far.wait_recv()
        self.to_mate(self.opposite)
        for copy in self.from_mate:
            copy.wait_recv()


class Reduce:
    def __init__(self, at, blocks, early, sums, landed):
        self.at, self.blocks = at, blocks
        self.early, self.sums, self.landed = early, sums, landed
        self.up_device, self.down_device = at.device(at.up, at.s), at.device(at.down, at.s)

    def start_far(self):
        at, far = self.at, self.blocks.at[3]
        self.first = at.send(far.at[0], self.early.at[0], self.down_device)
        self.second = at.send(far.at[1], self.early.at[1], self.up_device)

    def start_near(self):
        at = self.at
        self.third = at.send(self.blocks.at[1, 1], self.landed.at[0, 1], self.down_device)
        self.fourth = at.send(self.blocks.at[2, 0], self.landed.at[1, 0], self.up_device)

    def middle(self):
        at, blocks, early, sums = self.at, self.blocks, self.early, self.sums
        self.first.wait_recv()
        sums[0] = (blocks[1, 0].astype(F32) + early[0].astype(F32)).astype(BF16)
        self.fifth = at.send(sums.at[0], self.landed.at[0, 0], self.down_device)
        self.second.wait_recv()
        sums[1] = (blocks[2, 1].astype(F32) + early[1].astype(F32)).astype(BF16)
        self.sixth = at.send(sums.at[1], self.landed.at[1, 1], self.up_device)

    def finish(self):
        for copy in (self.third, self.fourth, self.fifth, self.sixth):
            copy.wait_recv()
        total = (
            self.blocks[0].astype(F32) + self.landed[0].astype(F32) + self.landed[1].astype(F32)
        )
        return total.reshape(total.shape[0] * total.shape[1], total.shape[2])


class Far:
    def __init__(self, at, src, on_up, on_down, relay):
        self.at, self.src, self.on_up, self.on_down, self.buf = at, src, on_up, on_down, relay
        self.up_device, self.down_device = at.device(at.up, at.s), at.device(at.down, at.s)
        self.low, self.high = pl.ds(0, OWN // 2), pl.ds(OWN // 2, OWN // 2)

    def first(self):
        at = self.at
        self.to_up = at.send(self.src.at[self.low], self.buf.at[0], self.up_device)
        self.to_down = at.send(self.src.at[self.high], self.buf.at[1], self.down_device)

    def relay(self):
        at = self.at
        self.to_up.wait_recv()
        self.last_up = at.send(self.buf.at[0], self.on_up.at[self.low], self.up_device)
        self.to_down.wait_recv()
        self.last_down = at.send(self.buf.at[1], self.on_down.at[self.high], self.down_device)

    def finish(self):
        self.last_up.wait_recv()
        self.last_down.wait_recv()


class Spread:
    def __init__(self, at, buf, guard=None):
        self.at, self.buf, self.guard = at, buf, guard
        self.slot = at.slots(18)

    def guarded(self, act):
        if self.guard is None:
            act()
        else:
            pl.when(self.guard)(act)

    def along(self, half, second, step):
        at = self.at
        if (half == 0) != second:
            return at.rank((at.z + step) % 4, at.x)
        return at.rank(at.z, (at.x + step) % 4)

    def first_copy(self, half, n):
        own = self.buf.at[self.at.z, self.at.x, half]
        return self.at.wire(own, own, self.along(half, False, (1, 3, 2)[n]), self.slot + half * 9 + n)

    def block(self, half, part, back):
        at, pair = self.at, pl.ds(2 * part, 2)
        if half == 0:
            return self.buf.at[pair, (at.x + 4 - back) % 4, half]
        return self.buf.at[(at.z + 4 - back) % 4, pair, half]

    def second_copy(self, half, n):
        step, part = ((1, 0), (3, 1), (1, 1), (3, 0))[n]
        src = self.block(half, part, 0)
        return self.at.wire(src, src, self.along(half, True, step), self.slot + half * 9 + 3 + n)

    def third_copy(self, half, n):
        step, part = ((1, 0), (3, 1))[n]
        src = self.block(half, part, step)
        return self.at.wire(src, src, self.along(half, True, step), self.slot + half * 9 + 7 + n)

    def first(self):
        def act():
            for half in range(2):
                for n in range(3):
                    self.first_copy(half, n).start()

        self.guarded(act)

    def second(self):
        def act():
            for half in range(2):
                for n in range(3):
                    self.first_copy(half, n).wait_recv()
                for n in range(4):
                    self.second_copy(half, n).start()

        self.guarded(act)

    def third(self):
        def act():
            for n in range(2):
                for half in range(2):
                    self.second_copy(half, n).wait_recv()
                    self.third_copy(half, n).start()

        self.guarded(act)

    def finish(self):
        def act():
            for half in range(2):
                for n in range(2, 4):
                    self.second_copy(half, n).wait_recv()
                for n in range(2):
                    self.third_copy(half, n).wait_recv()

        self.guarded(act)

    def drain(self):
        def act():
            for half in range(2):
                for n in range(3):
                    self.first_copy(half, n).wait_send()
                for n in range(4):
                    self.second_copy(half, n).wait_send()
                for n in range(2):
                    self.third_copy(half, n).wait_send()

        self.guarded(act)


class Collect:
    def __init__(self, at, kept, early, sums, landed, four, parts, total):
        self.at, self.kept, self.early, self.sums = at, kept, early, sums
        self.landed, self.four, self.parts, self.total = landed, four, parts, total

    def along(self, half, second, step):
        at = self.at
        if (half == 1) != second:
            return at.rank((at.z + step) % 4, at.x)
        return at.rank(at.z, (at.x + step) % 4)

    def block(self, half, step, part):
        at = self.at
        pair = slice(None) if part is None else pl.ds(2 * part, 2)
        if half == 0:
            return (pair, (at.x + step) % 4, half)
        return ((at.z + step) % 4, pair, half)

    def start(self):
        at, kept = self.at, self.kept
        self.far, self.near = {}, []
        for half in range(2):
            for n, step in ((0, 3), (1, 1)):
                self.far[half, n] = at.send(
                    kept.at[self.block(half, 2, n)], self.early.at[half, n], self.along(half, False, step)
                )
        for half in range(2):
            for n, step in ((0, 3), (1, 1)):
                self.near.append(
                    at.send(
                        kept.at[self.block(half, step, 1 - n)],
                        self.landed.at[half, n, pl.ds(2 * (1 - n), 2)],
                        self.along(half, False, step),
                    )
                )

    def middle(self):
        at, kept = self.at, self.kept
        for half in range(2):
            for n, step in ((0, 3), (1, 1)):
                self.far[half, n].wait_recv()
                self.sums[half, n] = (
                    kept[self.block(half, step, n)].astype(F32) + self.early[half, n].astype(F32)
                ).astype(BF16)
                self.near.append(
                    at.send(
                        self.sums.at[half, n],
                        self.landed.at[half, n, pl.ds(2 * n, 2)],
                        self.along(half, False, step),
                    )
                )

    def second(self):
        at = self.at
        for copy in self.near:
            copy.wait_recv()
        self.last = []
        for half in range(2):
            self.four[half] = (
                self.kept[self.block(half, 0, None)].astype(F32)
                + self.landed[half, 0].astype(F32)
                + self.landed[half, 1].astype(F32)
            ).astype(BF16)
            here = at.z if half == 0 else at.x
            for n, step in enumerate((1, 3, 2)):
                self.last.append(
                    at.send(
                        self.four.at[half, (here + step) % 4],
                        self.parts.at[half, n],
                        self.along(half, True, step),
                    )
                )

    def reduce(self):
        at = self.at
        for copy in self.last:
            copy.wait_recv()
        for half in range(2):
            acc = self.four[half, at.z if half == 0 else at.x].astype(F32)
            for n in range(3):
                acc = acc + self.parts[half, n].astype(F32)
            self.total[half] = acc.astype(BF16)


def unit_rows(values):
    inverse = lax.rsqrt(jnp.mean(values * values, axis=-1, keepdims=True) + norm_eps)
    return values * inverse, inverse


def norm_back(gradient, unit, inverse, gain_vec):
    scaled = gradient * gain_vec
    inner_sum = jnp.mean(scaled * unit, axis=1, keepdims=True)
    return (
        inverse * (scaled - unit * inner_sum),
        jnp.sum(gradient * unit, axis=0, keepdims=True),
    )


def turn(x, cosine, sine):
    half = HEAD_DIM // 2
    lane = lax.broadcasted_iota(jnp.int32, x.shape, 1) % HEAD_DIM
    swapped = jnp.where(lane < half, pltpu.roll(x, 128 - half, 1), pltpu.roll(x, half, 1))
    return x * cosine + swapped * sine


def turn_all(x, cosine, sine):
    width = x.shape[1]
    pieces = []
    for first in range(0, width, 128):
        piece = x[:, first : min(first + 128, width)]
        if piece.shape[1] < 128:
            wide = jnp.concatenate([piece, jnp.zeros_like(piece)], axis=1)
            piece = turn(wide, cosine, sine)[:, : piece.shape[1]]
        else:
            piece = turn(piece, cosine, sine)
        pieces.append(piece)
    return jnp.concatenate(pieces, axis=1)


IN_NAMES = ("hidden", "ids_in", "freq", "attn_gain", "ffn_gain")
IN_NAMES += ("q_w", "k_w", "v_w", "o_w", "gate_w", "up_w", "down_w", "d_out")
SCRATCH = dict(
    weights=((8, 400, HALF), BF16),
    o_parts=((2, 4, 4, 2, 2, 16, HALF), BF16),
    tokens=((2, OWN, D), BF16),
    own_o=((240, HALF), BF16),
    ids=((8, 16, OWN), BF16),
    normed_one=((2, OWN, HALF), BF16),
    bias=((OWN, KEYS), F32),
    cosine=((OWN, 128), F32),
    sine=((OWN, 128), F32),
    queries=((OWN, QD), BF16),
    kv=((8, OWN, 640), BF16),
    lse=((KV_HEADS, SHARE * OWN, 1), F32),
    attn=((OWN, QD), BF16),
    attn_halves=((2, OWN, HALF), BF16),
    attn_ring=((4, OWN, HALF), BF16),
    first_ring=((4, OWN, HALF), BF16),
    d_out_ring=((4, OWN, D), BF16),
    middle=((OWN, D), F32),
    normed_ring=((4, OWN, D), BF16),
    gate_up=((D, 2 * UNITS), BF16),
    down_parts=((2, 4, 4, 2, 16, UNITS), BF16),
    gate_land=((4, 4, 2, 16, 2 * UNITS), BF16),
    down=((D, UNITS), BF16),
    units=((4, OWN, UNITS), BF16),
    d_gate_up=((4, OWN, 2 * UNITS), BF16),
    ffn_parts=((4, 2, OWN // 2, D), BF16),
    ffn_early=((2, OWN // 2, D), BF16),
    ffn_sums=((2, OWN // 2, D), BF16),
    ffn_landed=((2, 2, OWN // 2, D), BF16),
    dn_parts=((4, 2, OWN // 2, D), BF16),
    dn_early=((2, OWN // 2, D), BF16),
    dn_sums=((2, OWN // 2, D), BF16),
    dn_landed=((2, 2, OWN // 2, D), BF16),
    ffn_halves=((2, 512, 1920), BF16),
    ffn_mate=((512, 1920), BF16),
    ffn_kept=((4, 4, 2, 16, 1920), BF16),
    ffn_far=((2, 2, 2, 16, 1920), BF16),
    ffn_pairs=((2, 2, 2, 16, 1920), BF16),
    ffn_near=((2, 2, 4, 16, 1920), BF16),
    ffn_four=((2, 4, 16, 1920), BF16),
    ffn_last=((2, 3, 16, 1920), BF16),
    ffn_sum=((2, 16, 1920), BF16),
    d_middle=((OWN, D), F32),
    d_y1_halves=((2, OWN, HALF), BF16),
    d_y1_ring=((4, OWN, HALF), BF16),
    d_kv=((8, OWN, 640), BF16),
    kv_mate=((4, OWN, 640), BF16),
    kv_parts=((4, 2, OWN // 2, 640), BF16),
    kv_early=((2, OWN // 2, 640), BF16),
    kv_sums=((2, OWN // 2, 640), BF16),
    kv_landed=((2, 2, OWN // 2, 640), BF16),
    d_q=((2, OWN, HALF), BF16),
    d_q_ring=((4, OWN, HALF), BF16),
    d_kv_own=((2, OWN, 320), BF16),
    d_kv_ring=((4, OWN, 320), BF16),
    gains=((4, 8, D), F32),
    qo_two=((2, 512, HALF), BF16),
    qo_mate=((512, HALF), BF16),
    kv_two=((2, 512, 160), BF16),
    kv_grad_mate=((512, 160), BF16),
    attn_kept=((4, 4, 2, 16, 640), BF16),
    attn_far=((2, 2, 2, 16, 640), BF16),
    attn_pairs=((2, 2, 2, 16, 640), BF16),
    attn_near=((2, 2, 4, 16, 640), BF16),
    attn_four=((2, 4, 16, 640), BF16),
    attn_last=((2, 3, 16, 640), BF16),
    attn_sum=((2, 16, 640), BF16),
    attn_relay=((2, OWN // 2, HALF), BF16),
    d_y1_relay=((2, OWN // 2, HALF), BF16),
    d_q_relay=((2, OWN // 2, HALF), BF16),
    d_kv_relay=((2, OWN // 2, 320), BF16),
    block_relay=((2, OWN // 2, D), BF16),
    input_relay=((2, OWN // 2, D), BF16),
    block_out=((2, OWN, D), BF16),
    input_grad=((2, OWN, D), BF16),
    attn_total=((4, 4, 2, 16, 640), BF16),
    ffn_total=((4, 4, 2, 16, 1920), BF16),
    out_sem=pltpu.SemaphoreType.DMA((4,)),
    send_sem=pltpu.SemaphoreType.DMA((SLOTS,)),
    recv_sem=pltpu.SemaphoreType.DMA((SLOTS,)),
)


def block_of(y, s):
    return ((y % 2) * 2 + s) * 2 + y // 2


def layer_kernel(*refs):
    count = len(IN_NAMES)
    outs, refs = refs[count : count + 4], refs[:count] + refs[count + 4 :]
    m = types.SimpleNamespace(**dict(zip(IN_NAMES + tuple(SCRATCH), refs)))
    leaving = []

    def leave(n, src):
        copy = pltpu.make_async_copy(src, outs[n], m.out_sem.at[n])
        copy.start()
        leaving.append(copy)

    at = Place(m.send_sem, m.recv_sem)
    row, low, s, y, dp = at.row, at.low, at.s, at.y, at.dp
    mate = at.device(y, 1 - s)
    up_device, down_device = at.device(at.up, s), at.device(at.down, s)
    far_device, cross = at.device(at.far, s), at.device(at.far, 1 - s)
    mine = block_of(y, s)
    active = dp < CHUNKS
    not_ = jnp.logical_not

    at.greet()

    weights, ids = m.weights, m.ids
    weights[mine, 0:240] = m.q_w[...].T
    weights[mine, 240:320] = m.k_w[...]
    weights[mine, 320:400] = m.v_w[...]
    own_row = jnp.where(row == 0, m.ids_in[:, 0:OWN], m.ids_in[:, OWN:]).astype(F32)
    ids[mine] = jnp.broadcast_to(own_row, (16, OWN)).astype(BF16)
    m.own_o[...] = m.o_w[...].T
    at.meet()

    gate_up, o_parts, down_parts = m.gate_up, m.o_parts, m.down_parts
    o_slot, down_slot, gate_slot = at.slots(3), at.slots(2), at.slots(4)
    gate_mate_slot = at.slots(1)
    own_core = s == row
    strip = rows_of(dp, 16)

    def o_copy(n):
        other = (up_device, down_device, far_device)[n]
        return at.wire(m.own_o.at[strip], o_parts.at[s, at.z, at.x, row, low], other, o_slot + n)

    def down_copy(r):
        target = r * 2 + row
        return target, at.wire(
            m.down_w.at[strip, pl.ds(r * UNITS, UNITS)],
            down_parts.at[s, at.z, at.x, low],
            at.device(target, s),
            down_slot + r,
            down_slot + low,
        )

    def down_arrive(a):
        return low * 2 + a, at.wire(
            m.down_w.at[strip, pl.ds(0, UNITS)],
            down_parts.at[s, at.z, at.x, a],
            up_device,
            down_slot + a,
        )

    gate_land = m.gate_land

    def gate_copy(n, part):
        source = (m.gate_w, m.up_w)[n]
        return at.wire(
            source.at[pl.ds(pl.multiple_of(dp * 32 + 16 * part, 16), 16)],
            gate_land.at[at.z, at.x, part, :, pl.ds(UNITS * n, UNITS)],
            cross,
            gate_slot + 2 * n + part,
        )

    gate_copies = [(n, part) for n in range(2) for part in range(2)]
    o_spread = Spread(at, o_parts.at[s])
    down_spread = Spread(at, down_parts.at[s])
    gate_spread = Spread(at, gate_land, not_(own_core))
    spreads = (o_spread, gate_spread, down_spread)

    def gate_mate(half):
        rows = pl.ds(pl.multiple_of(half * HALF, 32), HALF)
        return at.wire(gate_up.at[rows], gate_up.at[rows], mate, gate_mate_slot)

    gather_w = Gather(at, weights, 400, 192, block_of)
    gather_w.start()
    ids_copies = [at.send(ids.at[mine], ids.at[mine], mate)]
    for other in (at.up, at.down, at.far):
        for core in (s, 1 - s):
            ids_copies.append(at.send(ids.at[mine], ids.at[mine], at.device(other, core)))

    @pl.when(active)
    def _():
        o_parts[s, at.z, at.x, row, low] = m.own_o[strip]
        for n in range(3):
            o_copy(n).start()
        for r in range(2):
            target, copy = down_copy(r)

            @pl.when(target == y)
            def _():
                down_parts[s, at.z, at.x, low] = m.down_w[strip, r * UNITS : (r + 1) * UNITS]

            @pl.when(target != y)
            def _():
                copy.start()

        @pl.when(not_(own_core))
        def _():
            for n, part in gate_copies:
                gate_copy(n, part).start()

    @pl.when(not_(active))
    def _():
        o_parts[s, at.z, at.x] = jnp.zeros((2, 2, 16, HALF), BF16)
        down_parts[s, at.z, at.x] = jnp.zeros((2, 16, UNITS), BF16)
        gate_land[at.z, at.x] = jnp.zeros((2, 16, 2 * UNITS), BF16)

    @pl.when(own_core)
    def _():
        rows = pl.ds(pl.multiple_of(row * HALF, 32), HALF)
        gate_up[rows, 0:UNITS] = m.gate_w[...]
        gate_up[rows, UNITS:] = m.up_w[...]
        gate_mate(row).start()

    tokens_two, d_out_ring = m.tokens, m.d_out_ring
    hidden, d_out = m.hidden[...].T, m.d_out[...].T
    tokens_two[0], tokens_two[1] = hidden[:OWN], hidden[OWN:]
    first_half = row == 0
    d_out_ring[0] = jnp.where(first_half, d_out[:OWN], d_out[OWN:])
    d_out_ring[3] = jnp.where(first_half, d_out[OWN:], d_out[:OWN])
    attn_gain, ffn_gain = m.attn_gain[...], m.ffn_gain[...]
    unit_one, _ = unit_rows(tokens_two[row].astype(F32))
    normed = (unit_one * attn_gain).astype(BF16)
    m.normed_one[0] = normed[:, :HALF]
    m.normed_one[1] = normed[:, HALF:]
    first_ring = m.first_ring
    first_ring[0] = m.normed_one[row]
    unit_far, _ = unit_rows(tokens_two[1 - row].astype(F32))
    normed_far = (unit_far * attn_gain).astype(BF16)
    first_ring[3] = jnp.where(first_half, normed_far[:, :HALF], normed_far[:, HALF:])

    gather_w.relay()

    for copy in ids_copies:
        copy.wait_recv()
    own_ids = jnp.broadcast_to(own_row, (OWN, OWN)).T[:, 0:1].astype(jnp.int32)
    docs = jnp.concatenate([ids[b, 0:1, :] for b in range(8)], axis=1).astype(F32).astype(jnp.int32)
    earlier = jnp.sum((docs < own_ids).astype(F32), axis=1, keepdims=True)
    start = (low * 2 + s) * 256 + row * OWN
    position = start + lax.broadcasted_iota(jnp.int32, (OWN, 1), 0)
    angles = (position.astype(F32) - earlier) * m.freq[...]
    lane = lax.broadcasted_iota(jnp.int32, (OWN, 128), 1) % HEAD_DIM
    sine = jnp.sin(angles)
    m.cosine[...] = jnp.cos(angles)
    m.sine[...] = jnp.where(lane < HEAD_DIM // 2, -sine, sine)
    key_at = lax.broadcasted_iota(jnp.int32, (OWN, KEYS), 1)
    allowed = (own_ids == docs) & (key_at <= position)
    m.bias[...] = jnp.where(allowed, 0.0, -jnp.inf).astype(F32)

    @pl.when(active)
    def _():
        for n in range(3):
            o_copy(n).wait_recv()
        for a in range(2):
            source, copy = down_arrive(a)

            @pl.when(source != y)
            def _():
                copy.wait_recv()

        @pl.when(not_(own_core))
        def _():
            for n, part in gate_copies:
                gate_copy(n, part).wait_recv()

    for spread in spreads:
        spread.first()

    gather_w.near()
    for spread in spreads:
        spread.second()
    gather_w.finish()
    parts = []
    for c in range(4):
        part = dot_nt(m.normed_one[0], weights[2 * c]) + dot_nt(m.normed_one[1], weights[2 * c + 1])
        parts.append(part.astype(BF16).astype(F32))
    cosine, sine = m.cosine[...], m.sine[...]
    k = jnp.concatenate([part[:, 240:320] for part in parts], axis=1)
    v = jnp.concatenate([part[:, 320:400] for part in parts], axis=1)
    kv = m.kv
    kv[mine] = jnp.concatenate([turn_all(k, cosine, sine), v], axis=1).astype(BF16)
    gather_kv = Gather(at, kv, OWN, OWN // 2, block_of)
    gather_kv.start()
    q = jnp.concatenate([part[:, 0:240] for part in parts], axis=1)
    m.queries[...] = turn_all(q, cosine, sine).astype(BF16)
    gather_kv.relay()
    for spread in spreads:
        spread.third()
    gather_kv.near()
    gather_kv.finish()
    d_out_copies = [
        at.send(d_out_ring.at[0], d_out_ring.at[1], up_device),
        at.send(d_out_ring.at[0], d_out_ring.at[2], down_device),
    ]

    o_spread.finish()
    o_mate = at.send(o_parts.at[s], o_parts.at[s], mate)

    for g in range(KV_HEADS):
        key = kv[:, :, g * HEAD_DIM : (g + 1) * HEAD_DIM].reshape(KEYS, HEAD_DIM)
        value = kv[:, :, KVD + g * HEAD_DIM : KVD + (g + 1) * HEAD_DIM].reshape(KEYS, HEAD_DIM)
        scores = dot_nt(heads_of(m.queries, g), key) * SCALING
        scores = scores.reshape(SHARE, OWN, KEYS) + m.bias[...][None]
        top = jnp.max(scores, axis=-1, keepdims=True)
        terms = jnp.exp(scores - top)
        total = jnp.sum(terms, axis=-1, keepdims=True)
        probs = (terms / total).astype(BF16).reshape(SHARE * OWN, KEYS)
        out = dot(probs, value).astype(BF16)
        for j in range(SHARE):
            head = (g * SHARE + j) * HEAD_DIM
            m.attn[:, head : head + HEAD_DIM] = out[j * OWN : (j + 1) * OWN]
        m.lse[g] = (top + jnp.log(total)).reshape(SHARE * OWN, 1)
    attn_halves = m.attn_halves
    attn_halves[0] = m.attn[:, :HALF]
    attn_halves[1] = m.attn[:, HALF:]
    o_mate.wait_recv()

    def o_block(r, c):
        return o_parts[c % 2, :, :, r, c // 2].reshape(256, HALF)[0:240]

    attn_out = [
        dot_nt(attn_halves[0], o_block(0, c)) + dot_nt(attn_halves[1], o_block(1, c)) for c in range(4)
    ]
    middle = tokens_two[row].astype(F32) + jnp.concatenate(attn_out, axis=1)
    m.middle[...] = middle
    unit_two, _ = unit_rows(middle)
    ring = m.normed_ring
    ring[0] = (unit_two * ffn_gain).astype(BF16)
    gather_n = Gather(at, ring, OWN, OWN // 2)
    gather_n.start()

    gate_spread.finish()

    @pl.when(not_(own_core))
    def _():
        rows = pl.ds(pl.multiple_of((1 - row) * HALF, 32), HALF)
        gate_up[rows] = gate_land[...].reshape(512, 2 * UNITS)[0:HALF]
        gate_mate(1 - row).start()

    down_spread.finish()
    down_mate = at.send(down_parts.at[s], down_parts.at[s], mate)
    gather_n.relay()
    down_mate.wait_recv()
    for c in range(4):
        m.down[c * 240 : (c + 1) * 240] = down_parts[c % 2, :, :, c // 2].reshape(256, UNITS)[0:240]
    for copy in d_out_copies:
        copy.wait_recv()
    gate_mate(row).wait_recv()

    ffn_parts, dn_parts = m.ffn_parts, m.dn_parts

    def feed(p):
        gate_and_up = dot(ring[p], gate_up[...]).astype(BF16)
        gate, raise_ = gate_and_up[:, :UNITS].astype(F32), gate_and_up[:, UNITS:].astype(F32)
        sig = 1.0 / (1.0 + jnp.exp(-gate))
        silu = gate * sig
        unit = (silu * raise_).astype(BF16)
        m.units[p] = unit
        d_unit = dot(d_out_ring[p], m.down[...])
        d_gate = (d_unit * raise_ * sig * (1.0 + gate * (1.0 - sig))).astype(BF16)
        d_up = (d_unit * silu).astype(BF16)
        m.d_gate_up[p] = jnp.concatenate([d_gate, d_up], axis=1)
        d_normed = dot_nt(m.d_gate_up[p], gate_up[...]).astype(BF16)
        dn_parts[p] = d_normed.reshape(2, OWN // 2, D)

    def feed_out(p):
        ffn_parts[p] = dot_nt(m.units[p], m.down[...]).astype(BF16).reshape(2, OWN // 2, D)

    dn = Reduce(at, dn_parts, m.dn_early, m.dn_sums, m.dn_landed)
    ffn = Reduce(at, ffn_parts, m.ffn_early, m.ffn_sums, m.ffn_landed)
    feed(0)
    gather_n.near()
    feed(1)
    feed(2)
    dn.start_near()
    gather_n.finish()
    feed(3)
    dn.start_far()
    for p in (3, 1, 2):
        feed_out(p)
    dn.middle()
    feed_out(0)

    halves = m.ffn_halves
    tokens_n = ring[...].reshape(4 * OWN, D)
    d_gate_up = m.d_gate_up[...].reshape(4 * OWN, 2 * UNITS)
    tokens_d = d_out_ring[...].reshape(4 * OWN, D)
    units = m.units[...].reshape(4 * OWN, UNITS)
    for h in range(2):
        halves[h, 0:HALF, 0 : 2 * UNITS] = dot_tn(tokens_n[:, h * HALF : (h + 1) * HALF], d_gate_up).astype(BF16)
        grad = dot_tn(tokens_d[:, h * HALF : (h + 1) * HALF], units).astype(BF16)
        for i in range(CHUNKS):
            halves[h, 32 * i : 32 * i + 16, 2 * UNITS :] = grad[16 * i : 16 * i + 16]
            halves[h, 32 * i + 16 : 32 * i + 32, 2 * UNITS :] = grad[240 + 16 * i : 256 + 16 * i]
        halves[h, HALF:, :] = jnp.zeros((32, 1920), BF16)
    ffn_pair = at.send(halves.at[1 - s], m.ffn_mate, mate)
    ffn_collect = Collect(
        at,
        m.ffn_kept,
        m.ffn_far,
        m.ffn_pairs,
        m.ffn_near,
        m.ffn_four,
        m.ffn_last,
        m.ffn_sum,
    )

    d_normed = dn.finish()
    middle = m.middle[...]
    unit_two, inverse_two = unit_rows(middle)
    d_middle, ffn_gain_part = norm_back(d_normed, unit_two, inverse_two, ffn_gain)
    d_middle = d_middle + d_out_ring[0].astype(F32)
    m.d_middle[...] = d_middle
    d_y1 = d_middle.astype(BF16)
    d_y1_halves, d_y1_ring = m.d_y1_halves, m.d_y1_ring
    d_y1_halves[0] = d_y1[:, :HALF]
    d_y1_halves[1] = d_y1[:, HALF:]
    d_attn = [0.0, 0.0]
    for c in range(4):
        for r in range(2):
            d_attn[r] = d_attn[r] + dot(d_y1[:, c * 240 : (c + 1) * 240], o_block(r, c))
    d_attn = jnp.concatenate(d_attn, axis=1).astype(BF16)

    up_low, up_row, down_row = 1 - low, at.up // 2, at.down // 2
    attn_ring, first_send = m.attn_ring, m.normed_one
    attn_far = Far(at, attn_halves.at[1 - row], attn_ring.at[3], attn_ring.at[3], m.attn_relay)
    d_y1_far = Far(at, d_y1_halves.at[low], d_y1_ring.at[3], d_y1_ring.at[3], m.d_y1_relay)
    attn_far.first()
    d_y1_far.first()
    side_copies = [
        at.send(d_y1_halves.at[up_low], d_y1_ring.at[1], up_device),
        at.send(d_y1_halves.at[up_low], d_y1_ring.at[2], down_device),
        at.send(attn_halves.at[up_row], attn_ring.at[1], up_device),
        at.send(attn_halves.at[down_row], attn_ring.at[2], down_device),
        at.send(first_send.at[up_row], first_ring.at[1], up_device),
        at.send(first_send.at[down_row], first_ring.at[2], down_device),
    ]
    attn_ring[0] = attn_halves[row]
    d_y1_ring[0] = d_y1_halves[low]

    d_kv = m.d_kv
    d_q = []
    for g in range(KV_HEADS):
        own = slice(g * HEAD_DIM, (g + 1) * HEAD_DIM)
        val = slice(KVD + g * HEAD_DIM, KVD + (g + 1) * HEAD_DIM)
        key = kv[:, :, own].reshape(KEYS, HEAD_DIM)
        value = kv[:, :, val].reshape(KEYS, HEAD_DIM)
        query, d_head = heads_of(m.queries, g), heads_of(d_attn, g)
        scores = dot_nt(query, key) * SCALING
        scores = scores.reshape(SHARE, OWN, KEYS) + m.bias[...][None]
        probs = jnp.exp(scores.reshape(SHARE * OWN, KEYS) - m.lse[g])
        d_probs = dot_nt(d_head, value)
        inner = jnp.sum(probs * d_probs, axis=-1, keepdims=True)
        d_scores = (probs * (d_probs - inner)).astype(BF16)
        d_query = dot(d_scores, key) * SCALING
        d_q += [d_query[j * OWN : (j + 1) * OWN] for j in range(SHARE)]
        d_kv[:, :, own] = (dot_tn(d_scores, query) * SCALING).astype(BF16).reshape(8, OWN, HEAD_DIM)
        d_kv[:, :, val] = dot_tn(probs.astype(BF16), d_head).astype(BF16).reshape(8, OWN, HEAD_DIM)
        if g == 0:
            ffn_pair.wait_recv()
            for z in range(4):
                for x in range(4):
                    rows = pl.ds(32 * (4 * z + x), 32)
                    both = halves[s, rows].astype(F32) + m.ffn_mate[rows].astype(F32)
                    m.ffn_kept[z, x] = both.astype(BF16).reshape(2, 16, 1920)
            ffn_collect.start()
        if g == 1:
            attn_far.relay()
            d_y1_far.relay()
        if g == 3:
            ffn_collect.middle()

    ffn_collect.second()
    kv_copies = []
    order = ((3, at.far), (1, at.down), (2, at.up), (0, y))
    for p, t in order:
        kv_copies.append(at.send(d_kv.at[block_of(t, 1 - s)], m.kv_mate.at[p], mate))
    cosine, sine = m.cosine[...], -m.sine[...]
    d_q = turn_all(jnp.concatenate(d_q, axis=1), cosine, sine).astype(BF16)
    kv_sum = Reduce(at, m.kv_parts, m.kv_early, m.kv_sums, m.kv_landed)
    for (p, t), copy in zip(order, kv_copies):
        copy.wait_recv()
        both = d_kv[block_of(t, s)].astype(F32) + m.kv_mate[p].astype(F32)
        m.kv_parts[p] = both.astype(BF16).reshape(2, OWN // 2, 640)
        if p == 3:
            kv_sum.start_far()
        if p == 2:
            kv_sum.start_near()
    d_q_two, d_q_ring = m.d_q, m.d_q_ring
    d_q_two[0], d_q_two[1] = d_q[:, :HALF], d_q[:, HALF:]
    kv_sum.middle()
    q_copies = [
        at.send(d_q_two.at[up_low], d_q_ring.at[1], up_device),
        at.send(d_q_two.at[up_low], d_q_ring.at[2], down_device),
    ]
    d_q_far = Far(at, d_q_two.at[low], d_q_ring.at[3], d_q_ring.at[3], m.d_q_relay)
    d_q_far.first()
    d_q_ring[0] = d_q_two[low]
    d_normed_one = [0.0, 0.0]
    for c in range(4):
        for r in range(2):
            d_normed_one[r] = d_normed_one[r] + dot(d_q[:, c * 240 : (c + 1) * 240], weights[2 * c + r, 0:240])

    ffn_collect.reduce()
    sums, ffn_total = m.ffn_sum, m.ffn_total
    gate_back_slot, back_slot = at.slots(1), at.slots(2)
    lanes = pl.ds(2 * UNITS, UNITS)
    owner = low * 2 + s

    def gate_back():
        both = pl.ds(0, 2 * UNITS)
        return at.wire(
            sums.at[:, :, both], ffn_total.at[at.z, at.x, :, :, both], cross, gate_back_slot
        )

    def down_back(j):
        return at.wire(
            sums.at[j, :, lanes],
            ffn_total.at[at.z, at.x, row, :, lanes],
            at.device(owner, j),
            back_slot + j,
            back_slot + row,
        )

    @pl.when(own_core)
    def _():
        ffn_total[at.z, at.x, :, :, 0 : 2 * UNITS] = sums[:, :, 0 : 2 * UNITS]

    @pl.when(not_(own_core))
    def _():
        gate_back().start()

    for j in range(2):
        here = (owner == y) & (s == j)
        copy = down_back(j)

        @pl.when(here)
        def _():
            ffn_total[at.z, at.x, row, :, 2 * UNITS :] = sums[j, :, 2 * UNITS :]

        @pl.when(not_(here))
        def _():
            copy.start()

    d_kv_sum = kv_sum.finish()
    d_k = turn_all(d_kv_sum[:, :KVD], cosine, sine).astype(BF16)
    d_v = d_kv_sum[:, KVD:].astype(BF16)
    d_kv_own, d_kv_ring = m.d_kv_own, m.d_kv_ring
    for a in range(2):
        d_kv_own[a] = jnp.concatenate(
            [d_k[:, a * 160 : (a + 1) * 160], d_v[:, a * 160 : (a + 1) * 160]], axis=1
        )
    d_kv_far = Far(at, d_kv_own.at[low], d_kv_ring.at[3], d_kv_ring.at[3], m.d_kv_relay)
    d_kv_far.first()
    kv_out = [
        at.send(d_kv_own.at[up_low], d_kv_ring.at[1], up_device),
        at.send(d_kv_own.at[up_low], d_kv_ring.at[2], down_device),
    ]
    d_kv_ring[0] = d_kv_own[low]
    d_q_far.relay()

    for c in range(4):
        piece = jnp.concatenate(
            [d_k[:, c * 80 : (c + 1) * 80], d_v[:, c * 80 : (c + 1) * 80]], axis=1
        )
        for r in range(2):
            d_normed_one[r] = d_normed_one[r] + dot(piece, weights[2 * c + r, 240:400])
    unit_one, inverse_one = unit_rows(tokens_two[row].astype(F32))
    d_tokens, attn_gain_part = norm_back(
        jnp.concatenate(d_normed_one, axis=1), unit_one, inverse_one, attn_gain
    )
    gains = m.gains
    gains[0] = jnp.concatenate([attn_gain_part, ffn_gain_part, jnp.zeros((6, D), F32)], axis=0)
    gain_copies = [
        at.send(gains.at[0], gains.at[1], up_device),
        at.send(gains.at[0], gains.at[2], down_device),
        at.send(gains.at[0], gains.at[3], far_device),
    ]
    input_grad = m.input_grad
    input_grad[row] = (d_tokens + m.d_middle[...]).astype(BF16)
    input_far = Far(
        at, input_grad.at[row], input_grad.at[1 - up_row], input_grad.at[1 - down_row], m.input_relay
    )
    d_kv_far.relay()
    ffn.start_far()
    ffn.start_near()

    @pl.when(not_(own_core))
    def _():
        gate_back().wait_recv()

    for r in range(2):
        source = r * 2 + row

        @pl.when(not_((source == y) & (low == s)))
        def _():
            at.wire(
                sums.at[0, :, lanes],
                ffn_total.at[at.z, at.x, r, :, lanes],
                mate,
                back_slot + r,
            ).wait_recv()

    ffn_spread = Spread(at, ffn_total)
    ffn_spread.first()

    for copy in side_copies + q_copies:
        copy.wait_recv()
    for far in (attn_far, d_y1_far, d_q_far):
        far.finish()
    first_all = first_ring[...].reshape(4 * OWN, HALF)
    q_grad = dot_tn(first_all, d_q_ring[...].reshape(4 * OWN, HALF)).astype(BF16)
    o_grad = dot_tn(
        attn_ring[...].reshape(4 * OWN, HALF), d_y1_ring[...].reshape(4 * OWN, HALF)
    ).astype(BF16)
    qo_two, kv_two = m.qo_two, m.kv_two
    for b in range(2):
        pick = slice(b * 240, (b + 1) * 240)
        qo_two[b, 0:HALF, :] = jnp.concatenate([q_grad[:, pick], o_grad[:, pick]], axis=1)
        qo_two[b, HALF:, :] = jnp.zeros((32, HALF), BF16)
    qo_pair = at.send(qo_two.at[1 - s], m.qo_mate, mate)
    ffn.middle()

    for copy in kv_out + gain_copies:
        copy.wait_recv()
    d_kv_far.finish()
    kv_grad = dot_tn(first_all, d_kv_ring[...].reshape(4 * OWN, 320)).astype(BF16)
    gain_sum = (gains[0] + gains[1] + gains[2] + gains[3])[0:2].astype(BF16)
    gain_rows = [gain_sum[g : g + 1, p * 160 : (p + 1) * 160] for g in range(2) for p in range(6)]
    gain_block = jnp.concatenate(gain_rows + [jnp.zeros((20, 160), BF16)], axis=0)
    for b in range(2):
        kv_two[b, 0:HALF, :] = jnp.concatenate(
            [kv_grad[:, b * 80 : (b + 1) * 80], kv_grad[:, 160 + b * 80 : 160 + (b + 1) * 80]], axis=1
        )
        kv_two[b, HALF:, :] = gain_block
    kv_pair = at.send(kv_two.at[1 - s], m.kv_grad_mate, mate)
    ffn_spread.second()
    attn_kept = m.attn_kept
    for pair, two, theirs, first in (
        (qo_pair, qo_two, m.qo_mate, 0),
        (kv_pair, kv_two, m.kv_grad_mate, HALF),
    ):
        pair.wait_recv()
        both = (two[s].astype(F32) + theirs[...].astype(F32)).astype(BF16)
        width = both.shape[1]
        attn_kept[:, :, :, :, first : first + width] = both.reshape(4, 4, 2, 16, width)

    attn_collect = Collect(
        at,
        attn_kept,
        m.attn_far,
        m.attn_pairs,
        m.attn_near,
        m.attn_four,
        m.attn_last,
        m.attn_sum,
    )
    attn_collect.start()
    input_far.first()
    ffn_spread.third()
    attn_collect.middle()
    block_out = m.block_out
    block_out[row] = (m.middle[...] + ffn.finish()).astype(BF16)
    block_far = Far(
        at, block_out.at[row], block_out.at[1 - up_row], block_out.at[1 - down_row], m.block_relay
    )
    block_far.first()
    input_far.relay()
    attn_collect.second()
    block_far.relay()
    attn_collect.reduce()
    attn_total = m.attn_total
    attn_total[at.z, at.x] = m.attn_sum[...]
    attn_spread = Spread(at, attn_total)
    attn_spread.first()
    ffn_spread.finish()
    leave(3, ffn_total)
    attn_spread.second()
    input_far.finish()
    leave(1, input_grad)
    block_far.finish()
    leave(0, block_out)
    attn_spread.third()
    attn_spread.finish()
    leave(2, attn_total)
    for copy in leaving:
        copy.wait()

    for copy in at.open:
        copy.wait_send()
    gate_mate(row).wait_send()
    for spread in spreads + (ffn_spread, attn_spread):
        spread.drain()

    @pl.when(active)
    def _():
        for n in range(3):
            o_copy(n).wait_send()
        for r in range(2):
            target, copy = down_copy(r)

            @pl.when(target != y)
            def _():
                copy.wait_send()

        @pl.when(not_(own_core))
        def _():
            for n, part in gate_copies:
                gate_copy(n, part).wait_send()

    @pl.when(not_(own_core))
    def _():
        gate_back().wait_send()

    for j in range(2):
        copy = down_back(j)

        @pl.when(not_((owner == y) & (s == j)))
        def _():
            copy.wait_send()


RESULTS = (
    (D, 2 * OWN), (D, 2 * OWN), (1, D), (HALF, 240), (80, HALF), (80, HALF),
    (HALF, 240), (1, D), (HALF, UNITS), (HALF, UNITS), (240, 2 * UNITS),
)


def results_kernel(*refs):
    ins, outs, held, made = refs[:4], refs[4:15], refs[15:19], refs[19:30]
    in_sem, out_sem = refs[30:]
    copies = [
        pltpu.make_async_copy(ins[n], held[n], in_sem.at[n]) for n in range(4)
    ]
    for n in (3, 0, 1, 2):
        copies[n].start()
    block_in, input_in, attn_in, ffn_in = held
    leaving = []

    def leave(n):
        copy = pltpu.make_async_copy(made[n], outs[n], out_sem.at[n])
        copy.start()
        leaving.append(copy)

    copies[3].wait()
    for n in range(2):
        made[8 + n][...] = (
            ffn_in[0:CHUNKS, :, :, n * UNITS : (n + 1) * UNITS].reshape(HALF, UNITS).astype(F32)
        )
        leave(8 + n)
    for i in range(CHUNKS):
        for r in range(2):
            made[10][16 * i : 16 * i + 16, r * UNITS : (r + 1) * UNITS] = ffn_in[
                i, r, :, 2 * UNITS :
            ].astype(F32)
    leave(10)
    for n in range(2):
        copies[n].wait()
        made[n][...] = held[n][...].reshape(2 * OWN, D).astype(F32).T
        leave(n)
    copies[2].wait()
    made[3][...] = attn_in[0:CHUNKS, :, :, 0:240].reshape(HALF, 240).astype(F32)
    leave(3)
    made[6][...] = attn_in[0:CHUNKS, :, :, 240:480].reshape(HALF, 240).astype(F32)
    leave(6)
    kv_grad = attn_in[0:CHUNKS, :, :, 480:640].reshape(HALF, 160).astype(F32).T
    made[4][...] = kv_grad[0:80]
    made[5][...] = kv_grad[80:160]
    leave(4)
    leave(5)
    gains = attn_in[CHUNKS, 0, :, 480:640].astype(F32)
    for p in range(6):
        made[2][:, p * 160 : (p + 1) * 160] = gains[p : p + 1]
        made[7][:, p * 160 : (p + 1) * 160] = gains[6 + p : 7 + p]
    leave(2)
    leave(7)
    for copy in leaving:
        copy.wait()


def shards(
    hidden_in,
    segment_ids,
    attn_gain,
    q_weight,
    k_weight,
    v_weight,
    o_weight,
    ffn_gain,
    gate_weight,
    up_weight,
    down_weight,
    d_out,
):
    frequency = np.float32(rope_base) ** (-np.arange(HEAD_DIM // 2, dtype=np.float32) * 2 / HEAD_DIM)
    freq = jnp.asarray(np.tile(frequency.astype(np.float32), 4)[None, :])
    scratch = [
        pltpu.VMEM(*kind) if isinstance(kind, tuple) else kind for kind in SCRATCH.values()
    ]
    local = pl.BlockSpec(memory_space=pltpu.VMEM)
    kept = pl.pallas_call(
        layer_kernel,
        out_shape=[
            jax.ShapeDtypeStruct((2, OWN, D), BF16),
            jax.ShapeDtypeStruct((2, OWN, D), BF16),
            jax.ShapeDtypeStruct((4, 4, 2, 16, 640), BF16),
            jax.ShapeDtypeStruct((4, 4, 2, 16, 1920), BF16),
        ],
        in_specs=[local] * len(IN_NAMES),
        out_specs=[pl.BlockSpec(memory_space=pl.ANY)] * 4,
        scratch_shapes=scratch,
        compiler_params=pltpu.CompilerParams(
            collective_id=1, has_side_effects=True, vmem_limit_bytes=60 * 1024 * 1024
        ),
    )(
        hidden_in.T,
        segment_ids[None, :],
        freq,
        attn_gain[None, :],
        ffn_gain[None, :],
        q_weight,
        k_weight.T,
        v_weight.T,
        o_weight,
        gate_weight,
        up_weight,
        down_weight.T,
        d_out.T,
    )
    outs = pl.pallas_call(
        results_kernel,
        out_shape=[jax.ShapeDtypeStruct(shape, F32) for shape in RESULTS],
        in_specs=[pl.BlockSpec(memory_space=pl.ANY)] * 4,
        out_specs=[pl.BlockSpec(memory_space=pl.ANY)] * len(RESULTS),
        scratch_shapes=[
            pltpu.VMEM((2, OWN, D), BF16),
            pltpu.VMEM((2, OWN, D), BF16),
            pltpu.VMEM((16, 2, 16, 640), BF16),
            pltpu.VMEM((16, 2, 16, 1920), BF16),
        ]
        + [pltpu.VMEM(shape, F32) for shape in RESULTS]
        + [pltpu.SemaphoreType.DMA((4,)), pltpu.SemaphoreType.DMA((len(RESULTS),))],
        compiler_params=pltpu.CompilerParams(vmem_limit_bytes=62 * 1024 * 1024),
    )(kept[0], kept[1], kept[2].reshape(16, 2, 16, 640), kept[3].reshape(16, 2, 16, 1920))
    turned = (0, 1, 4, 5, 10)
    outs = [out.T if i in turned else out for i, out in enumerate(outs)]
    outs[2], outs[7] = outs[2].reshape(D), outs[7].reshape(D)
    return tuple(outs)


def solution(mesh):
    rows, blocks = P(("dp", "col"), None), P("row", "col")
    return jax.shard_map(
        shards,
        mesh=mesh,
        in_specs=(
            rows, P(("dp", "col")), P(), blocks, blocks, blocks, blocks, P(), blocks, blocks, blocks, rows,
        ),
        out_specs=(rows, rows, P(), blocks, blocks, blocks, blocks, P(), blocks, blocks, blocks),
        check_vma=False,
    )
```

```python
import types

import jax
import jax.numpy as jnp
import numpy as np
from jax import lax
from jax.experimental import pallas as pl
from jax.experimental.pallas import tpu as pltpu
from jax.sharding import PartitionSpec as P

HEADS = 15
KV_HEADS = 5
HEAD_DIM = 64
SHARE = HEADS // KV_HEADS
D = 960
HALF = 480
QD = 960
KVD = 320
UNITS = 640
OWN = 128
KEYS = 1024
SCALING = HEAD_DIM ** (-0.5)
MESH = pl.DeviceIdType.MESH
F32 = jnp.float32
BF16 = jnp.bfloat16
SLOTS = 288
CHUNKS = 15

norm_eps = 1e-05
rope_base = 100000.0


def dot(a, b):
    return jnp.dot(a, b, preferred_element_type=F32)


def dot_nt(a, b):
    return lax.dot_general(a, b, (((1,), (1,)), ((), ())), preferred_element_type=F32)


def dot_tn(a, b):
    return lax.dot_general(a, b, (((0,), (0,)), ((), ())), preferred_element_type=F32)


def heads_of(x, group):
    first = group * SHARE
    return jnp.concatenate(
        [x[:, (first + j) * HEAD_DIM : (first + j + 1) * HEAD_DIM] for j in range(SHARE)], axis=0
    )


def rows_of(index, count):
    return pl.ds(pl.multiple_of(index * count, count), count)


class Place:
    def __init__(self, send_sem, recv_sem):
        col = lax.axis_index("col")
        self.dp, self.row = lax.axis_index("dp"), lax.axis_index("row")
        self.ranks = lax.axis_size("dp")
        self.z, self.x = self.dp // 4, self.dp % 4
        self.low, self.s = col // 2, col % 2
        self.y = self.row * 2 + self.low
        self.up, self.down, self.far = (self.y + 1) % 4, (self.y + 3) % 4, (self.y + 2) % 4
        self.send_sem, self.recv_sem, self.used = send_sem, recv_sem, 0
        self.open = []

    def device(self, y, s):
        return (self.dp, y // 2, (y % 2) * 2 + s)

    def rank(self, z, x):
        return (z * 4 + x, self.row, self.low * 2 + self.s)

    def peer(self, k):
        return ((self.dp + k) % self.ranks, self.row, self.low * 2 + self.s)

    def slots(self, count):
        first = self.used
        self.used += count
        assert self.used <= SLOTS
        return first

    def wire(self, src, dst, other, slot, recv_slot=None):
        return pltpu.make_async_remote_copy(
            src_ref=src,
            dst_ref=dst,
            send_sem=self.send_sem.at[slot],
            recv_sem=self.recv_sem.at[slot if recv_slot is None else recv_slot],
            device_id=other,
            device_id_type=MESH,
        )

    def send(self, src, dst, other):
        copy = self.wire(src, dst, other, self.slots(1))
        copy.start()
        self.open.append(copy)
        return copy

    def others(self):
        others = [self.peer(k) for k in range(1, self.ranks)]
        others += [self.device(self.y, 1 - self.s)]
        for y in (self.up, self.down, self.far):
            others += [self.device(y, self.s), self.device(y, 1 - self.s)]
        return others

    def greet(self):
        barrier = pltpu.get_barrier_semaphore()
        for other in self.others():
            pl.semaphore_signal(barrier, inc=1, device_id=other, device_id_type=MESH)

    def meet(self):
        pl.semaphore_wait(pltpu.get_barrier_semaphore(), len(self.others()))


class Gather:
    def __init__(self, at, buf, rows, split, index=None):
        self.at, self.buf = at, buf
        self.both = index is not None
        if index is None:
            self.mine, self.low, self.high, self.opposite = 0, 1, 2, 3
            self.to_up, self.to_down, self.on_up, self.on_down = 1, 2, 3, 3
        else:
            self.mine, self.low = index(at.y, at.s), index(at.down, at.s)
            self.high, self.opposite = index(at.up, at.s), index(at.far, at.s)
            self.to_up, self.to_down = self.mine, self.mine
            self.on_up, self.on_down = self.low, self.high
        self.first, self.second = pl.ds(0, split), pl.ds(split, rows - split)
        self.up_device, self.down_device = at.device(at.up, at.s), at.device(at.down, at.s)
        self.mate = at.device(at.y, 1 - at.s)
        self.from_mate = []

    def ship(self, index, part, to_index, other):
        return self.at.send(self.buf.at[index, part], self.buf.at[to_index, part], other)

    def to_mate(self, index):
        if self.both:
            self.from_mate.append(self.at.send(self.buf.at[index], self.buf.at[index], self.mate))

    def start(self):
        self.up_first = self.ship(self.mine, self.first, self.to_up, self.up_device)
        self.down_second = self.ship(self.mine, self.second, self.to_down, self.down_device)
        self.up_second = self.ship(self.mine, self.second, self.to_up, self.up_device)
        self.down_first = self.ship(self.mine, self.first, self.to_down, self.down_device)
        self.to_mate(self.mine)

    def relay(self):
        self.up_first.wait_recv()
        self.up_far = self.ship(self.low, self.first, self.on_up, self.up_device)
        self.down_second.wait_recv()
        self.down_far = self.ship(self.high, self.second, self.on_down, self.down_device)

    def near(self):
        self.up_second.wait_recv()
        self.to_mate(self.low)
        self.down_first.wait_recv()
        self.to_mate(self.high)

    def finish(self):
        self.up_far.wait_recv()
        self.down_far.wait_recv()
        self.to_mate(self.opposite)
        for copy in self.from_mate:
            copy.wait_recv()


class Reduce:
    def __init__(self, at, blocks, early, sums, landed):
        self.at, self.blocks = at, blocks
        self.early, self.sums, self.landed = early, sums, landed
        self.up_device, self.down_device = at.device(at.up, at.s), at.device(at.down, at.s)

    def start_far(self):
        at, far = self.at, self.blocks.at[3]
        self.first = at.send(far.at[0], self.early.at[0], self.down_device)
        self.second = at.send(far.at[1], self.early.at[1], self.up_device)

    def start_near(self):
        at = self.at
        self.third = at.send(self.blocks.at[1, 1], self.landed.at[0, 1], self.down_device)
        self.fourth = at.send(self.blocks.at[2, 0], self.landed.at[1, 0], self.up_device)

    def middle(self):
        at, blocks, early, sums = self.at, self.blocks, self.early, self.sums
        self.first.wait_recv()
        sums[0] = (blocks[1, 0].astype(F32) + early[0].astype(F32)).astype(BF16)
        self.fifth = at.send(sums.at[0], self.landed.at[0, 0], self.down_device)
        self.second.wait_recv()
        sums[1] = (blocks[2, 1].astype(F32) + early[1].astype(F32)).astype(BF16)
        self.sixth = at.send(sums.at[1], self.landed.at[1, 1], self.up_device)

    def finish(self):
        for copy in (self.third, self.fourth, self.fifth, self.sixth):
            copy.wait_recv()
        total = (
            self.blocks[0].astype(F32) + self.landed[0].astype(F32) + self.landed[1].astype(F32)
        )
        return total.reshape(total.shape[0] * total.shape[1], total.shape[2])


class Far:
    def __init__(self, at, src, on_up, on_down, relay):
        self.at, self.src, self.on_up, self.on_down, self.buf = at, src, on_up, on_down, relay
        self.up_device, self.down_device = at.device(at.up, at.s), at.device(at.down, at.s)
        self.low, self.high = pl.ds(0, OWN // 2), pl.ds(OWN // 2, OWN // 2)

    def first(self):
        at = self.at
        self.to_up = at.send(self.src.at[self.low], self.buf.at[0], self.up_device)
        self.to_down = at.send(self.src.at[self.high], self.buf.at[1], self.down_device)

    def relay(self):
        at = self.at
        self.to_up.wait_recv()
        self.last_up = at.send(self.buf.at[0], self.on_up.at[self.low], self.up_device)
        self.to_down.wait_recv()
        self.last_down = at.send(self.buf.at[1], self.on_down.at[self.high], self.down_device)

    def finish(self):
        self.last_up.wait_recv()
        self.last_down.wait_recv()


class Spread:
    def __init__(self, at, buf, guard=None):
        self.at, self.buf, self.guard = at, buf, guard
        self.slot = at.slots(18)

    def guarded(self, act):
        if self.guard is None:
            act()
        else:
            pl.when(self.guard)(act)

    def along(self, half, second, step):
        at = self.at
        if (half == 0) != second:
            return at.rank((at.z + step) % 4, at.x)
        return at.rank(at.z, (at.x + step) % 4)

    def first_copy(self, half, n):
        own = self.buf.at[self.at.z, self.at.x, half]
        return self.at.wire(own, own, self.along(half, False, (1, 3, 2)[n]), self.slot + half * 9 + n)

    def block(self, half, part, back):
        at, pair = self.at, pl.ds(2 * part, 2)
        if half == 0:
            return self.buf.at[pair, (at.x + 4 - back) % 4, half]
        return self.buf.at[(at.z + 4 - back) % 4, pair, half]

    def second_copy(self, half, n):
        step, part = ((1, 0), (3, 1), (1, 1), (3, 0))[n]
        src = self.block(half, part, 0)
        return self.at.wire(src, src, self.along(half, True, step), self.slot + half * 9 + 3 + n)

    def third_copy(self, half, n):
        step, part = ((1, 0), (3, 1))[n]
        src = self.block(half, part, step)
        return self.at.wire(src, src, self.along(half, True, step), self.slot + half * 9 + 7 + n)

    def first(self):
        def act():
            for half in range(2):
                for n in range(3):
                    self.first_copy(half, n).start()

        self.guarded(act)

    def second(self):
        def act():
            for half in range(2):
                for n in range(3):
                    self.first_copy(half, n).wait_recv()
                for n in range(4):
                    self.second_copy(half, n).start()

        self.guarded(act)

    def third(self):
        def act():
            for n in range(2):
                for half in range(2):
                    self.second_copy(half, n).wait_recv()
                    self.third_copy(half, n).start()

        self.guarded(act)

    def finish(self):
        def act():
            for half in range(2):
                for n in range(2, 4):
                    self.second_copy(half, n).wait_recv()
                for n in range(2):
                    self.third_copy(half, n).wait_recv()

        self.guarded(act)

    def drain(self):
        def act():
            for half in range(2):
                for n in range(3):
                    self.first_copy(half, n).wait_send()
                for n in range(4):
                    self.second_copy(half, n).wait_send()
                for n in range(2):
                    self.third_copy(half, n).wait_send()

        self.guarded(act)


class Collect:
    def __init__(self, at, kept, early, sums, landed, four, parts, total):
        self.at, self.kept, self.early, self.sums = at, kept, early, sums
        self.landed, self.four, self.parts, self.total = landed, four, parts, total

    def along(self, half, second, step):
        at = self.at
        if (half == 1) != second:
            return at.rank((at.z + step) % 4, at.x)
        return at.rank(at.z, (at.x + step) % 4)

    def block(self, half, step, part):
        at = self.at
        pair = slice(None) if part is None else pl.ds(2 * part, 2)
        if half == 0:
            return (pair, (at.x + step) % 4, half)
        return ((at.z + step) % 4, pair, half)

    def start(self):
        at, kept = self.at, self.kept
        self.far, self.near = {}, []
        for half in range(2):
            for n, step in ((0, 3), (1, 1)):
                self.far[half, n] = at.send(
                    kept.at[self.block(half, 2, n)], self.early.at[half, n], self.along(half, False, step)
                )
        for half in range(2):
            for n, step in ((0, 3), (1, 1)):
                self.near.append(
                    at.send(
                        kept.at[self.block(half, step, 1 - n)],
                        self.landed.at[half, n, pl.ds(2 * (1 - n), 2)],
                        self.along(half, False, step),
                    )
                )

    def middle(self):
        at, kept = self.at, self.kept
        for half in range(2):
            for n, step in ((0, 3), (1, 1)):
                self.far[half, n].wait_recv()
                self.sums[half, n] = (
                    kept[self.block(half, step, n)].astype(F32) + self.early[half, n].astype(F32)
                ).astype(BF16)
                self.near.append(
                    at.send(
                        self.sums.at[half, n],
                        self.landed.at[half, n, pl.ds(2 * n, 2)],
                        self.along(half, False, step),
                    )
                )

    def second(self):
        at = self.at
        for copy in self.near:
            copy.wait_recv()
        self.last = []
        for half in range(2):
            self.four[half] = (
                self.kept[self.block(half, 0, None)].astype(F32)
                + self.landed[half, 0].astype(F32)
                + self.landed[half, 1].astype(F32)
            ).astype(BF16)
            here = at.z if half == 0 else at.x
            for n, step in enumerate((1, 3, 2)):
                self.last.append(
                    at.send(
                        self.four.at[half, (here + step) % 4],
                        self.parts.at[half, n],
                        self.along(half, True, step),
                    )
                )

    def reduce(self):
        at = self.at
        for copy in self.last:
            copy.wait_recv()
        for half in range(2):
            acc = self.four[half, at.z if half == 0 else at.x].astype(F32)
            for n in range(3):
                acc = acc + self.parts[half, n].astype(F32)
            self.total[half] = acc.astype(BF16)


def unit_rows(values):
    inverse = lax.rsqrt(jnp.mean(values * values, axis=-1, keepdims=True) + norm_eps)
    return values * inverse, inverse


def norm_back(gradient, unit, inverse, gain_vec):
    scaled = gradient * gain_vec
    inner_sum = jnp.mean(scaled * unit, axis=1, keepdims=True)
    return (
        inverse * (scaled - unit * inner_sum),
        jnp.sum(gradient * unit, axis=0, keepdims=True),
    )


def turn(x, cosine, sine):
    half = HEAD_DIM // 2
    lane = lax.broadcasted_iota(jnp.int32, x.shape, 1) % HEAD_DIM
    swapped = jnp.where(lane < half, pltpu.roll(x, 128 - half, 1), pltpu.roll(x, half, 1))
    return x * cosine + swapped * sine


def turn_all(x, cosine, sine):
    width = x.shape[1]
    pieces = []
    for first in range(0, width, 128):
        piece = x[:, first : min(first + 128, width)]
        if piece.shape[1] < 128:
            wide = jnp.concatenate([piece, jnp.zeros_like(piece)], axis=1)
            piece = turn(wide, cosine, sine)[:, : piece.shape[1]]
        else:
            piece = turn(piece, cosine, sine)
        pieces.append(piece)
    return jnp.concatenate(pieces, axis=1)


IN_NAMES = ("hidden", "ids_in", "freq", "attn_gain", "ffn_gain")
IN_NAMES += ("q_w", "k_w", "v_w", "o_w", "gate_w", "up_w", "down_w", "d_out")
SCRATCH = dict(
    wq=((8, 240, HALF), BF16),
    wkv=((8, 160, HALF), BF16),
    o_parts=((2, 4, 4, 2, 2, 16, HALF), BF16),
    tokens=((2, OWN, D), BF16),
    own_o=((240, HALF), BF16),
    ids=((8, 16, OWN), BF16),
    normed_one=((2, OWN, HALF), BF16),
    bias=((OWN, KEYS), F32),
    cosine=((OWN, 128), F32),
    sine=((OWN, 128), F32),
    queries=((OWN, QD), BF16),
    kv=((8, OWN, 640), BF16),
    lse=((KV_HEADS, SHARE * OWN, 1), F32),
    attn=((OWN, QD), BF16),
    attn_halves=((2, OWN, HALF), BF16),
    attn_ring=((4, OWN, HALF), BF16),
    first_ring=((4, OWN, HALF), BF16),
    d_out_ring=((4, OWN, D), BF16),
    middle=((OWN, D), F32),
    normed_ring=((4, OWN, D), BF16),
    gate_up=((D, 2 * UNITS), BF16),
    down_parts=((2, 4, 4, 2, 16, UNITS), BF16),
    gate_land=((4, 4, 2, 16, 2 * UNITS), BF16),
    down=((D, UNITS), BF16),
    units=((4, OWN, UNITS), BF16),
    d_gate_up=((4, OWN, 2 * UNITS), BF16),
    ffn_parts=((4, 2, OWN // 2, D), BF16),
    ffn_early=((2, OWN // 2, D), BF16),
    ffn_sums=((2, OWN // 2, D), BF16),
    ffn_landed=((2, 2, OWN // 2, D), BF16),
    dn_parts=((4, 2, OWN // 2, D), BF16),
    dn_early=((2, OWN // 2, D), BF16),
    dn_sums=((2, OWN // 2, D), BF16),
    dn_landed=((2, 2, OWN // 2, D), BF16),
    ffn_halves=((2, 512, 1920), BF16),
    ffn_mate=((512, 1920), BF16),
    ffn_kept=((4, 4, 2, 16, 1920), BF16),
    ffn_far=((2, 2, 2, 16, 1920), BF16),
    ffn_pairs=((2, 2, 2, 16, 1920), BF16),
    ffn_near=((2, 2, 4, 16, 1920), BF16),
    ffn_four=((2, 4, 16, 1920), BF16),
    ffn_last=((2, 3, 16, 1920), BF16),
    ffn_sum=((2, 16, 1920), BF16),
    d_middle=((OWN, D), F32),
    d_y1_halves=((2, OWN, HALF), BF16),
    d_y1_ring=((4, OWN, HALF), BF16),
    d_kv=((8, OWN, 640), BF16),
    kv_mate=((4, OWN, 640), BF16),
    kv_parts=((4, 2, OWN // 2, 640), BF16),
    kv_early=((2, OWN // 2, 640), BF16),
    kv_sums=((2, OWN // 2, 640), BF16),
    kv_landed=((2, 2, OWN // 2, 640), BF16),
    d_q=((2, OWN, HALF), BF16),
    d_q_ring=((4, OWN, HALF), BF16),
    d_kv_own=((2, OWN, 320), BF16),
    d_kv_ring=((4, OWN, 320), BF16),
    gains=((4, 8, D), F32),
    qo_two=((2, 512, HALF), BF16),
    qo_mate=((512, HALF), BF16),
    kv_two=((2, 512, 160), BF16),
    kv_grad_mate=((512, 160), BF16),
    attn_kept=((4, 4, 2, 16, 640), BF16),
    attn_far=((2, 2, 2, 16, 640), BF16),
    attn_pairs=((2, 2, 2, 16, 640), BF16),
    attn_near=((2, 2, 4, 16, 640), BF16),
    attn_four=((2, 4, 16, 640), BF16),
    attn_last=((2, 3, 16, 640), BF16),
    attn_sum=((2, 16, 640), BF16),
    attn_relay=((2, OWN // 2, HALF), BF16),
    d_y1_relay=((2, OWN // 2, HALF), BF16),
    d_q_relay=((2, OWN // 2, HALF), BF16),
    d_kv_relay=((2, OWN // 2, 320), BF16),
    block_relay=((2, OWN // 2, D), BF16),
    input_relay=((2, OWN // 2, D), BF16),
    block_out=((2, OWN, D), BF16),
    input_grad=((2, OWN, D), BF16),
    attn_total=((4, 4, 2, 16, 640), BF16),
    ffn_total=((4, 4, 2, 16, 1920), BF16),
    out_sem=pltpu.SemaphoreType.DMA((4,)),
    send_sem=pltpu.SemaphoreType.DMA((SLOTS,)),
    recv_sem=pltpu.SemaphoreType.DMA((SLOTS,)),
)


def block_of(y, s):
    return ((y % 2) * 2 + s) * 2 + y // 2


def layer_kernel(*refs):
    count = len(IN_NAMES)
    outs, refs = refs[count : count + 4], refs[:count] + refs[count + 4 :]
    m = types.SimpleNamespace(**dict(zip(IN_NAMES + tuple(SCRATCH), refs)))
    leaving = []

    def leave(n, src):
        copy = pltpu.make_async_copy(src, outs[n], m.out_sem.at[n])
        copy.start()
        leaving.append(copy)

    at = Place(m.send_sem, m.recv_sem)
    row, low, s, y, dp = at.row, at.low, at.s, at.y, at.dp
    mate = at.device(y, 1 - s)
    up_device, down_device = at.device(at.up, s), at.device(at.down, s)
    far_device, cross = at.device(at.far, s), at.device(at.far, 1 - s)
    mine = block_of(y, s)
    active = dp < CHUNKS
    not_ = jnp.logical_not

    at.greet()

    wq, wkv, ids = m.wq, m.wkv, m.ids
    wq[mine] = m.q_w[...].T
    wkv[mine, 0:80] = m.k_w[...]
    wkv[mine, 80:160] = m.v_w[...]
    own_row = jnp.where(row == 0, m.ids_in[:, 0:OWN], m.ids_in[:, OWN:]).astype(F32)
    ids[mine] = jnp.broadcast_to(own_row, (16, OWN)).astype(BF16)
    m.own_o[...] = m.o_w[...].T
    at.meet()

    gate_up, o_parts, down_parts = m.gate_up, m.o_parts, m.down_parts
    o_slot, down_slot, gate_slot = at.slots(3), at.slots(2), at.slots(4)
    gate_mate_slot = at.slots(1)
    own_core = s == row
    strip = rows_of(dp, 16)

    def o_copy(n):
        other = (up_device, down_device, far_device)[n]
        return at.wire(m.own_o.at[strip], o_parts.at[s, at.z, at.x, row, low], other, o_slot + n)

    def down_copy(r):
        target = r * 2 + row
        return target, at.wire(
            m.down_w.at[strip, pl.ds(r * UNITS, UNITS)],
            down_parts.at[s, at.z, at.x, low],
            at.device(target, s),
            down_slot + r,
            down_slot + low,
        )

    def down_arrive(a):
        return low * 2 + a, at.wire(
            m.down_w.at[strip, pl.ds(0, UNITS)],
            down_parts.at[s, at.z, at.x, a],
            up_device,
            down_slot + a,
        )

    gate_land = m.gate_land

    def gate_copy(n, part):
        source = (m.gate_w, m.up_w)[n]
        return at.wire(
            source.at[pl.ds(pl.multiple_of(dp * 32 + 16 * part, 16), 16)],
            gate_land.at[at.z, at.x, part, :, pl.ds(UNITS * n, UNITS)],
            cross,
            gate_slot + 2 * n + part,
        )

    gate_copies = [(n, part) for n in range(2) for part in range(2)]
    o_spread = Spread(at, o_parts.at[s])
    down_spread = Spread(at, down_parts.at[s])
    gate_spread = Spread(at, gate_land, not_(own_core))
    spreads = (o_spread, gate_spread, down_spread)

    def gate_mate(half):
        rows = pl.ds(pl.multiple_of(half * HALF, 32), HALF)
        return at.wire(gate_up.at[rows], gate_up.at[rows], mate, gate_mate_slot)

    gather_kw = Gather(at, wkv, 160, 80, block_of)
    gather_qw = Gather(at, wq, 240, 112, block_of)
    gather_kw.start()
    ids_copies = [at.send(ids.at[mine], ids.at[mine], mate)]
    for other in (at.up, at.down, at.far):
        for core in (s, 1 - s):
            ids_copies.append(at.send(ids.at[mine], ids.at[mine], at.device(other, core)))

    @pl.when(active)
    def _():
        o_parts[s, at.z, at.x, row, low] = m.own_o[strip]
        for n in range(3):
            o_copy(n).start()
        for r in range(2):
            target, copy = down_copy(r)

            @pl.when(target == y)
            def _():
                down_parts[s, at.z, at.x, low] = m.down_w[strip, r * UNITS : (r + 1) * UNITS]

            @pl.when(target != y)
            def _():
                copy.start()

        @pl.when(not_(own_core))
        def _():
            for n, part in gate_copies:
                gate_copy(n, part).start()

    @pl.when(not_(active))
    def _():
        o_parts[s, at.z, at.x] = jnp.zeros((2, 2, 16, HALF), BF16)
        down_parts[s, at.z, at.x] = jnp.zeros((2, 16, UNITS), BF16)
        gate_land[at.z, at.x] = jnp.zeros((2, 16, 2 * UNITS), BF16)

    @pl.when(own_core)
    def _():
        rows = pl.ds(pl.multiple_of(row * HALF, 32), HALF)
        gate_up[rows, 0:UNITS] = m.gate_w[...]
        gate_up[rows, UNITS:] = m.up_w[...]
        gate_mate(row).start()

    tokens_two, d_out_ring = m.tokens, m.d_out_ring
    hidden, d_out = m.hidden[...].T, m.d_out[...].T
    tokens_two[0], tokens_two[1] = hidden[:OWN], hidden[OWN:]
    first_half = row == 0
    d_out_ring[0] = jnp.where(first_half, d_out[:OWN], d_out[OWN:])
    d_out_ring[3] = jnp.where(first_half, d_out[OWN:], d_out[:OWN])
    gather_kw.relay()
    gather_qw.start()
    attn_gain, ffn_gain = m.attn_gain[...], m.ffn_gain[...]
    unit_one, _ = unit_rows(tokens_two[row].astype(F32))
    normed = (unit_one * attn_gain).astype(BF16)
    m.normed_one[0] = normed[:, :HALF]
    m.normed_one[1] = normed[:, HALF:]
    first_ring = m.first_ring
    first_ring[0] = m.normed_one[row]
    unit_far, _ = unit_rows(tokens_two[1 - row].astype(F32))
    normed_far = (unit_far * attn_gain).astype(BF16)
    first_ring[3] = jnp.where(first_half, normed_far[:, :HALF], normed_far[:, HALF:])

    gather_kw.near()

    for copy in ids_copies:
        copy.wait_recv()
    own_ids = jnp.broadcast_to(own_row, (OWN, OWN)).T[:, 0:1].astype(jnp.int32)
    docs = jnp.concatenate([ids[b, 0:1, :] for b in range(8)], axis=1).astype(F32).astype(jnp.int32)
    earlier = jnp.sum((docs < own_ids).astype(F32), axis=1, keepdims=True)
    start = (low * 2 + s) * 256 + row * OWN
    position = start + lax.broadcasted_iota(jnp.int32, (OWN, 1), 0)
    angles = (position.astype(F32) - earlier) * m.freq[...]
    lane = lax.broadcasted_iota(jnp.int32, (OWN, 128), 1) % HEAD_DIM
    sine = jnp.sin(angles)
    m.cosine[...] = jnp.cos(angles)
    m.sine[...] = jnp.where(lane < HEAD_DIM // 2, -sine, sine)
    key_at = lax.broadcasted_iota(jnp.int32, (OWN, KEYS), 1)
    allowed = (own_ids == docs) & (key_at <= position)
    m.bias[...] = jnp.where(allowed, 0.0, -jnp.inf).astype(F32)

    @pl.when(active)
    def _():
        for n in range(3):
            o_copy(n).wait_recv()
        for a in range(2):
            source, copy = down_arrive(a)

            @pl.when(source != y)
            def _():
                copy.wait_recv()

        @pl.when(not_(own_core))
        def _():
            for n, part in gate_copies:
                gate_copy(n, part).wait_recv()

    for spread in spreads:
        spread.first()

    gather_kw.finish()

    def project(buf, c):
        part = dot_nt(m.normed_one[0], buf[2 * c]) + dot_nt(m.normed_one[1], buf[2 * c + 1])
        return part.astype(BF16).astype(F32)

    parts = [project(wkv, c) for c in range(4)]
    cosine, sine = m.cosine[...], m.sine[...]
    k = jnp.concatenate([part[:, 0:80] for part in parts], axis=1)
    v = jnp.concatenate([part[:, 80:160] for part in parts], axis=1)
    kv = m.kv
    kv[mine] = jnp.concatenate([turn_all(k, cosine, sine), v], axis=1).astype(BF16)
    gather_kv = Gather(at, kv, OWN, OWN // 2, block_of)
    gather_kv.start()
    gather_qw.relay()
    for spread in spreads:
        spread.second()
    gather_qw.near()
    gather_kv.relay()
    gather_qw.finish()
    q = jnp.concatenate([project(wq, c) for c in range(4)], axis=1)
    m.queries[...] = turn_all(q, cosine, sine).astype(BF16)
    for spread in spreads:
        spread.third()
    gather_kv.near()
    gather_kv.finish()
    d_out_copies = [
        at.send(d_out_ring.at[0], d_out_ring.at[1], up_device),
        at.send(d_out_ring.at[0], d_out_ring.at[2], down_device),
    ]

    o_spread.finish()
    o_mate = at.send(o_parts.at[s], o_parts.at[s], mate)

    for g in range(KV_HEADS):
        key = kv[:, :, g * HEAD_DIM : (g + 1) * HEAD_DIM].reshape(KEYS, HEAD_DIM)
        value = kv[:, :, KVD + g * HEAD_DIM : KVD + (g + 1) * HEAD_DIM].reshape(KEYS, HEAD_DIM)
        scores = dot_nt(heads_of(m.queries, g), key) * SCALING
        scores = scores.reshape(SHARE, OWN, KEYS) + m.bias[...][None]
        top = jnp.max(scores, axis=-1, keepdims=True)
        terms = jnp.exp(scores - top)
        total = jnp.sum(terms, axis=-1, keepdims=True)
        probs = (terms / total).astype(BF16).reshape(SHARE * OWN, KEYS)
        out = dot(probs, value).astype(BF16)
        for j in range(SHARE):
            head = (g * SHARE + j) * HEAD_DIM
            m.attn[:, head : head + HEAD_DIM] = out[j * OWN : (j + 1) * OWN]
        m.lse[g] = (top + jnp.log(total)).reshape(SHARE * OWN, 1)
    attn_halves = m.attn_halves
    attn_halves[0] = m.attn[:, :HALF]
    attn_halves[1] = m.attn[:, HALF:]
    o_mate.wait_recv()

    def o_block(r, c):
        return o_parts[c % 2, :, :, r, c // 2].reshape(256, HALF)[0:240]

    attn_out = [
        dot_nt(attn_halves[0], o_block(0, c)) + dot_nt(attn_halves[1], o_block(1, c)) for c in range(4)
    ]
    middle = tokens_two[row].astype(F32) + jnp.concatenate(attn_out, axis=1)
    m.middle[...] = middle
    unit_two, _ = unit_rows(middle)
    ring = m.normed_ring
    ring[0] = (unit_two * ffn_gain).astype(BF16)
    gather_n = Gather(at, ring, OWN, OWN // 2)
    gather_n.start()

    gate_spread.finish()

    @pl.when(not_(own_core))
    def _():
        rows = pl.ds(pl.multiple_of((1 - row) * HALF, 32), HALF)
        gate_up[rows] = gate_land[...].reshape(512, 2 * UNITS)[0:HALF]
        gate_mate(1 - row).start()

    down_spread.finish()
    down_mate = at.send(down_parts.at[s], down_parts.at[s], mate)
    gather_n.relay()
    down_mate.wait_recv()
    for c in range(4):
        m.down[c * 240 : (c + 1) * 240] = down_parts[c % 2, :, :, c // 2].reshape(256, UNITS)[0:240]
    for copy in d_out_copies:
        copy.wait_recv()
    gate_mate(row).wait_recv()

    ffn_parts, dn_parts = m.ffn_parts, m.dn_parts

    def feed(p):
        gate_and_up = dot(ring[p], gate_up[...]).astype(BF16)
        gate, raise_ = gate_and_up[:, :UNITS].astype(F32), gate_and_up[:, UNITS:].astype(F32)
        sig = 1.0 / (1.0 + jnp.exp(-gate))
        silu = gate * sig
        unit = (silu * raise_).astype(BF16)
        m.units[p] = unit
        d_unit = dot(d_out_ring[p], m.down[...])
        d_gate = (d_unit * raise_ * sig * (1.0 + gate * (1.0 - sig))).astype(BF16)
        d_up = (d_unit * silu).astype(BF16)
        m.d_gate_up[p] = jnp.concatenate([d_gate, d_up], axis=1)
        d_normed = dot_nt(m.d_gate_up[p], gate_up[...]).astype(BF16)
        dn_parts[p] = d_normed.reshape(2, OWN // 2, D)

    def feed_out(p):
        ffn_parts[p] = dot_nt(m.units[p], m.down[...]).astype(BF16).reshape(2, OWN // 2, D)

    dn = Reduce(at, dn_parts, m.dn_early, m.dn_sums, m.dn_landed)
    ffn = Reduce(at, ffn_parts, m.ffn_early, m.ffn_sums, m.ffn_landed)
    feed(0)
    gather_n.near()
    feed(1)
    feed(2)
    dn.start_near()
    gather_n.finish()
    feed(3)
    dn.start_far()
    for p in (3, 1, 2):
        feed_out(p)
    dn.middle()
    feed_out(0)

    halves = m.ffn_halves
    tokens_n = ring[...].reshape(4 * OWN, D)
    d_gate_up = m.d_gate_up[...].reshape(4 * OWN, 2 * UNITS)
    tokens_d = d_out_ring[...].reshape(4 * OWN, D)
    units = m.units[...].reshape(4 * OWN, UNITS)
    for h in range(2):
        halves[h, 0:HALF, 0 : 2 * UNITS] = dot_tn(tokens_n[:, h * HALF : (h + 1) * HALF], d_gate_up).astype(BF16)
        grad = dot_tn(tokens_d[:, h * HALF : (h + 1) * HALF], units).astype(BF16)
        for i in range(CHUNKS):
            halves[h, 32 * i : 32 * i + 16, 2 * UNITS :] = grad[16 * i : 16 * i + 16]
            halves[h, 32 * i + 16 : 32 * i + 32, 2 * UNITS :] = grad[240 + 16 * i : 256 + 16 * i]
        halves[h, HALF:, :] = jnp.zeros((32, 1920), BF16)
    ffn_pair = at.send(halves.at[1 - s], m.ffn_mate, mate)
    ffn_collect = Collect(
        at,
        m.ffn_kept,
        m.ffn_far,
        m.ffn_pairs,
        m.ffn_near,
        m.ffn_four,
        m.ffn_last,
        m.ffn_sum,
    )

    d_normed = dn.finish()
    middle = m.middle[...]
    unit_two, inverse_two = unit_rows(middle)
    d_middle, ffn_gain_part = norm_back(d_normed, unit_two, inverse_two, ffn_gain)
    d_middle = d_middle + d_out_ring[0].astype(F32)
    m.d_middle[...] = d_middle
    d_y1 = d_middle.astype(BF16)
    d_y1_halves, d_y1_ring = m.d_y1_halves, m.d_y1_ring
    d_y1_halves[0] = d_y1[:, :HALF]
    d_y1_halves[1] = d_y1[:, HALF:]
    d_attn = [0.0, 0.0]
    for c in range(4):
        for r in range(2):
            d_attn[r] = d_attn[r] + dot(d_y1[:, c * 240 : (c + 1) * 240], o_block(r, c))
    d_attn = jnp.concatenate(d_attn, axis=1).astype(BF16)

    up_low, up_row, down_row = 1 - low, at.up // 2, at.down // 2
    attn_ring, first_send = m.attn_ring, m.normed_one
    attn_far = Far(at, attn_halves.at[1 - row], attn_ring.at[3], attn_ring.at[3], m.attn_relay)
    d_y1_far = Far(at, d_y1_halves.at[low], d_y1_ring.at[3], d_y1_ring.at[3], m.d_y1_relay)
    attn_far.first()
    d_y1_far.first()
    side_copies = [
        at.send(d_y1_halves.at[up_low], d_y1_ring.at[1], up_device),
        at.send(d_y1_halves.at[up_low], d_y1_ring.at[2], down_device),
        at.send(attn_halves.at[up_row], attn_ring.at[1], up_device),
        at.send(attn_halves.at[down_row], attn_ring.at[2], down_device),
        at.send(first_send.at[up_row], first_ring.at[1], up_device),
        at.send(first_send.at[down_row], first_ring.at[2], down_device),
    ]
    attn_ring[0] = attn_halves[row]
    d_y1_ring[0] = d_y1_halves[low]

    d_kv = m.d_kv
    d_q = []
    for g in range(KV_HEADS):
        own = slice(g * HEAD_DIM, (g + 1) * HEAD_DIM)
        val = slice(KVD + g * HEAD_DIM, KVD + (g + 1) * HEAD_DIM)
        key = kv[:, :, own].reshape(KEYS, HEAD_DIM)
        value = kv[:, :, val].reshape(KEYS, HEAD_DIM)
        query, d_head = heads_of(m.queries, g), heads_of(d_attn, g)
        scores = dot_nt(query, key) * SCALING
        scores = scores.reshape(SHARE, OWN, KEYS) + m.bias[...][None]
        probs = jnp.exp(scores.reshape(SHARE * OWN, KEYS) - m.lse[g])
        d_probs = dot_nt(d_head, value)
        inner = jnp.sum(probs * d_probs, axis=-1, keepdims=True)
        d_scores = (probs * (d_probs - inner)).astype(BF16)
        d_query = dot(d_scores, key) * SCALING
        d_q += [d_query[j * OWN : (j + 1) * OWN] for j in range(SHARE)]
        d_kv[:, :, own] = (dot_tn(d_scores, query) * SCALING).astype(BF16).reshape(8, OWN, HEAD_DIM)
        d_kv[:, :, val] = dot_tn(probs.astype(BF16), d_head).astype(BF16).reshape(8, OWN, HEAD_DIM)
        if g == 0:
            ffn_pair.wait_recv()
            for z in range(4):
                for x in range(4):
                    rows = pl.ds(32 * (4 * z + x), 32)
                    both = halves[s, rows].astype(F32) + m.ffn_mate[rows].astype(F32)
                    m.ffn_kept[z, x] = both.astype(BF16).reshape(2, 16, 1920)
            ffn_collect.start()
        if g == 1:
            attn_far.relay()
            d_y1_far.relay()
        if g == 3:
            ffn_collect.middle()

    ffn_collect.second()
    kv_copies = []
    order = ((3, at.far), (1, at.down), (2, at.up), (0, y))
    for p, t in order:
        kv_copies.append(at.send(d_kv.at[block_of(t, 1 - s)], m.kv_mate.at[p], mate))
    cosine, sine = m.cosine[...], -m.sine[...]
    d_q = turn_all(jnp.concatenate(d_q, axis=1), cosine, sine).astype(BF16)
    kv_sum = Reduce(at, m.kv_parts, m.kv_early, m.kv_sums, m.kv_landed)
    for (p, t), copy in zip(order, kv_copies):
        copy.wait_recv()
        both = d_kv[block_of(t, s)].astype(F32) + m.kv_mate[p].astype(F32)
        m.kv_parts[p] = both.astype(BF16).reshape(2, OWN // 2, 640)
        if p == 3:
            kv_sum.start_far()
        if p == 2:
            kv_sum.start_near()
    d_q_two, d_q_ring = m.d_q, m.d_q_ring
    d_q_two[0], d_q_two[1] = d_q[:, :HALF], d_q[:, HALF:]
    kv_sum.middle()
    q_copies = [
        at.send(d_q_two.at[up_low], d_q_ring.at[1], up_device),
        at.send(d_q_two.at[up_low], d_q_ring.at[2], down_device),
    ]
    d_q_far = Far(at, d_q_two.at[low], d_q_ring.at[3], d_q_ring.at[3], m.d_q_relay)
    d_q_far.first()
    d_q_ring[0] = d_q_two[low]
    d_normed_one = [0.0, 0.0]
    for c in range(4):
        for r in range(2):
            d_normed_one[r] = d_normed_one[r] + dot(d_q[:, c * 240 : (c + 1) * 240], wq[2 * c + r])

    ffn_collect.reduce()
    sums, ffn_total = m.ffn_sum, m.ffn_total
    gate_back_slot, back_slot = at.slots(1), at.slots(2)
    lanes = pl.ds(2 * UNITS, UNITS)
    owner = low * 2 + s

    def gate_back():
        both = pl.ds(0, 2 * UNITS)
        return at.wire(
            sums.at[:, :, both], ffn_total.at[at.z, at.x, :, :, both], cross, gate_back_slot
        )

    def down_back(j):
        return at.wire(
            sums.at[j, :, lanes],
            ffn_total.at[at.z, at.x, row, :, lanes],
            at.device(owner, j),
            back_slot + j,
            back_slot + row,
        )

    @pl.when(own_core)
    def _():
        ffn_total[at.z, at.x, :, :, 0 : 2 * UNITS] = sums[:, :, 0 : 2 * UNITS]

    @pl.when(not_(own_core))
    def _():
        gate_back().start()

    for j in range(2):
        here = (owner == y) & (s == j)
        copy = down_back(j)

        @pl.when(here)
        def _():
            ffn_total[at.z, at.x, row, :, 2 * UNITS :] = sums[j, :, 2 * UNITS :]

        @pl.when(not_(here))
        def _():
            copy.start()

    d_kv_sum = kv_sum.finish()
    d_k = turn_all(d_kv_sum[:, :KVD], cosine, sine).astype(BF16)
    d_v = d_kv_sum[:, KVD:].astype(BF16)
    d_kv_own, d_kv_ring = m.d_kv_own, m.d_kv_ring
    for a in range(2):
        d_kv_own[a] = jnp.concatenate(
            [d_k[:, a * 160 : (a + 1) * 160], d_v[:, a * 160 : (a + 1) * 160]], axis=1
        )
    d_kv_far = Far(at, d_kv_own.at[low], d_kv_ring.at[3], d_kv_ring.at[3], m.d_kv_relay)
    d_kv_far.first()
    kv_out = [
        at.send(d_kv_own.at[up_low], d_kv_ring.at[1], up_device),
        at.send(d_kv_own.at[up_low], d_kv_ring.at[2], down_device),
    ]
    d_kv_ring[0] = d_kv_own[low]
    d_q_far.relay()

    for c in range(4):
        piece = jnp.concatenate(
            [d_k[:, c * 80 : (c + 1) * 80], d_v[:, c * 80 : (c + 1) * 80]], axis=1
        )
        for r in range(2):
            d_normed_one[r] = d_normed_one[r] + dot(piece, wkv[2 * c + r])
    unit_one, inverse_one = unit_rows(tokens_two[row].astype(F32))
    d_tokens, attn_gain_part = norm_back(
        jnp.concatenate(d_normed_one, axis=1), unit_one, inverse_one, attn_gain
    )
    gains = m.gains
    gains[0] = jnp.concatenate([attn_gain_part, ffn_gain_part, jnp.zeros((6, D), F32)], axis=0)
    gain_copies = [
        at.send(gains.at[0], gains.at[1], up_device),
        at.send(gains.at[0], gains.at[2], down_device),
        at.send(gains.at[0], gains.at[3], far_device),
    ]
    input_grad = m.input_grad
    input_grad[row] = (d_tokens + m.d_middle[...]).astype(BF16)
    input_far = Far(
        at, input_grad.at[row], input_grad.at[1 - up_row], input_grad.at[1 - down_row], m.input_relay
    )
    d_kv_far.relay()
    ffn.start_far()
    ffn.start_near()

    @pl.when(not_(own_core))
    def _():
        gate_back().wait_recv()

    for r in range(2):
        source = r * 2 + row

        @pl.when(not_((source == y) & (low == s)))
        def _():
            at.wire(
                sums.at[0, :, lanes],
                ffn_total.at[at.z, at.x, r, :, lanes],
                mate,
                back_slot + r,
            ).wait_recv()

    ffn_spread = Spread(at, ffn_total)
    ffn_spread.first()

    for copy in side_copies + q_copies:
        copy.wait_recv()
    for far in (attn_far, d_y1_far, d_q_far):
        far.finish()
    first_all = first_ring[...].reshape(4 * OWN, HALF)
    q_grad = dot_tn(first_all, d_q_ring[...].reshape(4 * OWN, HALF)).astype(BF16)
    o_grad = dot_tn(
        attn_ring[...].reshape(4 * OWN, HALF), d_y1_ring[...].reshape(4 * OWN, HALF)
    ).astype(BF16)
    qo_two, kv_two = m.qo_two, m.kv_two
    for b in range(2):
        pick = slice(b * 240, (b + 1) * 240)
        qo_two[b, 0:HALF, :] = jnp.concatenate([q_grad[:, pick], o_grad[:, pick]], axis=1)
        qo_two[b, HALF:, :] = jnp.zeros((32, HALF), BF16)
    qo_pair = at.send(qo_two.at[1 - s], m.qo_mate, mate)
    ffn.middle()

    for copy in kv_out + gain_copies:
        copy.wait_recv()
    d_kv_far.finish()
    kv_grad = dot_tn(first_all, d_kv_ring[...].reshape(4 * OWN, 320)).astype(BF16)
    gain_sum = (gains[0] + gains[1] + gains[2] + gains[3])[0:2].astype(BF16)
    gain_rows = [gain_sum[g : g + 1, p * 160 : (p + 1) * 160] for g in range(2) for p in range(6)]
    gain_block = jnp.concatenate(gain_rows + [jnp.zeros((20, 160), BF16)], axis=0)
    for b in range(2):
        kv_two[b, 0:HALF, :] = jnp.concatenate(
            [kv_grad[:, b * 80 : (b + 1) * 80], kv_grad[:, 160 + b * 80 : 160 + (b + 1) * 80]], axis=1
        )
        kv_two[b, HALF:, :] = gain_block
    kv_pair = at.send(kv_two.at[1 - s], m.kv_grad_mate, mate)
    ffn_spread.second()
    attn_kept = m.attn_kept
    for pair, two, theirs, first in (
        (qo_pair, qo_two, m.qo_mate, 0),
        (kv_pair, kv_two, m.kv_grad_mate, HALF),
    ):
        pair.wait_recv()
        both = (two[s].astype(F32) + theirs[...].astype(F32)).astype(BF16)
        width = both.shape[1]
        attn_kept[:, :, :, :, first : first + width] = both.reshape(4, 4, 2, 16, width)

    attn_collect = Collect(
        at,
        attn_kept,
        m.attn_far,
        m.attn_pairs,
        m.attn_near,
        m.attn_four,
        m.attn_last,
        m.attn_sum,
    )
    attn_collect.start()
    input_far.first()
    ffn_spread.third()
    attn_collect.middle()
    block_out = m.block_out
    block_out[row] = (m.middle[...] + ffn.finish()).astype(BF16)
    block_far = Far(
        at, block_out.at[row], block_out.at[1 - up_row], block_out.at[1 - down_row], m.block_relay
    )
    block_far.first()
    input_far.relay()
    attn_collect.second()
    block_far.relay()
    attn_collect.reduce()
    attn_total = m.attn_total
    attn_total[at.z, at.x] = m.attn_sum[...]
    attn_spread = Spread(at, attn_total)
    attn_spread.first()
    ffn_spread.finish()
    leave(3, ffn_total)
    attn_spread.second()
    input_far.finish()
    leave(1, input_grad)
    block_far.finish()
    leave(0, block_out)
    attn_spread.third()
    attn_spread.finish()
    leave(2, attn_total)
    for copy in leaving:
        copy.wait()

    for copy in at.open:
        copy.wait_send()
    gate_mate(row).wait_send()
    for spread in spreads + (ffn_spread, attn_spread):
        spread.drain()

    @pl.when(active)
    def _():
        for n in range(3):
            o_copy(n).wait_send()
        for r in range(2):
            target, copy = down_copy(r)

            @pl.when(target != y)
            def _():
                copy.wait_send()

        @pl.when(not_(own_core))
        def _():
            for n, part in gate_copies:
                gate_copy(n, part).wait_send()

    @pl.when(not_(own_core))
    def _():
        gate_back().wait_send()

    for j in range(2):
        copy = down_back(j)

        @pl.when(not_((owner == y) & (s == j)))
        def _():
            copy.wait_send()


RESULTS = (
    (D, 2 * OWN), (D, 2 * OWN), (1, D), (HALF, 240), (80, HALF), (80, HALF),
    (HALF, 240), (1, D), (HALF, UNITS), (HALF, UNITS), (240, 2 * UNITS),
)


def results_kernel(*refs):
    ins, outs, held, made = refs[:4], refs[4:15], refs[15:19], refs[19:30]
    in_sem, out_sem = refs[30:]
    copies = [
        pltpu.make_async_copy(ins[n], held[n], in_sem.at[n]) for n in range(4)
    ]
    for n in (3, 0, 1, 2):
        copies[n].start()
    block_in, input_in, attn_in, ffn_in = held
    leaving = []

    def leave(n):
        copy = pltpu.make_async_copy(made[n], outs[n], out_sem.at[n])
        copy.start()
        leaving.append(copy)

    copies[3].wait()
    for n in range(2):
        made[8 + n][...] = (
            ffn_in[0:CHUNKS, :, :, n * UNITS : (n + 1) * UNITS].reshape(HALF, UNITS).astype(F32)
        )
        leave(8 + n)
    for i in range(CHUNKS):
        for r in range(2):
            made[10][16 * i : 16 * i + 16, r * UNITS : (r + 1) * UNITS] = ffn_in[
                i, r, :, 2 * UNITS :
            ].astype(F32)
    leave(10)
    for n in range(2):
        copies[n].wait()
        made[n][...] = held[n][...].reshape(2 * OWN, D).astype(F32).T
        leave(n)
    copies[2].wait()
    made[3][...] = attn_in[0:CHUNKS, :, :, 0:240].reshape(HALF, 240).astype(F32)
    leave(3)
    made[6][...] = attn_in[0:CHUNKS, :, :, 240:480].reshape(HALF, 240).astype(F32)
    leave(6)
    kv_grad = attn_in[0:CHUNKS, :, :, 480:640].reshape(HALF, 160).astype(F32).T
    made[4][...] = kv_grad[0:80]
    made[5][...] = kv_grad[80:160]
    leave(4)
    leave(5)
    gains = attn_in[CHUNKS, 0, :, 480:640].astype(F32)
    for p in range(6):
        made[2][:, p * 160 : (p + 1) * 160] = gains[p : p + 1]
        made[7][:, p * 160 : (p + 1) * 160] = gains[6 + p : 7 + p]
    leave(2)
    leave(7)
    for copy in leaving:
        copy.wait()


def shards(
    hidden_in,
    segment_ids,
    attn_gain,
    q_weight,
    k_weight,
    v_weight,
    o_weight,
    ffn_gain,
    gate_weight,
    up_weight,
    down_weight,
    d_out,
):
    frequency = np.float32(rope_base) ** (-np.arange(HEAD_DIM // 2, dtype=np.float32) * 2 / HEAD_DIM)
    freq = jnp.asarray(np.tile(frequency.astype(np.float32), 4)[None, :])
    scratch = [
        pltpu.VMEM(*kind) if isinstance(kind, tuple) else kind for kind in SCRATCH.values()
    ]
    local = pl.BlockSpec(memory_space=pltpu.VMEM)
    kept = pl.pallas_call(
        layer_kernel,
        out_shape=[
            jax.ShapeDtypeStruct((2, OWN, D), BF16),
            jax.ShapeDtypeStruct((2, OWN, D), BF16),
            jax.ShapeDtypeStruct((4, 4, 2, 16, 640), BF16),
            jax.ShapeDtypeStruct((4, 4, 2, 16, 1920), BF16),
        ],
        in_specs=[local] * len(IN_NAMES),
        out_specs=[pl.BlockSpec(memory_space=pl.ANY)] * 4,
        scratch_shapes=scratch,
        compiler_params=pltpu.CompilerParams(
            collective_id=1, has_side_effects=True, vmem_limit_bytes=60 * 1024 * 1024
        ),
    )(
        hidden_in.T,
        segment_ids[None, :],
        freq,
        attn_gain[None, :],
        ffn_gain[None, :],
        q_weight,
        k_weight.T,
        v_weight.T,
        o_weight,
        gate_weight,
        up_weight,
        down_weight.T,
        d_out.T,
    )
    outs = pl.pallas_call(
        results_kernel,
        out_shape=[jax.ShapeDtypeStruct(shape, F32) for shape in RESULTS],
        in_specs=[pl.BlockSpec(memory_space=pl.ANY)] * 4,
        out_specs=[pl.BlockSpec(memory_space=pl.ANY)] * len(RESULTS),
        scratch_shapes=[
            pltpu.VMEM((2, OWN, D), BF16),
            pltpu.VMEM((2, OWN, D), BF16),
            pltpu.VMEM((16, 2, 16, 640), BF16),
            pltpu.VMEM((16, 2, 16, 1920), BF16),
        ]
        + [pltpu.VMEM(shape, F32) for shape in RESULTS]
        + [pltpu.SemaphoreType.DMA((4,)), pltpu.SemaphoreType.DMA((len(RESULTS),))],
        compiler_params=pltpu.CompilerParams(vmem_limit_bytes=62 * 1024 * 1024),
    )(kept[0], kept[1], kept[2].reshape(16, 2, 16, 640), kept[3].reshape(16, 2, 16, 1920))
    turned = (0, 1, 4, 5, 10)
    outs = [out.T if i in turned else out for i, out in enumerate(outs)]
    outs[2], outs[7] = outs[2].reshape(D), outs[7].reshape(D)
    return tuple(outs)


def solution(mesh):
    rows, blocks = P(("dp", "col"), None), P("row", "col")
    return jax.shard_map(
        shards,
        mesh=mesh,
        in_specs=(
            rows, P(("dp", "col")), P(), blocks, blocks, blocks, blocks, P(), blocks, blocks, blocks, rows,
        ),
        out_specs=(rows, rows, P(), blocks, blocks, blocks, blocks, P(), blocks, blocks, blocks),
        check_vma=False,
    )
```

```python
import types

import jax
import jax.numpy as jnp
import numpy as np
from jax import lax
from jax.experimental import pallas as pl
from jax.experimental.pallas import tpu as pltpu
from jax.sharding import PartitionSpec as P

HEADS = 15
KV_HEADS = 5
HEAD_DIM = 64
SHARE = HEADS // KV_HEADS
D = 960
HALF = 480
QD = 960
KVD = 320
UNITS = 640
OWN = 128
KEYS = 1024
SCALING = HEAD_DIM ** (-0.5)
MESH = pl.DeviceIdType.MESH
F32 = jnp.float32
BF16 = jnp.bfloat16
SLOTS = 288
CHUNKS = 15

norm_eps = 1e-05
rope_base = 100000.0


def dot(a, b):
    return jnp.dot(a, b, preferred_element_type=F32)


def dot_nt(a, b):
    return lax.dot_general(a, b, (((1,), (1,)), ((), ())), preferred_element_type=F32)


def dot_tn(a, b):
    return lax.dot_general(a, b, (((0,), (0,)), ((), ())), preferred_element_type=F32)


def heads_of(x, group):
    first = group * SHARE
    return jnp.concatenate(
        [x[:, (first + j) * HEAD_DIM : (first + j + 1) * HEAD_DIM] for j in range(SHARE)], axis=0
    )


def rows_of(index, count):
    return pl.ds(pl.multiple_of(index * count, count), count)


class Place:
    def __init__(self, send_sem, recv_sem):
        col = lax.axis_index("col")
        self.dp, self.row = lax.axis_index("dp"), lax.axis_index("row")
        self.ranks = lax.axis_size("dp")
        self.z, self.x = self.dp // 4, self.dp % 4
        self.low, self.s = col // 2, col % 2
        self.y = self.row * 2 + self.low
        self.up, self.down, self.far = (self.y + 1) % 4, (self.y + 3) % 4, (self.y + 2) % 4
        self.send_sem, self.recv_sem, self.used = send_sem, recv_sem, 0
        self.open = []

    def device(self, y, s):
        return (self.dp, y // 2, (y % 2) * 2 + s)

    def rank(self, z, x):
        return (z * 4 + x, self.row, self.low * 2 + self.s)

    def peer(self, k):
        return ((self.dp + k) % self.ranks, self.row, self.low * 2 + self.s)

    def slots(self, count):
        first = self.used
        self.used += count
        assert self.used <= SLOTS
        return first

    def wire(self, src, dst, other, slot, recv_slot=None):
        return pltpu.make_async_remote_copy(
            src_ref=src,
            dst_ref=dst,
            send_sem=self.send_sem.at[slot],
            recv_sem=self.recv_sem.at[slot if recv_slot is None else recv_slot],
            device_id=other,
            device_id_type=MESH,
        )

    def send(self, src, dst, other):
        copy = self.wire(src, dst, other, self.slots(1))
        copy.start()
        self.open.append(copy)
        return copy

    def others(self):
        others = [self.peer(k) for k in range(1, self.ranks)]
        others += [self.device(self.y, 1 - self.s)]
        for y in (self.up, self.down, self.far):
            others += [self.device(y, self.s), self.device(y, 1 - self.s)]
        return others

    def greet(self):
        barrier = pltpu.get_barrier_semaphore()
        for other in self.others():
            pl.semaphore_signal(barrier, inc=1, device_id=other, device_id_type=MESH)

    def meet(self):
        pl.semaphore_wait(pltpu.get_barrier_semaphore(), len(self.others()))


class Gather:
    def __init__(self, at, buf, rows, split, index=None):
        self.at, self.buf = at, buf
        self.both = index is not None
        if index is None:
            self.mine, self.low, self.high, self.opposite = 0, 1, 2, 3
            self.to_up, self.to_down, self.on_up, self.on_down = 1, 2, 3, 3
        else:
            self.mine, self.low = index(at.y, at.s), index(at.down, at.s)
            self.high, self.opposite = index(at.up, at.s), index(at.far, at.s)
            self.to_up, self.to_down = self.mine, self.mine
            self.on_up, self.on_down = self.low, self.high
        self.first, self.second = pl.ds(0, split), pl.ds(split, rows - split)
        self.up_device, self.down_device = at.device(at.up, at.s), at.device(at.down, at.s)
        self.mate = at.device(at.y, 1 - at.s)
        self.from_mate = []

    def ship(self, index, part, to_index, other):
        return self.at.send(self.buf.at[index, part], self.buf.at[to_index, part], other)

    def to_mate(self, index):
        if self.both:
            self.from_mate.append(self.at.send(self.buf.at[index], self.buf.at[index], self.mate))

    def start(self):
        self.up_first = self.ship(self.mine, self.first, self.to_up, self.up_device)
        self.down_second = self.ship(self.mine, self.second, self.to_down, self.down_device)
        self.up_second = self.ship(self.mine, self.second, self.to_up, self.up_device)
        self.down_first = self.ship(self.mine, self.first, self.to_down, self.down_device)
        self.to_mate(self.mine)

    def relay(self):
        self.up_first.wait_recv()
        self.up_far = self.ship(self.low, self.first, self.on_up, self.up_device)
        self.down_second.wait_recv()
        self.down_far = self.ship(self.high, self.second, self.on_down, self.down_device)

    def near(self):
        self.up_second.wait_recv()
        self.to_mate(self.low)
        self.down_first.wait_recv()
        self.to_mate(self.high)

    def finish(self):
        self.up_far.wait_recv()
        self.down_far.wait_recv()
        self.to_mate(self.opposite)
        for copy in self.from_mate:
            copy.wait_recv()


class Reduce:
    def __init__(self, at, blocks, early, sums, landed):
        self.at, self.blocks = at, blocks
        self.early, self.sums, self.landed = early, sums, landed
        self.up_device, self.down_device = at.device(at.up, at.s), at.device(at.down, at.s)

    def start_far(self):
        at, far = self.at, self.blocks.at[3]
        self.first = at.send(far.at[0], self.early.at[0], self.down_device)
        self.second = at.send(far.at[1], self.early.at[1], self.up_device)

    def start_near(self):
        at = self.at
        self.third = at.send(self.blocks.at[1, 1], self.landed.at[0, 1], self.down_device)
        self.fourth = at.send(self.blocks.at[2, 0], self.landed.at[1, 0], self.up_device)

    def middle(self):
        at, blocks, early, sums = self.at, self.blocks, self.early, self.sums
        self.first.wait_recv()
        sums[0] = (blocks[1, 0].astype(F32) + early[0].astype(F32)).astype(BF16)
        self.fifth = at.send(sums.at[0], self.landed.at[0, 0], self.down_device)
        self.second.wait_recv()
        sums[1] = (blocks[2, 1].astype(F32) + early[1].astype(F32)).astype(BF16)
        self.sixth = at.send(sums.at[1], self.landed.at[1, 1], self.up_device)

    def finish(self):
        for copy in (self.third, self.fourth, self.fifth, self.sixth):
            copy.wait_recv()
        total = (
            self.blocks[0].astype(F32) + self.landed[0].astype(F32) + self.landed[1].astype(F32)
        )
        return total.reshape(total.shape[0] * total.shape[1], total.shape[2])


class Far:
    def __init__(self, at, src, on_up, on_down, relay):
        self.at, self.src, self.on_up, self.on_down, self.buf = at, src, on_up, on_down, relay
        self.up_device, self.down_device = at.device(at.up, at.s), at.device(at.down, at.s)
        self.low, self.high = pl.ds(0, OWN // 2), pl.ds(OWN // 2, OWN // 2)

    def first(self):
        at = self.at
        self.to_up = at.send(self.src.at[self.low], self.buf.at[0], self.up_device)
        self.to_down = at.send(self.src.at[self.high], self.buf.at[1], self.down_device)

    def relay(self):
        at = self.at
        self.to_up.wait_recv()
        self.last_up = at.send(self.buf.at[0], self.on_up.at[self.low], self.up_device)
        self.to_down.wait_recv()
        self.last_down = at.send(self.buf.at[1], self.on_down.at[self.high], self.down_device)

    def finish(self):
        self.last_up.wait_recv()
        self.last_down.wait_recv()


class Spread:
    def __init__(self, at, buf, guard=None):
        self.at, self.buf, self.guard = at, buf, guard
        self.slot = at.slots(18)

    def guarded(self, act):
        if self.guard is None:
            act()
        else:
            pl.when(self.guard)(act)

    def along(self, half, second, step):
        at = self.at
        if (half == 0) != second:
            return at.rank((at.z + step) % 4, at.x)
        return at.rank(at.z, (at.x + step) % 4)

    def first_copy(self, half, n):
        own = self.buf.at[self.at.z, self.at.x, half]
        return self.at.wire(own, own, self.along(half, False, (1, 3, 2)[n]), self.slot + half * 9 + n)

    def block(self, half, part, back):
        at, pair = self.at, pl.ds(2 * part, 2)
        if half == 0:
            return self.buf.at[pair, (at.x + 4 - back) % 4, half]
        return self.buf.at[(at.z + 4 - back) % 4, pair, half]

    def second_copy(self, half, n):
        step, part = ((1, 0), (3, 1), (1, 1), (3, 0))[n]
        src = self.block(half, part, 0)
        return self.at.wire(src, src, self.along(half, True, step), self.slot + half * 9 + 3 + n)

    def third_copy(self, half, n):
        step, part = ((1, 0), (3, 1))[n]
        src = self.block(half, part, step)
        return self.at.wire(src, src, self.along(half, True, step), self.slot + half * 9 + 7 + n)

    def first(self):
        def act():
            for half in range(2):
                for n in range(3):
                    self.first_copy(half, n).start()

        self.guarded(act)

    def second(self):
        def act():
            for half in range(2):
                for n in range(3):
                    self.first_copy(half, n).wait_recv()
                for n in range(4):
                    self.second_copy(half, n).start()

        self.guarded(act)

    def third(self):
        def act():
            for n in range(2):
                for half in range(2):
                    self.second_copy(half, n).wait_recv()
                    self.third_copy(half, n).start()

        self.guarded(act)

    def finish(self):
        def act():
            for half in range(2):
                for n in range(2, 4):
                    self.second_copy(half, n).wait_recv()
                for n in range(2):
                    self.third_copy(half, n).wait_recv()

        self.guarded(act)

    def drain(self):
        def act():
            for half in range(2):
                for n in range(3):
                    self.first_copy(half, n).wait_send()
                for n in range(4):
                    self.second_copy(half, n).wait_send()
                for n in range(2):
                    self.third_copy(half, n).wait_send()

        self.guarded(act)


class Collect:
    def __init__(self, at, kept, early, sums, landed, four, parts, total):
        self.at, self.kept, self.early, self.sums = at, kept, early, sums
        self.landed, self.four, self.parts, self.total = landed, four, parts, total

    def along(self, half, second, step):
        at = self.at
        if (half == 1) != second:
            return at.rank((at.z + step) % 4, at.x)
        return at.rank(at.z, (at.x + step) % 4)

    def block(self, half, step, part):
        at = self.at
        pair = slice(None) if part is None else pl.ds(2 * part, 2)
        if half == 0:
            return (pair, (at.x + step) % 4, half)
        return ((at.z + step) % 4, pair, half)

    def start(self):
        at, kept = self.at, self.kept
        self.far, self.near = {}, []
        for half in range(2):
            for n, step in ((0, 3), (1, 1)):
                self.far[half, n] = at.send(
                    kept.at[self.block(half, 2, n)], self.early.at[half, n], self.along(half, False, step)
                )
        for half in range(2):
            for n, step in ((0, 3), (1, 1)):
                self.near.append(
                    at.send(
                        kept.at[self.block(half, step, 1 - n)],
                        self.landed.at[half, n, pl.ds(2 * (1 - n), 2)],
                        self.along(half, False, step),
                    )
                )

    def middle(self):
        at, kept = self.at, self.kept
        for half in range(2):
            for n, step in ((0, 3), (1, 1)):
                self.far[half, n].wait_recv()
                self.sums[half, n] = (
                    kept[self.block(half, step, n)].astype(F32) + self.early[half, n].astype(F32)
                ).astype(BF16)
                self.near.append(
                    at.send(
                        self.sums.at[half, n],
                        self.landed.at[half, n, pl.ds(2 * n, 2)],
                        self.along(half, False, step),
                    )
                )

    def second(self):
        at = self.at
        for copy in self.near:
            copy.wait_recv()
        self.last = []
        for half in range(2):
            self.four[half] = (
                self.kept[self.block(half, 0, None)].astype(F32)
                + self.landed[half, 0].astype(F32)
                + self.landed[half, 1].astype(F32)
            ).astype(BF16)
            here = at.z if half == 0 else at.x
            for n, step in enumerate((1, 3, 2)):
                self.last.append(
                    at.send(
                        self.four.at[half, (here + step) % 4],
                        self.parts.at[half, n],
                        self.along(half, True, step),
                    )
                )

    def reduce(self):
        at = self.at
        for copy in self.last:
            copy.wait_recv()
        for half in range(2):
            acc = self.four[half, at.z if half == 0 else at.x].astype(F32)
            for n in range(3):
                acc = acc + self.parts[half, n].astype(F32)
            self.total[half] = acc.astype(BF16)


def unit_rows(values):
    inverse = lax.rsqrt(jnp.mean(values * values, axis=-1, keepdims=True) + norm_eps)
    return values * inverse, inverse


def norm_back(gradient, unit, inverse, gain_vec):
    scaled = gradient * gain_vec
    inner_sum = jnp.mean(scaled * unit, axis=1, keepdims=True)
    return (
        inverse * (scaled - unit * inner_sum),
        jnp.sum(gradient * unit, axis=0, keepdims=True),
    )


def turn(x, cosine, sine):
    half = HEAD_DIM // 2
    lane = lax.broadcasted_iota(jnp.int32, x.shape, 1) % HEAD_DIM
    swapped = jnp.where(lane < half, pltpu.roll(x, 128 - half, 1), pltpu.roll(x, half, 1))
    return x * cosine + swapped * sine


def turn_all(x, cosine, sine):
    width = x.shape[1]
    pieces = []
    for first in range(0, width, 128):
        piece = x[:, first : min(first + 128, width)]
        if piece.shape[1] < 128:
            wide = jnp.concatenate([piece, jnp.zeros_like(piece)], axis=1)
            piece = turn(wide, cosine, sine)[:, : piece.shape[1]]
        else:
            piece = turn(piece, cosine, sine)
        pieces.append(piece)
    return jnp.concatenate(pieces, axis=1)


IN_NAMES = ("hidden", "ids_in", "freq", "attn_gain", "ffn_gain")
IN_NAMES += ("q_w", "k_w", "v_w", "o_w", "gate_w", "up_w", "down_w", "d_out")
SCRATCH = dict(
    wq=((8, 240, HALF), BF16),
    wkv=((8, 160, HALF), BF16),
    o_parts=((2, 4, 4, 2, 2, 16, HALF), BF16),
    tokens=((2, OWN, D), BF16),
    own_o=((240, HALF), BF16),
    ids=((8, 16, OWN), BF16),
    normed_one=((2, OWN, HALF), BF16),
    bias=((OWN, KEYS), F32),
    cosine=((OWN, 128), F32),
    sine=((OWN, 128), F32),
    queries=((OWN, QD), BF16),
    kv=((8, OWN, 640), BF16),
    lse=((KV_HEADS, SHARE * OWN, 1), F32),
    attn=((OWN, QD), BF16),
    attn_halves=((2, OWN, HALF), BF16),
    attn_ring=((4, OWN, HALF), BF16),
    first_ring=((4, OWN, HALF), BF16),
    d_out_ring=((4, OWN, D), BF16),
    middle=((OWN, D), F32),
    normed_ring=((4, OWN, D), BF16),
    gate_up=((D, 2 * UNITS), BF16),
    down_parts=((2, 4, 4, 2, 16, UNITS), BF16),
    gate_land=((4, 4, 2, 16, 2 * UNITS), BF16),
    down=((D, UNITS), BF16),
    units=((4, OWN, UNITS), BF16),
    d_gate_up=((4, OWN, 2 * UNITS), BF16),
    ffn_parts=((4, 2, OWN // 2, D), BF16),
    ffn_early=((2, OWN // 2, D), BF16),
    ffn_sums=((2, OWN // 2, D), BF16),
    ffn_landed=((2, 2, OWN // 2, D), BF16),
    dn_parts=((4, 2, OWN // 2, D), BF16),
    dn_early=((2, OWN // 2, D), BF16),
    dn_sums=((2, OWN // 2, D), BF16),
    dn_landed=((2, 2, OWN // 2, D), BF16),
    ffn_halves=((2, 512, 1920), BF16),
    ffn_mate=((512, 1920), BF16),
    ffn_kept=((4, 4, 2, 16, 1920), BF16),
    ffn_far=((2, 2, 2, 16, 1920), BF16),
    ffn_pairs=((2, 2, 2, 16, 1920), BF16),
    ffn_near=((2, 2, 4, 16, 1920), BF16),
    ffn_four=((2, 4, 16, 1920), BF16),
    ffn_last=((2, 3, 16, 1920), BF16),
    ffn_sum=((2, 16, 1920), BF16),
    d_middle=((OWN, D), F32),
    d_y1_halves=((2, OWN, HALF), BF16),
    d_y1_ring=((4, OWN, HALF), BF16),
    d_kv=((8, OWN, 640), BF16),
    kv_mate=((4, OWN, 640), BF16),
    kv_parts=((4, 2, OWN // 2, 640), BF16),
    kv_early=((2, OWN // 2, 640), BF16),
    kv_sums=((2, OWN // 2, 640), BF16),
    kv_landed=((2, 2, OWN // 2, 640), BF16),
    d_q=((2, OWN, HALF), BF16),
    d_q_ring=((4, OWN, HALF), BF16),
    d_kv_own=((2, OWN, 320), BF16),
    d_kv_ring=((4, OWN, 320), BF16),
    gains=((4, 8, D), F32),
    qo_two=((2, 512, HALF), BF16),
    qo_mate=((512, HALF), BF16),
    kv_two=((2, 512, 160), BF16),
    kv_grad_mate=((512, 160), BF16),
    attn_kept=((4, 4, 2, 16, 640), BF16),
    attn_far=((2, 2, 2, 16, 640), BF16),
    attn_pairs=((2, 2, 2, 16, 640), BF16),
    attn_near=((2, 2, 4, 16, 640), BF16),
    attn_four=((2, 4, 16, 640), BF16),
    attn_last=((2, 3, 16, 640), BF16),
    attn_sum=((2, 16, 640), BF16),
    attn_relay=((2, OWN // 2, HALF), BF16),
    d_y1_relay=((2, OWN // 2, HALF), BF16),
    d_q_relay=((2, OWN // 2, HALF), BF16),
    d_kv_relay=((2, OWN // 2, 320), BF16),
    block_relay=((2, OWN // 2, D), BF16),
    input_relay=((2, OWN // 2, D), BF16),
    block_out=((2, OWN, D), BF16),
    input_grad=((2, OWN, D), BF16),
    attn_total=((4, 4, 2, 16, 640), BF16),
    ffn_total=((4, 4, 2, 16, 1920), BF16),
    out_sem=pltpu.SemaphoreType.DMA((4,)),
    send_sem=pltpu.SemaphoreType.DMA((SLOTS,)),
    recv_sem=pltpu.SemaphoreType.DMA((SLOTS,)),
)


def block_of(y, s):
    return ((y % 2) * 2 + s) * 2 + y // 2


def layer_kernel(*refs):
    count = len(IN_NAMES)
    outs, refs = refs[count : count + 4], refs[:count] + refs[count + 4 :]
    m = types.SimpleNamespace(**dict(zip(IN_NAMES + tuple(SCRATCH), refs)))
    leaving = []

    def leave(n, src):
        copy = pltpu.make_async_copy(src, outs[n], m.out_sem.at[n])
        copy.start()
        leaving.append(copy)

    at = Place(m.send_sem, m.recv_sem)
    row, low, s, y, dp = at.row, at.low, at.s, at.y, at.dp
    mate = at.device(y, 1 - s)
    up_device, down_device = at.device(at.up, s), at.device(at.down, s)
    far_device, cross = at.device(at.far, s), at.device(at.far, 1 - s)
    mine = block_of(y, s)
    active = dp < CHUNKS
    not_ = jnp.logical_not

    at.greet()

    wq, wkv, ids = m.wq, m.wkv, m.ids
    wq[mine] = m.q_w[...].T
    wkv[mine, 0:80] = m.k_w[...]
    wkv[mine, 80:160] = m.v_w[...]
    own_row = jnp.where(row == 0, m.ids_in[:, 0:OWN], m.ids_in[:, OWN:]).astype(F32)
    ids[mine] = jnp.broadcast_to(own_row, (16, OWN)).astype(BF16)
    m.own_o[...] = m.o_w[...].T
    at.meet()

    gate_up, o_parts, down_parts = m.gate_up, m.o_parts, m.down_parts
    o_slot, down_slot, gate_slot = at.slots(3), at.slots(2), at.slots(4)
    gate_mate_slot = at.slots(1)
    own_core = s == row
    strip = rows_of(dp, 16)

    def o_copy(n):
        other = (up_device, down_device, far_device)[n]
        return at.wire(m.own_o.at[strip], o_parts.at[s, at.z, at.x, row, low], other, o_slot + n)

    def down_copy(r):
        target = r * 2 + row
        return target, at.wire(
            m.down_w.at[strip, pl.ds(r * UNITS, UNITS)],
            down_parts.at[s, at.z, at.x, low],
            at.device(target, s),
            down_slot + r,
            down_slot + low,
        )

    def down_arrive(a):
        return low * 2 + a, at.wire(
            m.down_w.at[strip, pl.ds(0, UNITS)],
            down_parts.at[s, at.z, at.x, a],
            up_device,
            down_slot + a,
        )

    gate_land = m.gate_land

    def gate_copy(n, part):
        source = (m.gate_w, m.up_w)[n]
        return at.wire(
            source.at[pl.ds(pl.multiple_of(dp * 32 + 16 * part, 16), 16)],
            gate_land.at[at.z, at.x, part, :, pl.ds(UNITS * n, UNITS)],
            cross,
            gate_slot + 2 * n + part,
        )

    gate_copies = [(n, part) for n in range(2) for part in range(2)]
    o_spread = Spread(at, o_parts.at[s])
    down_spread = Spread(at, down_parts.at[s])
    gate_spread = Spread(at, gate_land, not_(own_core))
    spreads = (o_spread, gate_spread, down_spread)

    def gate_mate(half):
        rows = pl.ds(pl.multiple_of(half * HALF, 32), HALF)
        return at.wire(gate_up.at[rows], gate_up.at[rows], mate, gate_mate_slot)

    gather_kw = Gather(at, wkv, 160, 80, block_of)
    gather_qw = Gather(at, wq, 240, 112, block_of)
    gather_kw.start()
    ids_copies = [at.send(ids.at[mine], ids.at[mine], mate)]
    for other in (at.up, at.down, at.far):
        for core in (s, 1 - s):
            ids_copies.append(at.send(ids.at[mine], ids.at[mine], at.device(other, core)))

    @pl.when(active)
    def _():
        o_parts[s, at.z, at.x, row, low] = m.own_o[strip]
        for n in range(3):
            o_copy(n).start()
        for r in range(2):
            target, copy = down_copy(r)

            @pl.when(target == y)
            def _():
                down_parts[s, at.z, at.x, low] = m.down_w[strip, r * UNITS : (r + 1) * UNITS]

            @pl.when(target != y)
            def _():
                copy.start()

        @pl.when(not_(own_core))
        def _():
            for n, part in gate_copies:
                gate_copy(n, part).start()

    @pl.when(not_(active))
    def _():
        o_parts[s, at.z, at.x] = jnp.zeros((2, 2, 16, HALF), BF16)
        down_parts[s, at.z, at.x] = jnp.zeros((2, 16, UNITS), BF16)
        gate_land[at.z, at.x] = jnp.zeros((2, 16, 2 * UNITS), BF16)

    @pl.when(own_core)
    def _():
        rows = pl.ds(pl.multiple_of(row * HALF, 32), HALF)
        gate_up[rows, 0:UNITS] = m.gate_w[...]
        gate_up[rows, UNITS:] = m.up_w[...]
        gate_mate(row).start()

    tokens_two, d_out_ring = m.tokens, m.d_out_ring
    hidden, d_out = m.hidden[...].T, m.d_out[...].T
    tokens_two[0], tokens_two[1] = hidden[:OWN], hidden[OWN:]
    first_half = row == 0
    d_out_ring[0] = jnp.where(first_half, d_out[:OWN], d_out[OWN:])
    d_out_ring[3] = jnp.where(first_half, d_out[OWN:], d_out[:OWN])
    gather_kw.relay()
    gather_qw.start()
    attn_gain, ffn_gain = m.attn_gain[...], m.ffn_gain[...]
    unit_one, _ = unit_rows(tokens_two[row].astype(F32))
    normed = (unit_one * attn_gain).astype(BF16)
    m.normed_one[0] = normed[:, :HALF]
    m.normed_one[1] = normed[:, HALF:]
    first_ring = m.first_ring
    first_ring[0] = m.normed_one[row]
    unit_far, _ = unit_rows(tokens_two[1 - row].astype(F32))
    normed_far = (unit_far * attn_gain).astype(BF16)
    first_ring[3] = jnp.where(first_half, normed_far[:, :HALF], normed_far[:, HALF:])

    gather_kw.near()

    for copy in ids_copies:
        copy.wait_recv()
    own_ids = jnp.broadcast_to(own_row, (OWN, OWN)).T[:, 0:1].astype(jnp.int32)
    docs = jnp.concatenate([ids[b, 0:1, :] for b in range(8)], axis=1).astype(F32).astype(jnp.int32)
    earlier = jnp.sum((docs < own_ids).astype(F32), axis=1, keepdims=True)
    start = (low * 2 + s) * 256 + row * OWN
    position = start + lax.broadcasted_iota(jnp.int32, (OWN, 1), 0)
    angles = (position.astype(F32) - earlier) * m.freq[...]
    lane = lax.broadcasted_iota(jnp.int32, (OWN, 128), 1) % HEAD_DIM
    sine = jnp.sin(angles)
    m.cosine[...] = jnp.cos(angles)
    m.sine[...] = jnp.where(lane < HEAD_DIM // 2, -sine, sine)
    key_at = lax.broadcasted_iota(jnp.int32, (OWN, KEYS), 1)
    allowed = (own_ids == docs) & (key_at <= position)
    m.bias[...] = jnp.where(allowed, 0.0, -jnp.inf).astype(F32)

    @pl.when(active)
    def _():
        for n in range(3):
            o_copy(n).wait_recv()
        for a in range(2):
            source, copy = down_arrive(a)

            @pl.when(source != y)
            def _():
                copy.wait_recv()

        @pl.when(not_(own_core))
        def _():
            for n, part in gate_copies:
                gate_copy(n, part).wait_recv()

    for spread in spreads:
        spread.first()

    gather_kw.finish()

    def project(buf, c):
        part = dot_nt(m.normed_one[0], buf[2 * c]) + dot_nt(m.normed_one[1], buf[2 * c + 1])
        return part.astype(BF16).astype(F32)

    parts = [project(wkv, c) for c in range(4)]
    cosine, sine = m.cosine[...], m.sine[...]
    k = jnp.concatenate([part[:, 0:80] for part in parts], axis=1)
    v = jnp.concatenate([part[:, 80:160] for part in parts], axis=1)
    kv = m.kv
    kv[mine] = jnp.concatenate([turn_all(k, cosine, sine), v], axis=1).astype(BF16)
    gather_kv = Gather(at, kv, OWN, OWN // 2, block_of)
    gather_kv.start()
    gather_qw.relay()
    for spread in spreads:
        spread.second()
    gather_qw.near()
    gather_kv.relay()
    gather_qw.finish()
    q = jnp.concatenate([project(wq, c) for c in range(4)], axis=1)
    m.queries[...] = turn_all(q, cosine, sine).astype(BF16)
    for spread in spreads:
        spread.third()
    gather_kv.near()
    gather_kv.finish()
    d_out_copies = [
        at.send(d_out_ring.at[0], d_out_ring.at[1], up_device),
        at.send(d_out_ring.at[0], d_out_ring.at[2], down_device),
    ]

    o_spread.finish()
    o_mate = at.send(o_parts.at[s], o_parts.at[s], mate)

    for g in range(KV_HEADS):
        key = kv[:, :, g * HEAD_DIM : (g + 1) * HEAD_DIM].reshape(KEYS, HEAD_DIM)
        value = kv[:, :, KVD + g * HEAD_DIM : KVD + (g + 1) * HEAD_DIM].reshape(KEYS, HEAD_DIM)
        scores = dot_nt(heads_of(m.queries, g), key) * SCALING
        scores = scores.reshape(SHARE, OWN, KEYS) + m.bias[...][None]
        top = jnp.max(scores, axis=-1, keepdims=True)
        terms = jnp.exp(scores - top)
        total = jnp.sum(terms, axis=-1, keepdims=True)
        probs = (terms / total).astype(BF16).reshape(SHARE * OWN, KEYS)
        out = dot(probs, value).astype(BF16)
        for j in range(SHARE):
            head = (g * SHARE + j) * HEAD_DIM
            m.attn[:, head : head + HEAD_DIM] = out[j * OWN : (j + 1) * OWN]
        m.lse[g] = (top + jnp.log(total)).reshape(SHARE * OWN, 1)
    attn_halves = m.attn_halves
    attn_halves[0] = m.attn[:, :HALF]
    attn_halves[1] = m.attn[:, HALF:]
    o_mate.wait_recv()

    def o_block(r, c):
        return o_parts[c % 2, :, :, r, c // 2].reshape(256, HALF)[0:240]

    attn_out = [
        dot_nt(attn_halves[0], o_block(0, c)) + dot_nt(attn_halves[1], o_block(1, c)) for c in range(4)
    ]
    middle = tokens_two[row].astype(F32) + jnp.concatenate(attn_out, axis=1)
    m.middle[...] = middle
    unit_two, _ = unit_rows(middle)
    ring = m.normed_ring
    ring[0] = (unit_two * ffn_gain).astype(BF16)
    gather_n = Gather(at, ring, OWN, OWN // 2)
    gather_n.start()

    gate_spread.finish()

    @pl.when(not_(own_core))
    def _():
        rows = pl.ds(pl.multiple_of((1 - row) * HALF, 32), HALF)
        gate_up[rows] = gate_land[...].reshape(512, 2 * UNITS)[0:HALF]
        gate_mate(1 - row).start()

    down_spread.finish()
    down_mate = at.send(down_parts.at[s], down_parts.at[s], mate)
    gather_n.relay()
    down_mate.wait_recv()
    for c in range(4):
        m.down[c * 240 : (c + 1) * 240] = down_parts[c % 2, :, :, c // 2].reshape(256, UNITS)[0:240]
    for copy in d_out_copies:
        copy.wait_recv()
    gate_mate(row).wait_recv()

    ffn_parts, dn_parts = m.ffn_parts, m.dn_parts

    def feed(p):
        gate_and_up = dot(ring[p], gate_up[...]).astype(BF16)
        gate, raise_ = gate_and_up[:, :UNITS].astype(F32), gate_and_up[:, UNITS:].astype(F32)
        sig = 1.0 / (1.0 + jnp.exp(-gate))
        silu = gate * sig
        unit = (silu * raise_).astype(BF16)
        m.units[p] = unit
        d_unit = dot(d_out_ring[p], m.down[...])
        d_gate = (d_unit * raise_ * sig * (1.0 + gate * (1.0 - sig))).astype(BF16)
        d_up = (d_unit * silu).astype(BF16)
        m.d_gate_up[p] = jnp.concatenate([d_gate, d_up], axis=1)
        d_normed = dot_nt(m.d_gate_up[p], gate_up[...]).astype(BF16)
        dn_parts[p] = d_normed.reshape(2, OWN // 2, D)

    def feed_out(p):
        ffn_parts[p] = dot_nt(m.units[p], m.down[...]).astype(BF16).reshape(2, OWN // 2, D)

    dn = Reduce(at, dn_parts, m.dn_early, m.dn_sums, m.dn_landed)
    ffn = Reduce(at, ffn_parts, m.ffn_early, m.ffn_sums, m.ffn_landed)
    feed(0)
    gather_n.near()
    feed(1)
    feed(2)
    dn.start_near()
    gather_n.finish()
    feed(3)
    dn.start_far()

    halves = m.ffn_halves
    tokens_n = ring[...].reshape(4 * OWN, D)
    d_gate_up = m.d_gate_up[...].reshape(4 * OWN, 2 * UNITS)
    tokens_d = d_out_ring[...].reshape(4 * OWN, D)
    units = m.units[...].reshape(4 * OWN, UNITS)
    for h in range(2):
        halves[h, 0:HALF, 0 : 2 * UNITS] = dot_tn(tokens_n[:, h * HALF : (h + 1) * HALF], d_gate_up).astype(BF16)
        grad = dot_tn(tokens_d[:, h * HALF : (h + 1) * HALF], units).astype(BF16)
        for i in range(CHUNKS):
            halves[h, 32 * i : 32 * i + 16, 2 * UNITS :] = grad[16 * i : 16 * i + 16]
            halves[h, 32 * i + 16 : 32 * i + 32, 2 * UNITS :] = grad[240 + 16 * i : 256 + 16 * i]
        halves[h, HALF:, :] = jnp.zeros((32, 1920), BF16)
        if h == 0:
            dn.middle()
    ffn_pair = at.send(halves.at[1 - s], m.ffn_mate, mate)
    ffn_collect = Collect(
        at,
        m.ffn_kept,
        m.ffn_far,
        m.ffn_pairs,
        m.ffn_near,
        m.ffn_four,
        m.ffn_last,
        m.ffn_sum,
    )

    for p in (3, 1, 2, 0):
        feed_out(p)
    d_normed = dn.finish()
    middle = m.middle[...]
    unit_two, inverse_two = unit_rows(middle)
    d_middle, ffn_gain_part = norm_back(d_normed, unit_two, inverse_two, ffn_gain)
    d_middle = d_middle + d_out_ring[0].astype(F32)
    m.d_middle[...] = d_middle
    d_y1 = d_middle.astype(BF16)
    d_y1_halves, d_y1_ring = m.d_y1_halves, m.d_y1_ring
    d_y1_halves[0] = d_y1[:, :HALF]
    d_y1_halves[1] = d_y1[:, HALF:]
    d_attn = [0.0, 0.0]
    for c in range(4):
        for r in range(2):
            d_attn[r] = d_attn[r] + dot(d_y1[:, c * 240 : (c + 1) * 240], o_block(r, c))
    d_attn = jnp.concatenate(d_attn, axis=1).astype(BF16)

    up_low, up_row, down_row = 1 - low, at.up // 2, at.down // 2
    attn_ring, first_send = m.attn_ring, m.normed_one
    attn_far = Far(at, attn_halves.at[1 - row], attn_ring.at[3], attn_ring.at[3], m.attn_relay)
    d_y1_far = Far(at, d_y1_halves.at[low], d_y1_ring.at[3], d_y1_ring.at[3], m.d_y1_relay)
    attn_far.first()
    d_y1_far.first()
    side_copies = [
        at.send(d_y1_halves.at[up_low], d_y1_ring.at[1], up_device),
        at.send(d_y1_halves.at[up_low], d_y1_ring.at[2], down_device),
        at.send(attn_halves.at[up_row], attn_ring.at[1], up_device),
        at.send(attn_halves.at[down_row], attn_ring.at[2], down_device),
        at.send(first_send.at[up_row], first_ring.at[1], up_device),
        at.send(first_send.at[down_row], first_ring.at[2], down_device),
    ]
    attn_ring[0] = attn_halves[row]
    d_y1_ring[0] = d_y1_halves[low]

    d_kv = m.d_kv
    d_q = []
    for g in range(KV_HEADS):
        own = slice(g * HEAD_DIM, (g + 1) * HEAD_DIM)
        val = slice(KVD + g * HEAD_DIM, KVD + (g + 1) * HEAD_DIM)
        key = kv[:, :, own].reshape(KEYS, HEAD_DIM)
        value = kv[:, :, val].reshape(KEYS, HEAD_DIM)
        query, d_head = heads_of(m.queries, g), heads_of(d_attn, g)
        scores = dot_nt(query, key) * SCALING
        scores = scores.reshape(SHARE, OWN, KEYS) + m.bias[...][None]
        probs = jnp.exp(scores.reshape(SHARE * OWN, KEYS) - m.lse[g])
        d_probs = dot_nt(d_head, value)
        inner = jnp.sum(probs * d_probs, axis=-1, keepdims=True)
        d_scores = (probs * (d_probs - inner)).astype(BF16)
        d_query = dot(d_scores, key) * SCALING
        d_q += [d_query[j * OWN : (j + 1) * OWN] for j in range(SHARE)]
        d_kv[:, :, own] = (dot_tn(d_scores, query) * SCALING).astype(BF16).reshape(8, OWN, HEAD_DIM)
        d_kv[:, :, val] = dot_tn(probs.astype(BF16), d_head).astype(BF16).reshape(8, OWN, HEAD_DIM)
        if g == 0:
            ffn_pair.wait_recv()
            for z in range(4):
                for x in range(4):
                    rows = pl.ds(32 * (4 * z + x), 32)
                    both = halves[s, rows].astype(F32) + m.ffn_mate[rows].astype(F32)
                    m.ffn_kept[z, x] = both.astype(BF16).reshape(2, 16, 1920)
            ffn_collect.start()
        if g == 1:
            attn_far.relay()
            d_y1_far.relay()

    kv_copies = []
    order = ((3, at.far), (1, at.down), (2, at.up), (0, y))
    for p, t in order:
        kv_copies.append(at.send(d_kv.at[block_of(t, 1 - s)], m.kv_mate.at[p], mate))
    ffn_collect.middle()
    cosine, sine = m.cosine[...], -m.sine[...]
    d_q = turn_all(jnp.concatenate(d_q, axis=1), cosine, sine).astype(BF16)
    kv_sum = Reduce(at, m.kv_parts, m.kv_early, m.kv_sums, m.kv_landed)
    for (p, t), copy in zip(order, kv_copies):
        copy.wait_recv()
        both = d_kv[block_of(t, s)].astype(F32) + m.kv_mate[p].astype(F32)
        m.kv_parts[p] = both.astype(BF16).reshape(2, OWN // 2, 640)
        if p == 3:
            kv_sum.start_far()
        if p == 2:
            kv_sum.start_near()
    d_q_two, d_q_ring = m.d_q, m.d_q_ring
    d_q_two[0], d_q_two[1] = d_q[:, :HALF], d_q[:, HALF:]
    kv_sum.middle()
    q_copies = [
        at.send(d_q_two.at[up_low], d_q_ring.at[1], up_device),
        at.send(d_q_two.at[up_low], d_q_ring.at[2], down_device),
    ]
    d_q_far = Far(at, d_q_two.at[low], d_q_ring.at[3], d_q_ring.at[3], m.d_q_relay)
    d_q_far.first()
    d_q_ring[0] = d_q_two[low]
    d_normed_one = [0.0, 0.0]
    for c in range(4):
        for r in range(2):
            d_normed_one[r] = d_normed_one[r] + dot(d_q[:, c * 240 : (c + 1) * 240], wq[2 * c + r])

    ffn_collect.second()

    sums, ffn_total = m.ffn_sum, m.ffn_total
    gate_back_slot, back_slot = at.slots(1), at.slots(2)
    lanes = pl.ds(2 * UNITS, UNITS)
    owner = low * 2 + s

    def gate_back():
        both = pl.ds(0, 2 * UNITS)
        return at.wire(
            sums.at[:, :, both], ffn_total.at[at.z, at.x, :, :, both], cross, gate_back_slot
        )

    def down_back(j):
        return at.wire(
            sums.at[j, :, lanes],
            ffn_total.at[at.z, at.x, row, :, lanes],
            at.device(owner, j),
            back_slot + j,
            back_slot + row,
        )

    d_kv_sum = kv_sum.finish()
    d_k = turn_all(d_kv_sum[:, :KVD], cosine, sine).astype(BF16)
    d_v = d_kv_sum[:, KVD:].astype(BF16)
    d_kv_own, d_kv_ring = m.d_kv_own, m.d_kv_ring
    for a in range(2):
        d_kv_own[a] = jnp.concatenate(
            [d_k[:, a * 160 : (a + 1) * 160], d_v[:, a * 160 : (a + 1) * 160]], axis=1
        )
    d_kv_far = Far(at, d_kv_own.at[low], d_kv_ring.at[3], d_kv_ring.at[3], m.d_kv_relay)
    d_kv_far.first()
    kv_out = [
        at.send(d_kv_own.at[up_low], d_kv_ring.at[1], up_device),
        at.send(d_kv_own.at[up_low], d_kv_ring.at[2], down_device),
    ]
    d_kv_ring[0] = d_kv_own[low]
    d_q_far.relay()
    ffn_collect.reduce()

    @pl.when(own_core)
    def _():
        ffn_total[at.z, at.x, :, :, 0 : 2 * UNITS] = sums[:, :, 0 : 2 * UNITS]

    @pl.when(not_(own_core))
    def _():
        gate_back().start()

    for j in range(2):
        here = (owner == y) & (s == j)
        copy = down_back(j)

        @pl.when(here)
        def _():
            ffn_total[at.z, at.x, row, :, 2 * UNITS :] = sums[j, :, 2 * UNITS :]

        @pl.when(not_(here))
        def _():
            copy.start()

    for c in range(4):
        piece = jnp.concatenate(
            [d_k[:, c * 80 : (c + 1) * 80], d_v[:, c * 80 : (c + 1) * 80]], axis=1
        )
        for r in range(2):
            d_normed_one[r] = d_normed_one[r] + dot(piece, wkv[2 * c + r])
    unit_one, inverse_one = unit_rows(tokens_two[row].astype(F32))
    d_tokens, attn_gain_part = norm_back(
        jnp.concatenate(d_normed_one, axis=1), unit_one, inverse_one, attn_gain
    )
    gains = m.gains
    gains[0] = jnp.concatenate([attn_gain_part, ffn_gain_part, jnp.zeros((6, D), F32)], axis=0)
    gain_copies = [
        at.send(gains.at[0], gains.at[1], up_device),
        at.send(gains.at[0], gains.at[2], down_device),
        at.send(gains.at[0], gains.at[3], far_device),
    ]
    input_grad = m.input_grad
    input_grad[row] = (d_tokens + m.d_middle[...]).astype(BF16)
    input_far = Far(
        at, input_grad.at[row], input_grad.at[1 - up_row], input_grad.at[1 - down_row], m.input_relay
    )
    d_kv_far.relay()
    ffn.start_far()
    ffn.start_near()

    @pl.when(not_(own_core))
    def _():
        gate_back().wait_recv()

    for r in range(2):
        source = r * 2 + row

        @pl.when(not_((source == y) & (low == s)))
        def _():
            at.wire(
                sums.at[0, :, lanes],
                ffn_total.at[at.z, at.x, r, :, lanes],
                mate,
                back_slot + r,
            ).wait_recv()

    ffn_spread = Spread(at, ffn_total)
    ffn_spread.first()

    for copy in side_copies + q_copies:
        copy.wait_recv()
    for far in (attn_far, d_y1_far, d_q_far):
        far.finish()
    first_all = first_ring[...].reshape(4 * OWN, HALF)
    q_grad = dot_tn(first_all, d_q_ring[...].reshape(4 * OWN, HALF)).astype(BF16)
    o_grad = dot_tn(
        attn_ring[...].reshape(4 * OWN, HALF), d_y1_ring[...].reshape(4 * OWN, HALF)
    ).astype(BF16)
    qo_two, kv_two = m.qo_two, m.kv_two
    for b in range(2):
        pick = slice(b * 240, (b + 1) * 240)
        qo_two[b, 0:HALF, :] = jnp.concatenate([q_grad[:, pick], o_grad[:, pick]], axis=1)
        qo_two[b, HALF:, :] = jnp.zeros((32, HALF), BF16)
    qo_pair = at.send(qo_two.at[1 - s], m.qo_mate, mate)
    ffn.middle()

    for copy in kv_out + gain_copies:
        copy.wait_recv()
    d_kv_far.finish()
    kv_grad = dot_tn(first_all, d_kv_ring[...].reshape(4 * OWN, 320)).astype(BF16)
    gain_sum = (gains[0] + gains[1] + gains[2] + gains[3])[0:2].astype(BF16)
    gain_rows = [gain_sum[g : g + 1, p * 160 : (p + 1) * 160] for g in range(2) for p in range(6)]
    gain_block = jnp.concatenate(gain_rows + [jnp.zeros((20, 160), BF16)], axis=0)
    for b in range(2):
        kv_two[b, 0:HALF, :] = jnp.concatenate(
            [kv_grad[:, b * 80 : (b + 1) * 80], kv_grad[:, 160 + b * 80 : 160 + (b + 1) * 80]], axis=1
        )
        kv_two[b, HALF:, :] = gain_block
    kv_pair = at.send(kv_two.at[1 - s], m.kv_grad_mate, mate)
    ffn_spread.second()
    attn_kept = m.attn_kept
    for pair, two, theirs, first in (
        (qo_pair, qo_two, m.qo_mate, 0),
        (kv_pair, kv_two, m.kv_grad_mate, HALF),
    ):
        pair.wait_recv()
        both = (two[s].astype(F32) + theirs[...].astype(F32)).astype(BF16)
        width = both.shape[1]
        attn_kept[:, :, :, :, first : first + width] = both.reshape(4, 4, 2, 16, width)

    attn_collect = Collect(
        at,
        attn_kept,
        m.attn_far,
        m.attn_pairs,
        m.attn_near,
        m.attn_four,
        m.attn_last,
        m.attn_sum,
    )
    attn_collect.start()
    input_far.first()
    ffn_spread.third()
    attn_collect.middle()
    attn_collect.second()
    block_out = m.block_out
    block_out[row] = (m.middle[...] + ffn.finish()).astype(BF16)
    block_far = Far(
        at, block_out.at[row], block_out.at[1 - up_row], block_out.at[1 - down_row], m.block_relay
    )
    block_far.first()
    input_far.relay()
    attn_collect.reduce()
    attn_total = m.attn_total
    attn_total[at.z, at.x] = m.attn_sum[...]
    attn_spread = Spread(at, attn_total)
    attn_spread.first()
    block_far.relay()
    ffn_spread.finish()
    leave(3, ffn_total)
    attn_spread.second()
    input_far.finish()
    leave(1, input_grad)
    attn_spread.third()
    block_far.finish()
    leave(0, block_out)
    attn_spread.finish()
    leave(2, attn_total)
    for copy in leaving:
        copy.wait()

    for copy in at.open:
        copy.wait_send()
    gate_mate(row).wait_send()
    for spread in spreads + (ffn_spread, attn_spread):
        spread.drain()

    @pl.when(active)
    def _():
        for n in range(3):
            o_copy(n).wait_send()
        for r in range(2):
            target, copy = down_copy(r)

            @pl.when(target != y)
            def _():
                copy.wait_send()

        @pl.when(not_(own_core))
        def _():
            for n, part in gate_copies:
                gate_copy(n, part).wait_send()

    @pl.when(not_(own_core))
    def _():
        gate_back().wait_send()

    for j in range(2):
        copy = down_back(j)

        @pl.when(not_((owner == y) & (s == j)))
        def _():
            copy.wait_send()


RESULTS = (
    (D, 2 * OWN), (D, 2 * OWN), (1, D), (HALF, 240), (80, HALF), (80, HALF),
    (HALF, 240), (1, D), (HALF, UNITS), (HALF, UNITS), (240, 2 * UNITS),
)


def results_kernel(*refs):
    ins, outs, held, made = refs[:4], refs[4:15], refs[15:19], refs[19:30]
    in_sem, out_sem = refs[30:]
    copies = [
        pltpu.make_async_copy(ins[n], held[n], in_sem.at[n]) for n in range(4)
    ]
    for n in (3, 0, 1, 2):
        copies[n].start()
    block_in, input_in, attn_in, ffn_in = held
    leaving = []

    def leave(n):
        copy = pltpu.make_async_copy(made[n], outs[n], out_sem.at[n])
        copy.start()
        leaving.append(copy)

    copies[3].wait()
    for n in range(2):
        made[8 + n][...] = (
            ffn_in[0:CHUNKS, :, :, n * UNITS : (n + 1) * UNITS].reshape(HALF, UNITS).astype(F32)
        )
        leave(8 + n)
    for i in range(CHUNKS):
        for r in range(2):
            made[10][16 * i : 16 * i + 16, r * UNITS : (r + 1) * UNITS] = ffn_in[
                i, r, :, 2 * UNITS :
            ].astype(F32)
    leave(10)
    for n in range(2):
        copies[n].wait()
        made[n][...] = held[n][...].reshape(2 * OWN, D).astype(F32).T
        leave(n)
    copies[2].wait()
    made[3][...] = attn_in[0:CHUNKS, :, :, 0:240].reshape(HALF, 240).astype(F32)
    leave(3)
    made[6][...] = attn_in[0:CHUNKS, :, :, 240:480].reshape(HALF, 240).astype(F32)
    leave(6)
    kv_grad = attn_in[0:CHUNKS, :, :, 480:640].reshape(HALF, 160).astype(F32).T
    made[4][...] = kv_grad[0:80]
    made[5][...] = kv_grad[80:160]
    leave(4)
    leave(5)
    gains = attn_in[CHUNKS, 0, :, 480:640].astype(F32)
    for p in range(6):
        made[2][:, p * 160 : (p + 1) * 160] = gains[p : p + 1]
        made[7][:, p * 160 : (p + 1) * 160] = gains[6 + p : 7 + p]
    leave(2)
    leave(7)
    for copy in leaving:
        copy.wait()


def shards(
    hidden_in,
    segment_ids,
    attn_gain,
    q_weight,
    k_weight,
    v_weight,
    o_weight,
    ffn_gain,
    gate_weight,
    up_weight,
    down_weight,
    d_out,
):
    frequency = np.float32(rope_base) ** (-np.arange(HEAD_DIM // 2, dtype=np.float32) * 2 / HEAD_DIM)
    freq = jnp.asarray(np.tile(frequency.astype(np.float32), 4)[None, :])
    scratch = [
        pltpu.VMEM(*kind) if isinstance(kind, tuple) else kind for kind in SCRATCH.values()
    ]
    local = pl.BlockSpec(memory_space=pltpu.VMEM)
    kept = pl.pallas_call(
        layer_kernel,
        out_shape=[
            jax.ShapeDtypeStruct((2, OWN, D), BF16),
            jax.ShapeDtypeStruct((2, OWN, D), BF16),
            jax.ShapeDtypeStruct((4, 4, 2, 16, 640), BF16),
            jax.ShapeDtypeStruct((4, 4, 2, 16, 1920), BF16),
        ],
        in_specs=[local] * len(IN_NAMES),
        out_specs=[pl.BlockSpec(memory_space=pl.ANY)] * 4,
        scratch_shapes=scratch,
        compiler_params=pltpu.CompilerParams(
            collective_id=1, has_side_effects=True, vmem_limit_bytes=60 * 1024 * 1024
        ),
    )(
        hidden_in.T,
        segment_ids[None, :],
        freq,
        attn_gain[None, :],
        ffn_gain[None, :],
        q_weight,
        k_weight.T,
        v_weight.T,
        o_weight,
        gate_weight,
        up_weight,
        down_weight.T,
        d_out.T,
    )
    outs = pl.pallas_call(
        results_kernel,
        out_shape=[jax.ShapeDtypeStruct(shape, F32) for shape in RESULTS],
        in_specs=[pl.BlockSpec(memory_space=pl.ANY)] * 4,
        out_specs=[pl.BlockSpec(memory_space=pl.ANY)] * len(RESULTS),
        scratch_shapes=[
            pltpu.VMEM((2, OWN, D), BF16),
            pltpu.VMEM((2, OWN, D), BF16),
            pltpu.VMEM((16, 2, 16, 640), BF16),
            pltpu.VMEM((16, 2, 16, 1920), BF16),
        ]
        + [pltpu.VMEM(shape, F32) for shape in RESULTS]
        + [pltpu.SemaphoreType.DMA((4,)), pltpu.SemaphoreType.DMA((len(RESULTS),))],
        compiler_params=pltpu.CompilerParams(vmem_limit_bytes=62 * 1024 * 1024),
    )(kept[0], kept[1], kept[2].reshape(16, 2, 16, 640), kept[3].reshape(16, 2, 16, 1920))
    turned = (0, 1, 4, 5, 10)
    outs = [out.T if i in turned else out for i, out in enumerate(outs)]
    outs[2], outs[7] = outs[2].reshape(D), outs[7].reshape(D)
    return tuple(outs)


def solution(mesh):
    rows, blocks = P(("dp", "col"), None), P("row", "col")
    return jax.shard_map(
        shards,
        mesh=mesh,
        in_specs=(
            rows, P(("dp", "col")), P(), blocks, blocks, blocks, blocks, P(), blocks, blocks, blocks, rows,
        ),
        out_specs=(rows, rows, P(), blocks, blocks, blocks, blocks, P(), blocks, blocks, blocks),
        check_vma=False,
    )
```

```python
import types

import jax
import jax.numpy as jnp
import numpy as np
from jax import lax
from jax.experimental import pallas as pl
from jax.experimental.pallas import tpu as pltpu
from jax.sharding import PartitionSpec as P

HEADS = 15
KV_HEADS = 5
HEAD_DIM = 64
SHARE = HEADS // KV_HEADS
D = 960
HALF = 480
QD = 960
KVD = 320
UNITS = 640
OWN = 128
KEYS = 1024
SCALING = HEAD_DIM ** (-0.5)
MESH = pl.DeviceIdType.MESH
F32 = jnp.float32
BF16 = jnp.bfloat16
SLOTS = 288
CHUNKS = 15

norm_eps = 1e-05
rope_base = 100000.0


def dot(a, b):
    return jnp.dot(a, b, preferred_element_type=F32)


def dot_nt(a, b):
    return lax.dot_general(a, b, (((1,), (1,)), ((), ())), preferred_element_type=F32)


def dot_tn(a, b):
    return lax.dot_general(a, b, (((0,), (0,)), ((), ())), preferred_element_type=F32)


def heads_of(x, group):
    first = group * SHARE
    return jnp.concatenate(
        [x[:, (first + j) * HEAD_DIM : (first + j + 1) * HEAD_DIM] for j in range(SHARE)], axis=0
    )


def rows_of(index, count):
    return pl.ds(pl.multiple_of(index * count, count), count)


class Place:
    def __init__(self, send_sem, recv_sem):
        col = lax.axis_index("col")
        self.dp, self.row = lax.axis_index("dp"), lax.axis_index("row")
        self.ranks = lax.axis_size("dp")
        self.z, self.x = self.dp // 4, self.dp % 4
        self.low, self.s = col // 2, col % 2
        self.y = self.row * 2 + self.low
        self.up, self.down, self.far = (self.y + 1) % 4, (self.y + 3) % 4, (self.y + 2) % 4
        self.send_sem, self.recv_sem, self.used = send_sem, recv_sem, 0
        self.open = []

    def device(self, y, s):
        return (self.dp, y // 2, (y % 2) * 2 + s)

    def rank(self, z, x):
        return (z * 4 + x, self.row, self.low * 2 + self.s)

    def peer(self, k):
        return ((self.dp + k) % self.ranks, self.row, self.low * 2 + self.s)

    def slots(self, count):
        first = self.used
        self.used += count
        assert self.used <= SLOTS
        return first

    def wire(self, src, dst, other, slot, recv_slot=None):
        return pltpu.make_async_remote_copy(
            src_ref=src,
            dst_ref=dst,
            send_sem=self.send_sem.at[slot],
            recv_sem=self.recv_sem.at[slot if recv_slot is None else recv_slot],
            device_id=other,
            device_id_type=MESH,
        )

    def send(self, src, dst, other):
        copy = self.wire(src, dst, other, self.slots(1))
        copy.start()
        self.open.append(copy)
        return copy

    def others(self):
        others = [self.peer(k) for k in range(1, self.ranks)]
        others += [self.device(self.y, 1 - self.s)]
        for y in (self.up, self.down, self.far):
            others += [self.device(y, self.s), self.device(y, 1 - self.s)]
        return others

    def greet(self):
        barrier = pltpu.get_barrier_semaphore()
        for other in self.others():
            pl.semaphore_signal(barrier, inc=1, device_id=other, device_id_type=MESH)

    def meet(self):
        pl.semaphore_wait(pltpu.get_barrier_semaphore(), len(self.others()))


class Gather:
    def __init__(self, at, buf, rows, split, index=None):
        self.at, self.buf = at, buf
        self.both = index is not None
        if index is None:
            self.mine, self.low, self.high, self.opposite = 0, 1, 2, 3
            self.to_up, self.to_down, self.on_up, self.on_down = 1, 2, 3, 3
        else:
            self.mine, self.low = index(at.y, at.s), index(at.down, at.s)
            self.high, self.opposite = index(at.up, at.s), index(at.far, at.s)
            self.to_up, self.to_down = self.mine, self.mine
            self.on_up, self.on_down = self.low, self.high
        self.first, self.second = pl.ds(0, split), pl.ds(split, rows - split)
        self.up_device, self.down_device = at.device(at.up, at.s), at.device(at.down, at.s)
        self.mate = at.device(at.y, 1 - at.s)
        self.from_mate = []

    def ship(self, index, part, to_index, other):
        return self.at.send(self.buf.at[index, part], self.buf.at[to_index, part], other)

    def to_mate(self, index):
        if self.both:
            self.from_mate.append(self.at.send(self.buf.at[index], self.buf.at[index], self.mate))

    def start(self):
        self.up_first = self.ship(self.mine, self.first, self.to_up, self.up_device)
        self.down_second = self.ship(self.mine, self.second, self.to_down, self.down_device)
        self.up_second = self.ship(self.mine, self.second, self.to_up, self.up_device)
        self.down_first = self.ship(self.mine, self.first, self.to_down, self.down_device)
        self.to_mate(self.mine)

    def relay(self):
        self.up_first.wait_recv()
        self.up_far = self.ship(self.low, self.first, self.on_up, self.up_device)
        self.down_second.wait_recv()
        self.down_far = self.ship(self.high, self.second, self.on_down, self.down_device)

    def near(self):
        self.up_second.wait_recv()
        self.to_mate(self.low)
        self.down_first.wait_recv()
        self.to_mate(self.high)

    def finish(self):
        self.up_far.wait_recv()
        self.down_far.wait_recv()
        self.to_mate(self.opposite)
        for copy in self.from_mate:
            copy.wait_recv()


class Reduce:
    def __init__(self, at, blocks, early, sums, landed):
        self.at, self.blocks = at, blocks
        self.early, self.sums, self.landed = early, sums, landed
        self.up_device, self.down_device = at.device(at.up, at.s), at.device(at.down, at.s)

    def start_far(self):
        at, far = self.at, self.blocks.at[3]
        self.first = at.send(far.at[0], self.early.at[0], self.down_device)
        self.second = at.send(far.at[1], self.early.at[1], self.up_device)

    def start_near(self):
        at = self.at
        self.third = at.send(self.blocks.at[1, 1], self.landed.at[0, 1], self.down_device)
        self.fourth = at.send(self.blocks.at[2, 0], self.landed.at[1, 0], self.up_device)

    def middle(self):
        at, blocks, early, sums = self.at, self.blocks, self.early, self.sums
        self.first.wait_recv()
        sums[0] = (blocks[1, 0].astype(F32) + early[0].astype(F32)).astype(BF16)
        self.fifth = at.send(sums.at[0], self.landed.at[0, 0], self.down_device)
        self.second.wait_recv()
        sums[1] = (blocks[2, 1].astype(F32) + early[1].astype(F32)).astype(BF16)
        self.sixth = at.send(sums.at[1], self.landed.at[1, 1], self.up_device)

    def finish(self):
        for copy in (self.third, self.fourth, self.fifth, self.sixth):
            copy.wait_recv()
        total = (
            self.blocks[0].astype(F32) + self.landed[0].astype(F32) + self.landed[1].astype(F32)
        )
        return total.reshape(total.shape[0] * total.shape[1], total.shape[2])


class Far:
    def __init__(self, at, src, on_up, on_down, relay):
        self.at, self.src, self.on_up, self.on_down, self.buf = at, src, on_up, on_down, relay
        self.up_device, self.down_device = at.device(at.up, at.s), at.device(at.down, at.s)
        self.low, self.high = pl.ds(0, OWN // 2), pl.ds(OWN // 2, OWN // 2)

    def first(self):
        at = self.at
        self.to_up = at.send(self.src.at[self.low], self.buf.at[0], self.up_device)
        self.to_down = at.send(self.src.at[self.high], self.buf.at[1], self.down_device)

    def relay(self):
        at = self.at
        self.to_up.wait_recv()
        self.last_up = at.send(self.buf.at[0], self.on_up.at[self.low], self.up_device)
        self.to_down.wait_recv()
        self.last_down = at.send(self.buf.at[1], self.on_down.at[self.high], self.down_device)

    def finish(self):
        self.last_up.wait_recv()
        self.last_down.wait_recv()


class Spread:
    def __init__(self, at, buf, guard=None):
        self.at, self.buf, self.guard = at, buf, guard
        self.slot = at.slots(18)

    def guarded(self, act):
        if self.guard is None:
            act()
        else:
            pl.when(self.guard)(act)

    def along(self, half, second, step):
        at = self.at
        if (half == 0) != second:
            return at.rank((at.z + step) % 4, at.x)
        return at.rank(at.z, (at.x + step) % 4)

    def first_copy(self, half, n):
        own = self.buf.at[self.at.z, self.at.x, half]
        return self.at.wire(own, own, self.along(half, False, (1, 3, 2)[n]), self.slot + half * 9 + n)

    def block(self, half, part, back):
        at, pair = self.at, pl.ds(2 * part, 2)
        if half == 0:
            return self.buf.at[pair, (at.x + 4 - back) % 4, half]
        return self.buf.at[(at.z + 4 - back) % 4, pair, half]

    def second_copy(self, half, n):
        step, part = ((1, 0), (3, 1), (1, 1), (3, 0))[n]
        src = self.block(half, part, 0)
        return self.at.wire(src, src, self.along(half, True, step), self.slot + half * 9 + 3 + n)

    def third_copy(self, half, n):
        step, part = ((1, 0), (3, 1))[n]
        src = self.block(half, part, step)
        return self.at.wire(src, src, self.along(half, True, step), self.slot + half * 9 + 7 + n)

    def first(self):
        def act():
            for half in range(2):
                for n in range(3):
                    self.first_copy(half, n).start()

        self.guarded(act)

    def second(self):
        def act():
            for half in range(2):
                for n in range(3):
                    self.first_copy(half, n).wait_recv()
                for n in range(4):
                    self.second_copy(half, n).start()

        self.guarded(act)

    def third(self):
        def act():
            for n in range(2):
                for half in range(2):
                    self.second_copy(half, n).wait_recv()
                    self.third_copy(half, n).start()

        self.guarded(act)

    def finish(self):
        def act():
            for half in range(2):
                for n in range(2, 4):
                    self.second_copy(half, n).wait_recv()
                for n in range(2):
                    self.third_copy(half, n).wait_recv()

        self.guarded(act)

    def drain(self):
        def act():
            for half in range(2):
                for n in range(3):
                    self.first_copy(half, n).wait_send()
                for n in range(4):
                    self.second_copy(half, n).wait_send()
                for n in range(2):
                    self.third_copy(half, n).wait_send()

        self.guarded(act)


class Collect:
    def __init__(self, at, kept, early, sums, landed, four, parts, total):
        self.at, self.kept, self.early, self.sums = at, kept, early, sums
        self.landed, self.four, self.parts, self.total = landed, four, parts, total

    def along(self, half, second, step):
        at = self.at
        if (half == 1) != second:
            return at.rank((at.z + step) % 4, at.x)
        return at.rank(at.z, (at.x + step) % 4)

    def block(self, half, step, part):
        at = self.at
        pair = slice(None) if part is None else pl.ds(2 * part, 2)
        if half == 0:
            return (pair, (at.x + step) % 4, half)
        return ((at.z + step) % 4, pair, half)

    def start(self):
        at, kept = self.at, self.kept
        self.far, self.near = {}, []
        for half in range(2):
            for n, step in ((0, 3), (1, 1)):
                self.far[half, n] = at.send(
                    kept.at[self.block(half, 2, n)], self.early.at[half, n], self.along(half, False, step)
                )
        for half in range(2):
            for n, step in ((0, 3), (1, 1)):
                self.near.append(
                    at.send(
                        kept.at[self.block(half, step, 1 - n)],
                        self.landed.at[half, n, pl.ds(2 * (1 - n), 2)],
                        self.along(half, False, step),
                    )
                )

    def middle(self):
        at, kept = self.at, self.kept
        for half in range(2):
            for n, step in ((0, 3), (1, 1)):
                self.far[half, n].wait_recv()
                self.sums[half, n] = (
                    kept[self.block(half, step, n)].astype(F32) + self.early[half, n].astype(F32)
                ).astype(BF16)
                self.near.append(
                    at.send(
                        self.sums.at[half, n],
                        self.landed.at[half, n, pl.ds(2 * n, 2)],
                        self.along(half, False, step),
                    )
                )

    def second(self):
        at = self.at
        for copy in self.near:
            copy.wait_recv()
        self.last = []
        for half in range(2):
            self.four[half] = (
                self.kept[self.block(half, 0, None)].astype(F32)
                + self.landed[half, 0].astype(F32)
                + self.landed[half, 1].astype(F32)
            ).astype(BF16)
            here = at.z if half == 0 else at.x
            for n, step in enumerate((1, 3, 2)):
                self.last.append(
                    at.send(
                        self.four.at[half, (here + step) % 4],
                        self.parts.at[half, n],
                        self.along(half, True, step),
                    )
                )

    def reduce(self):
        at = self.at
        for copy in self.last:
            copy.wait_recv()
        for half in range(2):
            acc = self.four[half, at.z if half == 0 else at.x].astype(F32)
            for n in range(3):
                acc = acc + self.parts[half, n].astype(F32)
            self.total[half] = acc.astype(BF16)


def unit_rows(values):
    inverse = lax.rsqrt(jnp.mean(values * values, axis=-1, keepdims=True) + norm_eps)
    return values * inverse, inverse


def norm_back(gradient, unit, inverse, gain_vec):
    scaled = gradient * gain_vec
    inner_sum = jnp.mean(scaled * unit, axis=1, keepdims=True)
    return (
        inverse * (scaled - unit * inner_sum),
        jnp.sum(gradient * unit, axis=0, keepdims=True),
    )


def turn(x, cosine, sine):
    half = HEAD_DIM // 2
    lane = lax.broadcasted_iota(jnp.int32, x.shape, 1) % HEAD_DIM
    swapped = jnp.where(lane < half, pltpu.roll(x, 128 - half, 1), pltpu.roll(x, half, 1))
    return x * cosine + swapped * sine


def turn_all(x, cosine, sine):
    width = x.shape[1]
    pieces = []
    for first in range(0, width, 128):
        piece = x[:, first : min(first + 128, width)]
        if piece.shape[1] < 128:
            wide = jnp.concatenate([piece, jnp.zeros_like(piece)], axis=1)
            piece = turn(wide, cosine, sine)[:, : piece.shape[1]]
        else:
            piece = turn(piece, cosine, sine)
        pieces.append(piece)
    return jnp.concatenate(pieces, axis=1)


IN_NAMES = ("hidden", "ids_in", "freq", "attn_gain", "ffn_gain")
LARGE = ("hidden", "q_w", "k_w", "v_w", "o_w", "gate_w", "up_w", "down_w", "d_out")
IN_NAMES += ("q_w", "k_w", "v_w", "o_w", "gate_w", "up_w", "down_w", "d_out")
SCRATCH = dict(
    hidden=((D, 2 * OWN), BF16),
    q_w=((HALF, 240), BF16),
    k_w=((80, HALF), BF16),
    v_w=((80, HALF), BF16),
    o_w=((HALF, 240), BF16),
    gate_w=((HALF, UNITS), BF16),
    up_w=((HALF, UNITS), BF16),
    down_w=((240, 2 * UNITS), BF16),
    d_out=((D, 2 * OWN), BF16),
    in_sem=pltpu.SemaphoreType.DMA((9,)),
    wq=((8, 240, HALF), BF16),
    wkv=((8, 160, HALF), BF16),
    o_parts=((2, 4, 4, 2, 2, 16, HALF), BF16),
    tokens=((2, OWN, D), BF16),
    own_o=((240, HALF), BF16),
    ids=((8, 16, OWN), BF16),
    normed_one=((2, OWN, HALF), BF16),
    bias=((OWN, KEYS), F32),
    cosine=((OWN, 128), F32),
    sine=((OWN, 128), F32),
    queries=((OWN, QD), BF16),
    kv=((8, OWN, 640), BF16),
    lse=((KV_HEADS, SHARE * OWN, 1), F32),
    attn=((OWN, QD), BF16),
    attn_halves=((2, OWN, HALF), BF16),
    attn_ring=((4, OWN, HALF), BF16),
    first_ring=((4, OWN, HALF), BF16),
    d_out_ring=((4, OWN, D), BF16),
    middle=((OWN, D), F32),
    normed_ring=((4, OWN, D), BF16),
    gate_up=((D, 2 * UNITS), BF16),
    down_parts=((2, 4, 4, 2, 16, UNITS), BF16),
    gate_land=((4, 4, 2, 16, 2 * UNITS), BF16),
    down=((D, UNITS), BF16),
    units=((4, OWN, UNITS), BF16),
    d_gate_up=((4, OWN, 2 * UNITS), BF16),
    ffn_parts=((4, 2, OWN // 2, D), BF16),
    ffn_early=((2, OWN // 2, D), BF16),
    ffn_sums=((2, OWN // 2, D), BF16),
    ffn_landed=((2, 2, OWN // 2, D), BF16),
    dn_parts=((4, 2, OWN // 2, D), BF16),
    dn_early=((2, OWN // 2, D), BF16),
    dn_sums=((2, OWN // 2, D), BF16),
    dn_landed=((2, 2, OWN // 2, D), BF16),
    ffn_halves=((2, 512, 1920), BF16),
    ffn_mate=((512, 1920), BF16),
    ffn_kept=((4, 4, 2, 16, 1920), BF16),
    ffn_far=((2, 2, 2, 16, 1920), BF16),
    ffn_pairs=((2, 2, 2, 16, 1920), BF16),
    ffn_near=((2, 2, 4, 16, 1920), BF16),
    ffn_four=((2, 4, 16, 1920), BF16),
    ffn_last=((2, 3, 16, 1920), BF16),
    ffn_sum=((2, 16, 1920), BF16),
    d_middle=((OWN, D), F32),
    d_y1_halves=((2, OWN, HALF), BF16),
    d_y1_ring=((4, OWN, HALF), BF16),
    d_kv=((8, OWN, 640), BF16),
    kv_mate=((4, OWN, 640), BF16),
    kv_parts=((4, 2, OWN // 2, 640), BF16),
    kv_early=((2, OWN // 2, 640), BF16),
    kv_sums=((2, OWN // 2, 640), BF16),
    kv_landed=((2, 2, OWN // 2, 640), BF16),
    d_q=((2, OWN, HALF), BF16),
    d_q_ring=((4, OWN, HALF), BF16),
    d_kv_own=((2, OWN, 320), BF16),
    d_kv_ring=((4, OWN, 320), BF16),
    gains=((4, 8, D), F32),
    qo_two=((2, 512, HALF), BF16),
    qo_mate=((512, HALF), BF16),
    kv_two=((2, 512, 160), BF16),
    kv_grad_mate=((512, 160), BF16),
    attn_kept=((4, 4, 2, 16, 640), BF16),
    attn_far=((2, 2, 2, 16, 640), BF16),
    attn_pairs=((2, 2, 2, 16, 640), BF16),
    attn_near=((2, 2, 4, 16, 640), BF16),
    attn_four=((2, 4, 16, 640), BF16),
    attn_last=((2, 3, 16, 640), BF16),
    attn_sum=((2, 16, 640), BF16),
    attn_relay=((2, OWN // 2, HALF), BF16),
    d_y1_relay=((2, OWN // 2, HALF), BF16),
    d_q_relay=((2, OWN // 2, HALF), BF16),
    d_kv_relay=((2, OWN // 2, 320), BF16),
    block_relay=((2, OWN // 2, D), BF16),
    input_relay=((2, OWN // 2, D), BF16),
    block_out=((2, OWN, D), BF16),
    input_grad=((2, OWN, D), BF16),
    attn_total=((4, 4, 2, 16, 640), BF16),
    ffn_total=((4, 4, 2, 16, 1920), BF16),
    out_sem=pltpu.SemaphoreType.DMA((4,)),
    send_sem=pltpu.SemaphoreType.DMA((SLOTS,)),
    recv_sem=pltpu.SemaphoreType.DMA((SLOTS,)),
)


def block_of(y, s):
    return ((y % 2) * 2 + s) * 2 + y // 2


def layer_kernel(*refs):
    count = len(IN_NAMES)
    outs, refs = refs[count : count + 4], refs[:count] + refs[count + 4 :]
    given = dict(zip(IN_NAMES, refs))
    held = dict(zip(SCRATCH, refs[count:]))
    m = types.SimpleNamespace(**{**given, **held})
    leaving = []

    def leave(n, src):
        copy = pltpu.make_async_copy(src, outs[n], m.out_sem.at[n])
        copy.start()
        leaving.append(copy)

    at = Place(m.send_sem, m.recv_sem)
    row, low, s, y, dp = at.row, at.low, at.s, at.y, at.dp
    mate = at.device(y, 1 - s)
    up_device, down_device = at.device(at.up, s), at.device(at.down, s)
    far_device, cross = at.device(at.far, s), at.device(at.far, 1 - s)
    mine = block_of(y, s)
    active = dp < CHUNKS
    not_ = jnp.logical_not

    at.greet()
    fetches = {}
    for n, name in enumerate(("k_w", "v_w", "q_w", "o_w", "down_w", "gate_w", "up_w", "hidden", "d_out")):
        fetches[name] = pltpu.make_async_copy(given[name], held[name], m.in_sem.at[n])
        fetches[name].start()

    def fetched(*some):
        for name in some:
            fetches[name].wait()

    wq, wkv, ids = m.wq, m.wkv, m.ids
    fetched("k_w", "v_w", "q_w", "o_w")
    wq[mine] = m.q_w[...].T
    wkv[mine, 0:80] = m.k_w[...]
    wkv[mine, 80:160] = m.v_w[...]
    own_row = jnp.where(row == 0, m.ids_in[:, 0:OWN], m.ids_in[:, OWN:]).astype(F32)
    ids[mine] = jnp.broadcast_to(own_row, (16, OWN)).astype(BF16)
    m.own_o[...] = m.o_w[...].T
    fetched("down_w", "gate_w", "up_w")
    at.meet()

    gate_up, o_parts, down_parts = m.gate_up, m.o_parts, m.down_parts
    o_slot, down_slot, gate_slot = at.slots(3), at.slots(2), at.slots(4)
    gate_mate_slot = at.slots(1)
    own_core = s == row
    strip = rows_of(dp, 16)

    def o_copy(n):
        other = (up_device, down_device, far_device)[n]
        return at.wire(m.own_o.at[strip], o_parts.at[s, at.z, at.x, row, low], other, o_slot + n)

    def down_copy(r):
        target = r * 2 + row
        return target, at.wire(
            m.down_w.at[strip, pl.ds(r * UNITS, UNITS)],
            down_parts.at[s, at.z, at.x, low],
            at.device(target, s),
            down_slot + r,
            down_slot + low,
        )

    def down_arrive(a):
        return low * 2 + a, at.wire(
            m.down_w.at[strip, pl.ds(0, UNITS)],
            down_parts.at[s, at.z, at.x, a],
            up_device,
            down_slot + a,
        )

    gate_land = m.gate_land

    def gate_copy(n, part):
        source = (m.gate_w, m.up_w)[n]
        return at.wire(
            source.at[pl.ds(pl.multiple_of(dp * 32 + 16 * part, 16), 16)],
            gate_land.at[at.z, at.x, part, :, pl.ds(UNITS * n, UNITS)],
            cross,
            gate_slot + 2 * n + part,
        )

    gate_copies = [(n, part) for n in range(2) for part in range(2)]
    o_spread = Spread(at, o_parts.at[s])
    down_spread = Spread(at, down_parts.at[s])
    gate_spread = Spread(at, gate_land, not_(own_core))
    spreads = (o_spread, gate_spread, down_spread)

    def gate_mate(half):
        rows = pl.ds(pl.multiple_of(half * HALF, 32), HALF)
        return at.wire(gate_up.at[rows], gate_up.at[rows], mate, gate_mate_slot)

    gather_kw = Gather(at, wkv, 160, 80, block_of)
    gather_qw = Gather(at, wq, 240, 112, block_of)
    gather_kw.start()
    ids_copies = [at.send(ids.at[mine], ids.at[mine], mate)]
    for other in (at.up, at.down, at.far):
        for core in (s, 1 - s):
            ids_copies.append(at.send(ids.at[mine], ids.at[mine], at.device(other, core)))

    @pl.when(active)
    def _():
        o_parts[s, at.z, at.x, row, low] = m.own_o[strip]
        for n in range(3):
            o_copy(n).start()
        for r in range(2):
            target, copy = down_copy(r)

            @pl.when(target == y)
            def _():
                down_parts[s, at.z, at.x, low] = m.down_w[strip, r * UNITS : (r + 1) * UNITS]

            @pl.when(target != y)
            def _():
                copy.start()

        @pl.when(not_(own_core))
        def _():
            for n, part in gate_copies:
                gate_copy(n, part).start()

    @pl.when(not_(active))
    def _():
        o_parts[s, at.z, at.x] = jnp.zeros((2, 2, 16, HALF), BF16)
        down_parts[s, at.z, at.x] = jnp.zeros((2, 16, UNITS), BF16)
        gate_land[at.z, at.x] = jnp.zeros((2, 16, 2 * UNITS), BF16)

    @pl.when(own_core)
    def _():
        rows = pl.ds(pl.multiple_of(row * HALF, 32), HALF)
        gate_up[rows, 0:UNITS] = m.gate_w[...]
        gate_up[rows, UNITS:] = m.up_w[...]
        gate_mate(row).start()

    tokens_two, d_out_ring = m.tokens, m.d_out_ring
    fetched("hidden", "d_out")
    hidden, d_out = m.hidden[...].T, m.d_out[...].T
    tokens_two[0], tokens_two[1] = hidden[:OWN], hidden[OWN:]
    first_half = row == 0
    d_out_ring[0] = jnp.where(first_half, d_out[:OWN], d_out[OWN:])
    d_out_ring[3] = jnp.where(first_half, d_out[OWN:], d_out[:OWN])
    gather_kw.relay()
    gather_qw.start()
    attn_gain, ffn_gain = m.attn_gain[...], m.ffn_gain[...]
    unit_one, _ = unit_rows(tokens_two[row].astype(F32))
    normed = (unit_one * attn_gain).astype(BF16)
    m.normed_one[0] = normed[:, :HALF]
    m.normed_one[1] = normed[:, HALF:]
    first_ring = m.first_ring
    first_ring[0] = m.normed_one[row]
    unit_far, _ = unit_rows(tokens_two[1 - row].astype(F32))
    normed_far = (unit_far * attn_gain).astype(BF16)
    first_ring[3] = jnp.where(first_half, normed_far[:, :HALF], normed_far[:, HALF:])

    gather_kw.near()

    for copy in ids_copies:
        copy.wait_recv()
    own_ids = jnp.broadcast_to(own_row, (OWN, OWN)).T[:, 0:1].astype(jnp.int32)
    docs = jnp.concatenate([ids[b, 0:1, :] for b in range(8)], axis=1).astype(F32).astype(jnp.int32)
    earlier = jnp.sum((docs < own_ids).astype(F32), axis=1, keepdims=True)
    start = (low * 2 + s) * 256 + row * OWN
    position = start + lax.broadcasted_iota(jnp.int32, (OWN, 1), 0)
    angles = (position.astype(F32) - earlier) * m.freq[...]
    lane = lax.broadcasted_iota(jnp.int32, (OWN, 128), 1) % HEAD_DIM
    sine = jnp.sin(angles)
    m.cosine[...] = jnp.cos(angles)
    m.sine[...] = jnp.where(lane < HEAD_DIM // 2, -sine, sine)
    key_at = lax.broadcasted_iota(jnp.int32, (OWN, KEYS), 1)
    allowed = (own_ids == docs) & (key_at <= position)
    m.bias[...] = jnp.where(allowed, 0.0, -jnp.inf).astype(F32)

    @pl.when(active)
    def _():
        for n in range(3):
            o_copy(n).wait_recv()
        for a in range(2):
            source, copy = down_arrive(a)

            @pl.when(source != y)
            def _():
                copy.wait_recv()

        @pl.when(not_(own_core))
        def _():
            for n, part in gate_copies:
                gate_copy(n, part).wait_recv()

    for spread in spreads:
        spread.first()

    gather_kw.finish()

    def project(buf, c):
        part = dot_nt(m.normed_one[0], buf[2 * c]) + dot_nt(m.normed_one[1], buf[2 * c + 1])
        return part.astype(BF16).astype(F32)

    parts = [project(wkv, c) for c in range(4)]
    cosine, sine = m.cosine[...], m.sine[...]
    k = jnp.concatenate([part[:, 0:80] for part in parts], axis=1)
    v = jnp.concatenate([part[:, 80:160] for part in parts], axis=1)
    kv = m.kv
    kv[mine] = jnp.concatenate([turn_all(k, cosine, sine), v], axis=1).astype(BF16)
    gather_kv = Gather(at, kv, OWN, OWN // 2, block_of)
    gather_kv.start()
    gather_qw.relay()
    for spread in spreads:
        spread.second()
    gather_qw.near()
    gather_kv.relay()
    gather_qw.finish()
    q = jnp.concatenate([project(wq, c) for c in range(4)], axis=1)
    m.queries[...] = turn_all(q, cosine, sine).astype(BF16)
    for spread in spreads:
        spread.third()
    gather_kv.near()
    gather_kv.finish()
    d_out_copies = [
        at.send(d_out_ring.at[0], d_out_ring.at[1], up_device),
        at.send(d_out_ring.at[0], d_out_ring.at[2], down_device),
    ]

    o_spread.finish()
    o_mate = at.send(o_parts.at[s], o_parts.at[s], mate)

    for g in range(KV_HEADS):
        key = kv[:, :, g * HEAD_DIM : (g + 1) * HEAD_DIM].reshape(KEYS, HEAD_DIM)
        value = kv[:, :, KVD + g * HEAD_DIM : KVD + (g + 1) * HEAD_DIM].reshape(KEYS, HEAD_DIM)
        scores = dot_nt(heads_of(m.queries, g), key) * SCALING
        scores = scores.reshape(SHARE, OWN, KEYS) + m.bias[...][None]
        top = jnp.max(scores, axis=-1, keepdims=True)
        terms = jnp.exp(scores - top)
        total = jnp.sum(terms, axis=-1, keepdims=True)
        probs = (terms / total).astype(BF16).reshape(SHARE * OWN, KEYS)
        out = dot(probs, value).astype(BF16)
        for j in range(SHARE):
            head = (g * SHARE + j) * HEAD_DIM
            m.attn[:, head : head + HEAD_DIM] = out[j * OWN : (j + 1) * OWN]
        m.lse[g] = (top + jnp.log(total)).reshape(SHARE * OWN, 1)
    attn_halves = m.attn_halves
    attn_halves[0] = m.attn[:, :HALF]
    attn_halves[1] = m.attn[:, HALF:]
    o_mate.wait_recv()

    def o_block(r, c):
        return o_parts[c % 2, :, :, r, c // 2].reshape(256, HALF)[0:240]

    attn_out = [
        dot_nt(attn_halves[0], o_block(0, c)) + dot_nt(attn_halves[1], o_block(1, c)) for c in range(4)
    ]
    middle = tokens_two[row].astype(F32) + jnp.concatenate(attn_out, axis=1)
    m.middle[...] = middle
    unit_two, _ = unit_rows(middle)
    ring = m.normed_ring
    ring[0] = (unit_two * ffn_gain).astype(BF16)
    gather_n = Gather(at, ring, OWN, OWN // 2)
    gather_n.start()

    gate_spread.finish()

    @pl.when(not_(own_core))
    def _():
        rows = pl.ds(pl.multiple_of((1 - row) * HALF, 32), HALF)
        gate_up[rows] = gate_land[...].reshape(512, 2 * UNITS)[0:HALF]
        gate_mate(1 - row).start()

    down_spread.finish()
    down_mate = at.send(down_parts.at[s], down_parts.at[s], mate)
    gather_n.relay()
    down_mate.wait_recv()
    for c in range(4):
        m.down[c * 240 : (c + 1) * 240] = down_parts[c % 2, :, :, c // 2].reshape(256, UNITS)[0:240]
    for copy in d_out_copies:
        copy.wait_recv()
    gate_mate(row).wait_recv()

    ffn_parts, dn_parts = m.ffn_parts, m.dn_parts

    def feed(p):
        gate_and_up = dot(ring[p], gate_up[...]).astype(BF16)
        gate, raise_ = gate_and_up[:, :UNITS].astype(F32), gate_and_up[:, UNITS:].astype(F32)
        sig = 1.0 / (1.0 + jnp.exp(-gate))
        silu = gate * sig
        unit = (silu * raise_).astype(BF16)
        m.units[p] = unit
        d_unit = dot(d_out_ring[p], m.down[...])
        d_gate = (d_unit * raise_ * sig * (1.0 + gate * (1.0 - sig))).astype(BF16)
        d_up = (d_unit * silu).astype(BF16)
        m.d_gate_up[p] = jnp.concatenate([d_gate, d_up], axis=1)
        d_normed = dot_nt(m.d_gate_up[p], gate_up[...]).astype(BF16)
        dn_parts[p] = d_normed.reshape(2, OWN // 2, D)

    def feed_out(p):
        ffn_parts[p] = dot_nt(m.units[p], m.down[...]).astype(BF16).reshape(2, OWN // 2, D)

    dn = Reduce(at, dn_parts, m.dn_early, m.dn_sums, m.dn_landed)
    ffn = Reduce(at, ffn_parts, m.ffn_early, m.ffn_sums, m.ffn_landed)
    feed(0)
    gather_n.near()
    feed(1)
    feed(2)
    dn.start_near()
    gather_n.finish()
    feed(3)
    dn.start_far()

    halves = m.ffn_halves
    tokens_n = ring[...].reshape(4 * OWN, D)
    d_gate_up = m.d_gate_up[...].reshape(4 * OWN, 2 * UNITS)
    tokens_d = d_out_ring[...].reshape(4 * OWN, D)
    units = m.units[...].reshape(4 * OWN, UNITS)
    for h in range(2):
        halves[h, 0:HALF, 0 : 2 * UNITS] = dot_tn(tokens_n[:, h * HALF : (h + 1) * HALF], d_gate_up).astype(BF16)
        grad = dot_tn(tokens_d[:, h * HALF : (h + 1) * HALF], units).astype(BF16)
        for i in range(CHUNKS):
            halves[h, 32 * i : 32 * i + 16, 2 * UNITS :] = grad[16 * i : 16 * i + 16]
            halves[h, 32 * i + 16 : 32 * i + 32, 2 * UNITS :] = grad[240 + 16 * i : 256 + 16 * i]
        halves[h, HALF:, :] = jnp.zeros((32, 1920), BF16)
        if h == 0:
            dn.middle()
    ffn_pair = at.send(halves.at[1 - s], m.ffn_mate, mate)
    ffn_collect = Collect(
        at,
        m.ffn_kept,
        m.ffn_far,
        m.ffn_pairs,
        m.ffn_near,
        m.ffn_four,
        m.ffn_last,
        m.ffn_sum,
    )

    for p in (3, 1, 2, 0):
        feed_out(p)
    d_normed = dn.finish()
    middle = m.middle[...]
    unit_two, inverse_two = unit_rows(middle)
    d_middle, ffn_gain_part = norm_back(d_normed, unit_two, inverse_two, ffn_gain)
    d_middle = d_middle + d_out_ring[0].astype(F32)
    m.d_middle[...] = d_middle
    d_y1 = d_middle.astype(BF16)
    d_y1_halves, d_y1_ring = m.d_y1_halves, m.d_y1_ring
    d_y1_halves[0] = d_y1[:, :HALF]
    d_y1_halves[1] = d_y1[:, HALF:]
    d_attn = [0.0, 0.0]
    for c in range(4):
        for r in range(2):
            d_attn[r] = d_attn[r] + dot(d_y1[:, c * 240 : (c + 1) * 240], o_block(r, c))
    d_attn = jnp.concatenate(d_attn, axis=1).astype(BF16)

    up_low, up_row, down_row = 1 - low, at.up // 2, at.down // 2
    attn_ring, first_send = m.attn_ring, m.normed_one
    attn_far = Far(at, attn_halves.at[1 - row], attn_ring.at[3], attn_ring.at[3], m.attn_relay)
    d_y1_far = Far(at, d_y1_halves.at[low], d_y1_ring.at[3], d_y1_ring.at[3], m.d_y1_relay)
    attn_far.first()
    d_y1_far.first()
    side_copies = [
        at.send(d_y1_halves.at[up_low], d_y1_ring.at[1], up_device),
        at.send(d_y1_halves.at[up_low], d_y1_ring.at[2], down_device),
        at.send(attn_halves.at[up_row], attn_ring.at[1], up_device),
        at.send(attn_halves.at[down_row], attn_ring.at[2], down_device),
        at.send(first_send.at[up_row], first_ring.at[1], up_device),
        at.send(first_send.at[down_row], first_ring.at[2], down_device),
    ]
    attn_ring[0] = attn_halves[row]
    d_y1_ring[0] = d_y1_halves[low]

    d_kv = m.d_kv
    d_q = []
    for g in range(KV_HEADS):
        own = slice(g * HEAD_DIM, (g + 1) * HEAD_DIM)
        val = slice(KVD + g * HEAD_DIM, KVD + (g + 1) * HEAD_DIM)
        key = kv[:, :, own].reshape(KEYS, HEAD_DIM)
        value = kv[:, :, val].reshape(KEYS, HEAD_DIM)
        query, d_head = heads_of(m.queries, g), heads_of(d_attn, g)
        scores = dot_nt(query, key) * SCALING
        scores = scores.reshape(SHARE, OWN, KEYS) + m.bias[...][None]
        probs = jnp.exp(scores.reshape(SHARE * OWN, KEYS) - m.lse[g])
        d_probs = dot_nt(d_head, value)
        inner = jnp.sum(probs * d_probs, axis=-1, keepdims=True)
        d_scores = (probs * (d_probs - inner)).astype(BF16)
        d_query = dot(d_scores, key) * SCALING
        d_q += [d_query[j * OWN : (j + 1) * OWN] for j in range(SHARE)]
        d_kv[:, :, own] = (dot_tn(d_scores, query) * SCALING).astype(BF16).reshape(8, OWN, HEAD_DIM)
        d_kv[:, :, val] = dot_tn(probs.astype(BF16), d_head).astype(BF16).reshape(8, OWN, HEAD_DIM)
        if g == 0:
            ffn_pair.wait_recv()
            for z in range(4):
                for x in range(4):
                    rows = pl.ds(32 * (4 * z + x), 32)
                    both = halves[s, rows].astype(F32) + m.ffn_mate[rows].astype(F32)
                    m.ffn_kept[z, x] = both.astype(BF16).reshape(2, 16, 1920)
            ffn_collect.start()
        if g == 1:
            attn_far.relay()
            d_y1_far.relay()

    kv_copies = []
    order = ((3, at.far), (1, at.down), (2, at.up), (0, y))
    for p, t in order:
        kv_copies.append(at.send(d_kv.at[block_of(t, 1 - s)], m.kv_mate.at[p], mate))
    ffn_collect.middle()
    cosine, sine = m.cosine[...], -m.sine[...]
    d_q = turn_all(jnp.concatenate(d_q, axis=1), cosine, sine).astype(BF16)
    kv_sum = Reduce(at, m.kv_parts, m.kv_early, m.kv_sums, m.kv_landed)
    for (p, t), copy in zip(order, kv_copies):
        copy.wait_recv()
        both = d_kv[block_of(t, s)].astype(F32) + m.kv_mate[p].astype(F32)
        m.kv_parts[p] = both.astype(BF16).reshape(2, OWN // 2, 640)
        if p == 3:
            kv_sum.start_far()
        if p == 2:
            kv_sum.start_near()
    d_q_two, d_q_ring = m.d_q, m.d_q_ring
    d_q_two[0], d_q_two[1] = d_q[:, :HALF], d_q[:, HALF:]
    kv_sum.middle()
    q_copies = [
        at.send(d_q_two.at[up_low], d_q_ring.at[1], up_device),
        at.send(d_q_two.at[up_low], d_q_ring.at[2], down_device),
    ]
    d_q_far = Far(at, d_q_two.at[low], d_q_ring.at[3], d_q_ring.at[3], m.d_q_relay)
    d_q_far.first()
    d_q_ring[0] = d_q_two[low]
    d_normed_one = [0.0, 0.0]
    for c in range(4):
        for r in range(2):
            d_normed_one[r] = d_normed_one[r] + dot(d_q[:, c * 240 : (c + 1) * 240], wq[2 * c + r])

    ffn_collect.second()

    sums, ffn_total = m.ffn_sum, m.ffn_total
    gate_back_slot, back_slot = at.slots(1), at.slots(2)
    lanes = pl.ds(2 * UNITS, UNITS)
    owner = low * 2 + s

    def gate_back():
        both = pl.ds(0, 2 * UNITS)
        return at.wire(
            sums.at[:, :, both], ffn_total.at[at.z, at.x, :, :, both], cross, gate_back_slot
        )

    def down_back(j):
        return at.wire(
            sums.at[j, :, lanes],
            ffn_total.at[at.z, at.x, row, :, lanes],
            at.device(owner, j),
            back_slot + j,
            back_slot + row,
        )

    d_kv_sum = kv_sum.finish()
    d_k = turn_all(d_kv_sum[:, :KVD], cosine, sine).astype(BF16)
    d_v = d_kv_sum[:, KVD:].astype(BF16)
    d_kv_own, d_kv_ring = m.d_kv_own, m.d_kv_ring
    for a in range(2):
        d_kv_own[a] = jnp.concatenate(
            [d_k[:, a * 160 : (a + 1) * 160], d_v[:, a * 160 : (a + 1) * 160]], axis=1
        )
    d_kv_far = Far(at, d_kv_own.at[low], d_kv_ring.at[3], d_kv_ring.at[3], m.d_kv_relay)
    d_kv_far.first()
    kv_out = [
        at.send(d_kv_own.at[up_low], d_kv_ring.at[1], up_device),
        at.send(d_kv_own.at[up_low], d_kv_ring.at[2], down_device),
    ]
    d_kv_ring[0] = d_kv_own[low]
    d_q_far.relay()
    ffn_collect.reduce()

    @pl.when(own_core)
    def _():
        ffn_total[at.z, at.x, :, :, 0 : 2 * UNITS] = sums[:, :, 0 : 2 * UNITS]

    @pl.when(not_(own_core))
    def _():
        gate_back().start()

    for j in range(2):
        here = (owner == y) & (s == j)
        copy = down_back(j)

        @pl.when(here)
        def _():
            ffn_total[at.z, at.x, row, :, 2 * UNITS :] = sums[j, :, 2 * UNITS :]

        @pl.when(not_(here))
        def _():
            copy.start()

    for c in range(4):
        piece = jnp.concatenate(
            [d_k[:, c * 80 : (c + 1) * 80], d_v[:, c * 80 : (c + 1) * 80]], axis=1
        )
        for r in range(2):
            d_normed_one[r] = d_normed_one[r] + dot(piece, wkv[2 * c + r])
    unit_one, inverse_one = unit_rows(tokens_two[row].astype(F32))
    d_tokens, attn_gain_part = norm_back(
        jnp.concatenate(d_normed_one, axis=1), unit_one, inverse_one, attn_gain
    )
    gains = m.gains
    gains[0] = jnp.concatenate([attn_gain_part, ffn_gain_part, jnp.zeros((6, D), F32)], axis=0)
    gain_copies = [
        at.send(gains.at[0], gains.at[1], up_device),
        at.send(gains.at[0], gains.at[2], down_device),
        at.send(gains.at[0], gains.at[3], far_device),
    ]
    d_kv_far.relay()

    @pl.when(not_(own_core))
    def _():
        gate_back().wait_recv()

    for r in range(2):
        source = r * 2 + row

        @pl.when(not_((source == y) & (low == s)))
        def _():
            at.wire(
                sums.at[0, :, lanes],
                ffn_total.at[at.z, at.x, r, :, lanes],
                mate,
                back_slot + r,
            ).wait_recv()

    ffn_spread = Spread(at, ffn_total)
    ffn_spread.first()

    input_grad = m.input_grad
    input_grad[row] = (d_tokens + m.d_middle[...]).astype(BF16)
    input_far = Far(
        at, input_grad.at[row], input_grad.at[1 - up_row], input_grad.at[1 - down_row], m.input_relay
    )
    ffn.start_far()
    ffn.start_near()

    for copy in side_copies + q_copies:
        copy.wait_recv()
    for far in (attn_far, d_y1_far, d_q_far):
        far.finish()
    first_all = first_ring[...].reshape(4 * OWN, HALF)
    q_grad = dot_tn(first_all, d_q_ring[...].reshape(4 * OWN, HALF)).astype(BF16)
    o_grad = dot_tn(
        attn_ring[...].reshape(4 * OWN, HALF), d_y1_ring[...].reshape(4 * OWN, HALF)
    ).astype(BF16)
    qo_two, kv_two = m.qo_two, m.kv_two
    for b in range(2):
        pick = slice(b * 240, (b + 1) * 240)
        qo_two[b, 0:HALF, :] = jnp.concatenate([q_grad[:, pick], o_grad[:, pick]], axis=1)
        qo_two[b, HALF:, :] = jnp.zeros((32, HALF), BF16)
    qo_pair = at.send(qo_two.at[1 - s], m.qo_mate, mate)
    ffn.middle()

    for copy in kv_out + gain_copies:
        copy.wait_recv()
    d_kv_far.finish()
    kv_grad = dot_tn(first_all, d_kv_ring[...].reshape(4 * OWN, 320)).astype(BF16)
    gain_sum = (gains[0] + gains[1] + gains[2] + gains[3])[0:2].astype(BF16)
    gain_rows = [gain_sum[g : g + 1, p * 160 : (p + 1) * 160] for g in range(2) for p in range(6)]
    gain_block = jnp.concatenate(gain_rows + [jnp.zeros((20, 160), BF16)], axis=0)
    for b in range(2):
        kv_two[b, 0:HALF, :] = jnp.concatenate(
            [kv_grad[:, b * 80 : (b + 1) * 80], kv_grad[:, 160 + b * 80 : 160 + (b + 1) * 80]], axis=1
        )
        kv_two[b, HALF:, :] = gain_block
    kv_pair = at.send(kv_two.at[1 - s], m.kv_grad_mate, mate)
    ffn_spread.second()
    attn_kept = m.attn_kept
    for pair, two, theirs, first in (
        (qo_pair, qo_two, m.qo_mate, 0),
        (kv_pair, kv_two, m.kv_grad_mate, HALF),
    ):
        pair.wait_recv()
        both = (two[s].astype(F32) + theirs[...].astype(F32)).astype(BF16)
        width = both.shape[1]
        attn_kept[:, :, :, :, first : first + width] = both.reshape(4, 4, 2, 16, width)

    attn_collect = Collect(
        at,
        attn_kept,
        m.attn_far,
        m.attn_pairs,
        m.attn_near,
        m.attn_four,
        m.attn_last,
        m.attn_sum,
    )
    attn_collect.start()
    input_far.first()
    ffn_spread.third()
    attn_collect.middle()
    attn_collect.second()
    block_out = m.block_out
    block_out[row] = (m.middle[...] + ffn.finish()).astype(BF16)
    block_far = Far(
        at, block_out.at[row], block_out.at[1 - up_row], block_out.at[1 - down_row], m.block_relay
    )
    block_far.first()
    input_far.relay()
    attn_collect.reduce()
    attn_total = m.attn_total
    attn_total[at.z, at.x] = m.attn_sum[...]
    attn_spread = Spread(at, attn_total)
    attn_spread.first()
    block_far.relay()
    ffn_spread.finish()
    leave(3, ffn_total)
    attn_spread.second()
    input_far.finish()
    leave(1, input_grad)
    attn_spread.third()
    block_far.finish()
    leave(0, block_out)
    attn_spread.finish()
    leave(2, attn_total)
    for copy in leaving:
        copy.wait()

    for copy in at.open:
        copy.wait_send()
    gate_mate(row).wait_send()
    for spread in spreads + (ffn_spread, attn_spread):
        spread.drain()

    @pl.when(active)
    def _():
        for n in range(3):
            o_copy(n).wait_send()
        for r in range(2):
            target, copy = down_copy(r)

            @pl.when(target != y)
            def _():
                copy.wait_send()

        @pl.when(not_(own_core))
        def _():
            for n, part in gate_copies:
                gate_copy(n, part).wait_send()

    @pl.when(not_(own_core))
    def _():
        gate_back().wait_send()

    for j in range(2):
        copy = down_back(j)

        @pl.when(not_((owner == y) & (s == j)))
        def _():
            copy.wait_send()


RESULTS = (
    (D, 2 * OWN), (D, 2 * OWN), (1, D), (HALF, 240), (80, HALF), (80, HALF),
    (HALF, 240), (1, D), (HALF, UNITS), (HALF, UNITS), (240, 2 * UNITS),
)


def results_kernel(*refs):
    ins, outs, held, made = refs[:4], refs[4:15], refs[15:19], refs[19:30]
    in_sem, out_sem = refs[30:]
    copies = [
        pltpu.make_async_copy(ins[n], held[n], in_sem.at[n]) for n in range(4)
    ]
    for n in (3, 0, 1, 2):
        copies[n].start()
    block_in, input_in, attn_in, ffn_in = held
    leaving = []

    def leave(n):
        copy = pltpu.make_async_copy(made[n], outs[n], out_sem.at[n])
        copy.start()
        leaving.append(copy)

    copies[3].wait()
    for n in range(2):
        made[8 + n][...] = (
            ffn_in[0:CHUNKS, :, :, n * UNITS : (n + 1) * UNITS].reshape(HALF, UNITS).astype(F32)
        )
        leave(8 + n)
    for i in range(CHUNKS):
        for r in range(2):
            made[10][16 * i : 16 * i + 16, r * UNITS : (r + 1) * UNITS] = ffn_in[
                i, r, :, 2 * UNITS :
            ].astype(F32)
    leave(10)
    for n in range(2):
        copies[n].wait()
        made[n][...] = held[n][...].reshape(2 * OWN, D).astype(F32).T
        leave(n)
    copies[2].wait()
    made[3][...] = attn_in[0:CHUNKS, :, :, 0:240].reshape(HALF, 240).astype(F32)
    leave(3)
    made[6][...] = attn_in[0:CHUNKS, :, :, 240:480].reshape(HALF, 240).astype(F32)
    leave(6)
    kv_grad = attn_in[0:CHUNKS, :, :, 480:640].reshape(HALF, 160).astype(F32).T
    made[4][...] = kv_grad[0:80]
    made[5][...] = kv_grad[80:160]
    leave(4)
    leave(5)
    gains = attn_in[CHUNKS, 0, :, 480:640].astype(F32)
    for p in range(6):
        made[2][:, p * 160 : (p + 1) * 160] = gains[p : p + 1]
        made[7][:, p * 160 : (p + 1) * 160] = gains[6 + p : 7 + p]
    leave(2)
    leave(7)
    for copy in leaving:
        copy.wait()


def shards(
    hidden_in,
    segment_ids,
    attn_gain,
    q_weight,
    k_weight,
    v_weight,
    o_weight,
    ffn_gain,
    gate_weight,
    up_weight,
    down_weight,
    d_out,
):
    frequency = np.float32(rope_base) ** (-np.arange(HEAD_DIM // 2, dtype=np.float32) * 2 / HEAD_DIM)
    freq = jnp.asarray(np.tile(frequency.astype(np.float32), 4)[None, :])
    scratch = [
        pltpu.VMEM(*kind) if isinstance(kind, tuple) else kind for kind in SCRATCH.values()
    ]
    local = pl.BlockSpec(memory_space=pltpu.VMEM)
    kept = pl.pallas_call(
        layer_kernel,
        out_shape=[
            jax.ShapeDtypeStruct((2, OWN, D), BF16),
            jax.ShapeDtypeStruct((2, OWN, D), BF16),
            jax.ShapeDtypeStruct((4, 4, 2, 16, 640), BF16),
            jax.ShapeDtypeStruct((4, 4, 2, 16, 1920), BF16),
        ],
        in_specs=[pl.BlockSpec(memory_space=pl.ANY) if n in LARGE else local for n in IN_NAMES],
        out_specs=[pl.BlockSpec(memory_space=pl.ANY)] * 4,
        scratch_shapes=scratch,
        compiler_params=pltpu.CompilerParams(
            collective_id=1, has_side_effects=True, vmem_limit_bytes=60 * 1024 * 1024
        ),
    )(
        hidden_in.T,
        segment_ids[None, :],
        freq,
        attn_gain[None, :],
        ffn_gain[None, :],
        q_weight,
        k_weight.T,
        v_weight.T,
        o_weight,
        gate_weight,
        up_weight,
        down_weight.T,
        d_out.T,
    )
    outs = pl.pallas_call(
        results_kernel,
        out_shape=[jax.ShapeDtypeStruct(shape, F32) for shape in RESULTS],
        in_specs=[pl.BlockSpec(memory_space=pl.ANY)] * 4,
        out_specs=[pl.BlockSpec(memory_space=pl.ANY)] * len(RESULTS),
        scratch_shapes=[
            pltpu.VMEM((2, OWN, D), BF16),
            pltpu.VMEM((2, OWN, D), BF16),
            pltpu.VMEM((16, 2, 16, 640), BF16),
            pltpu.VMEM((16, 2, 16, 1920), BF16),
        ]
        + [pltpu.VMEM(shape, F32) for shape in RESULTS]
        + [pltpu.SemaphoreType.DMA((4,)), pltpu.SemaphoreType.DMA((len(RESULTS),))],
        compiler_params=pltpu.CompilerParams(vmem_limit_bytes=62 * 1024 * 1024),
    )(kept[0], kept[1], kept[2].reshape(16, 2, 16, 640), kept[3].reshape(16, 2, 16, 1920))
    turned = (0, 1, 4, 5, 10)
    outs = [out.T if i in turned else out for i, out in enumerate(outs)]
    outs[2], outs[7] = outs[2].reshape(D), outs[7].reshape(D)
    return tuple(outs)


def solution(mesh):
    rows, blocks = P(("dp", "col"), None), P("row", "col")
    return jax.shard_map(
        shards,
        mesh=mesh,
        in_specs=(
            rows, P(("dp", "col")), P(), blocks, blocks, blocks, blocks, P(), blocks, blocks, blocks, rows,
        ),
        out_specs=(rows, rows, P(), blocks, blocks, blocks, blocks, P(), blocks, blocks, blocks),
        check_vma=False,
    )
```
